32 devices in a mesh: grp: 2 (over x), sp: 16 (over z, y, core).
Axes of the slice: x: 2, y: 2, z: 4, core: 2. Of those that a mesh axis runs over, the one named last changes fastest.
Arguments:
- tokens: bfloat16 [2, 6, 1024, 1152], P('grp', None, 'sp'), parts along dimension 0, may hold values from -6 to 6
- gain_spatial: float32 [1152], replicated, may hold values from 0.5 to 1.5
- qkv_spatial: bfloat16 [1152, 1728], replicated, may hold values from -0.25 to 0.25
- out_spatial: bfloat16 [576, 1152], replicated, may hold values from -0.75 to 0.75
- gain_cross: float32 [1152], replicated, may hold values from 0.5 to 1.5
- qkv_cross: bfloat16 [1152, 1728], replicated, may hold values from -0.25 to 0.25
- out_cross: bfloat16 [576, 1152], replicated, may hold values from -0.75 to 0.75
- lengths: int32 [2, 6], P('grp'), parts along dimension 0, may hold values from 512 to 1024, as said below
- left_view: int32 [2, 6], P('grp'), parts along dimension 0, may hold values from 0 to 5, as said below
- right_view: int32 [2, 6], P('grp'), parts along dimension 0, may hold values from 0 to 5, as said below
- window_mask: int32 [2, 6, 8, 8], P('grp'), parts along dimension 0, may hold values from 0 to 1, as said below
Outputs:
- result: bfloat16 [2, 6, 1024, 1152], P('grp', None, 'sp'), parts along dimension 0
The draws below stay inside these ranges and needn't reach their ends.
There are 2 independent parts, one for each index of `grp`. The reference program is written for one: setup_inputs(seed, part) draws one part's arguments, and reference() takes and returns one part's arrays. A program takes and returns all parts, laid end to end along the dimension named above; an argument that names none is the same for every part. Nothing has to cross between parts.
Inputs may be any that keep to these rules, and one draw needn't show every extreme that they name: `lengths`: in every frame some view has exactly 1024 live tokens. In each frame the views form one cycle: right_view[f, left_view[f, v]] = v, and no view is its own neighbour. In each frame the views form one cycle: left_view[f, right_view[f, v]] = v, and no view is its own neighbour. window_mask[f, v, a, b] is 1 where b = a or b = 0, and 0 where b > 0 and the distance of a and b exceeds 2.
All inputs are finite; a program needn't handle non-finite values.
Results may differ from the reference program's by a relative error of at most 0.035.
The reference program's roundings to bfloat16 on the way count: a program that leaves them out, or rounds other values in their place, can miss the bound.
Values may be sent and summed in bfloat16 or wider, within the bound.
No kernel may reach another device: no remote copies, remote signals or barrier semaphores. Data moves between devices by JAX's collectives and lax.ppermute only.
A program may use at most 128 MiB of HBM per device.

```python
import jax
import jax.numpy as jnp
from jax import lax

D = 1152
HD = 72
HEADS = 8
VIEWS = 6
VLEN = 1024
BLK = 128
WIN = 2
FRAMES = 1


def view_cycle(key):
    keys = jax.random.split(key, FRAMES)
    order = jax.vmap(lambda single: jax.random.permutation(single, VIEWS))(keys).astype(jnp.int32)
    place = jnp.argsort(order, axis=1).astype(jnp.int32)
    before = jnp.take_along_axis(order, (place - 1) % VIEWS, axis=1)
    after = jnp.take_along_axis(order, (place + 1) % VIEWS, axis=1)
    return (before.astype(jnp.int32), after.astype(jnp.int32))


def draw_left_view(key, part):
    return view_cycle(key)[0]


def draw_right_view(key, part):
    return view_cycle(key)[1]


def draw_lengths(key, part):
    key = jax.random.fold_in(key, 7)
    first, second = jax.random.split(key)
    spans = jax.random.randint(first, (FRAMES, VIEWS), VLEN // 2, VLEN + 1)
    full = jax.random.randint(second, (FRAMES,), 0, VIEWS)
    views = jnp.arange(VIEWS, dtype=jnp.int32)
    return jnp.where(views[None, :] == full[:, None], VLEN, spans).astype(jnp.int32)


def draw_window_mask(key, part):
    key = jax.random.fold_in(key, 11)
    blocks = VLEN // BLK
    coins = jax.random.randint(key, (FRAMES, VIEWS, blocks, blocks), 0, 2)
    rows = jnp.arange(blocks, dtype=jnp.int32)[:, None]
    cols = jnp.arange(blocks, dtype=jnp.int32)[None, :]
    inside = jnp.abs(rows - cols) <= WIN
    chosen = jnp.where(inside, coins, 0)
    return jnp.where((rows == cols) | (cols == 0), 1, chosen).astype(jnp.int32)


def head_projection(key, lowest, highest):
    inner = HEADS * HD
    base_key, sign_key, pattern_key, strength_key = jax.random.split(key, 4)
    base = jnp.clip(jax.random.normal(base_key, (D, 3 * inner), jnp.float32) * D ** (-0.5), -0.1875, 0.1875)
    direction = jnp.where(jax.random.bernoulli(sign_key, 0.5, (D, HEADS)), 1.0, -1.0).astype(jnp.float32) * D ** (-0.5)
    pattern = jnp.where(jax.random.bernoulli(pattern_key, 0.5, (HEADS, HD)), 1.0, -1.0).astype(jnp.float32)
    strength = jax.random.uniform(strength_key, (HEADS,), jnp.float32, lowest, highest)
    shared = (direction[:, :, None] * (strength[:, None] * pattern)[None, :, :]).reshape(D, inner)
    zeros = jnp.zeros((D, inner), jnp.float32)
    total = base + jnp.concatenate([shared, shared, zeros], axis=1)
    return jnp.clip(total, -0.25, 0.25).astype(jnp.bfloat16)


def draw_qkv_spatial(key, part):
    key = jax.random.fold_in(key, 13)
    return head_projection(key, 0.3, 0.6)


def draw_qkv_cross(key, part):
    key = jax.random.fold_in(key, 17)
    return head_projection(key, 0.3, 0.6)


def steps_of(rng, extent, pieces, least, largest):
    level, own = 1.0, jax.random.fold_in(rng, 6)
    for position, parts in pieces:
        draws = jnp.exp(jax.random.uniform(jax.random.fold_in(own, position), (parts,), jnp.float32, least / len(pieces), largest / len(pieces)))
        level = level * jnp.repeat(draws, extent[position] // parts).reshape([-1 if axis == position else 1 for axis in range(len(extent))])
    return level


def bell_draw(stream_key, shape, scale, most, shards=(), kind=jnp.bfloat16):
    values = scale * jax.random.normal(stream_key, shape, jnp.float32)
    if shards:
        values = values * steps_of(stream_key, shape, shards, -0.22, 0.18)
    return jnp.clip(values, -most, most).astype(kind)


def setup_inputs(seed: int = 0, part: int = 0) -> dict:
    key_list = jax.random.split(jax.random.key(seed), 12)
    own_keys = jax.random.split(jax.random.fold_in(key_list[11], part), 12)
    tokens = bell_draw(own_keys[0], (FRAMES, VIEWS, VLEN, D), 1.0, 6.0, ((2, 16),))
    gain_spatial = jnp.clip(1.0 + 0.1 * jax.random.normal(key_list[1], (D,), jnp.float32), 0.5, 1.5)
    qkv_spatial = draw_qkv_spatial(jax.random.fold_in(key_list[11], 71), part)
    out_spatial = bell_draw(key_list[3], (HEADS * HD, D), (HEADS * HD // 8) ** -0.5, 0.75)
    gain_cross = jnp.clip(1.0 + 0.1 * jax.random.normal(key_list[4], (D,), jnp.float32), 0.5, 1.5)
    qkv_cross = draw_qkv_cross(jax.random.fold_in(key_list[11], 71), part)
    out_cross = bell_draw(key_list[6], (HEADS * HD, D), (HEADS * HD // 8) ** -0.5, 0.75)
    lengths = draw_lengths(jax.random.fold_in(jax.random.fold_in(key_list[11], part), 71), part)
    left_view = draw_left_view(jax.random.fold_in(jax.random.fold_in(key_list[11], part), 71), part)
    right_view = draw_right_view(jax.random.fold_in(jax.random.fold_in(key_list[11], part), 71), part)
    window_mask = draw_window_mask(jax.random.fold_in(jax.random.fold_in(key_list[11], part), 71), part)
    return {"tokens": tokens, "gain_spatial": gain_spatial, "qkv_spatial": qkv_spatial, "out_spatial": out_spatial, "gain_cross": gain_cross, "qkv_cross": qkv_cross, "out_cross": out_cross, "lengths": lengths, "left_view": left_view, "right_view": right_view, "window_mask": window_mask}


EPSILON = 1e-06

def rms_norm(values, gain):
    floats = values.astype(jnp.float32)
    square = lax.optimization_barrier(jnp.mean(floats * floats, axis=-1, keepdims=True))
    return (floats * lax.rsqrt(square + EPSILON) * gain).astype(jnp.bfloat16)

def attend(query, keys, values, allow):
    scores = jnp.einsum('hqd,hkd->hqk', query.astype(jnp.float32), keys.astype(jnp.float32)) * HD ** (-0.5)
    scores = jnp.where(allow, scores, -1e+30)
    top = lax.optimization_barrier(jnp.max(scores, axis=-1, keepdims=True))
    weights = jnp.where(allow, jnp.exp(scores - top), 0.0)
    probs = (weights / lax.optimization_barrier(jnp.sum(weights, axis=-1, keepdims=True))).astype(jnp.bfloat16)
    return jnp.einsum('hqk,hkd->hqd', probs.astype(jnp.float32), values.astype(jnp.float32)).astype(jnp.bfloat16)

def reference(tokens, gain_spatial, qkv_spatial, out_spatial, gain_cross, qkv_cross, out_cross, lengths, left_view, right_view, window_mask):
    inner = HEADS * HD
    positions = jnp.arange(VLEN, dtype=jnp.int32)
    live = (positions[None, None, :] < lengths[:, :, None]).astype(jnp.float32)[..., None]
    flat_len = lengths.reshape(-1)
    order = jnp.arange(FRAMES * VIEWS, dtype=jnp.int32)
    blocks = VLEN // BLK
    masks = window_mask.reshape(FRAMES * VIEWS, blocks, blocks)
    flat_left = left_view.reshape(-1)
    flat_right = right_view.reshape(-1)

    def project(stream, gain, weights):
        normed = rms_norm(stream, gain)
        mixed = jnp.dot(normed.reshape(-1, D), weights, preferred_element_type=jnp.float32).astype(jnp.bfloat16)
        return mixed.reshape(FRAMES * VIEWS, VLEN, 3, HEADS, HD).transpose(0, 2, 3, 1, 4)

    def finish(stream, attended, weights):
        merged = attended.transpose(0, 2, 1, 3).reshape(-1, inner)
        branch = jnp.dot(merged, weights, preferred_element_type=jnp.float32).reshape(FRAMES, VIEWS, VLEN, D)
        return (stream.astype(jnp.float32) + live * branch).astype(jnp.bfloat16)
    spatial_heads = project(tokens, gain_spatial, qkv_spatial)

    def spatial(index):
        block_mask = jnp.repeat(jnp.repeat(masks[index], BLK, axis=0), BLK, axis=1) > 0
        allow = block_mask & (positions[None, :] < flat_len[index])
        return attend(spatial_heads[index, 0], spatial_heads[index, 1], spatial_heads[index, 2], allow[None])
    middle = finish(tokens, lax.map(spatial, order), out_spatial)
    cross_heads = project(middle, gain_cross, qkv_cross)

    def cross(index):
        frame = index // VIEWS
        left = frame * VIEWS + flat_left[index]
        right = frame * VIEWS + flat_right[index]
        keys = jnp.concatenate([cross_heads[left, 1], cross_heads[right, 1]], axis=1)
        values = jnp.concatenate([cross_heads[left, 2], cross_heads[right, 2]], axis=1)
        allow = jnp.concatenate([positions < flat_len[left], positions < flat_len[right]])
        return attend(cross_heads[index, 0], keys, values, allow[None, None, :])
    return finish(middle, lax.map(cross, order), out_cross)
```

```python
import functools

import jax
import jax.numpy as jnp
from jax import lax
from jax.experimental import pallas as pl
from jax.experimental.pallas import tpu as pltpu
from jax.sharding import PartitionSpec as P

HEADS = 8
EPSILON = 1e-06


HS = 72
TILE = 64
LANES = 128
TOP = 40
QKV_ROWS = 336
OUT_ROWS = 112
NEG = -1e30
VMEM = 56 * 1024 * 1024


def cycle_order(right_ref):
    order = [jnp.int32(0)]
    for _ in range(5):
        order.append(right_ref[0, order[-1]])
    return order


def low_lanes(rows):
    return lax.broadcasted_iota(jnp.int32, (rows, LANES), 1) < TILE


def swap(tile):
    return pltpu.roll(tile, TILE, 1)


def side_by_side(first, first_half, second, second_half):
    left = first if first_half == 0 else swap(first)
    right = second if second_half == 1 else swap(second)
    return jnp.where(low_lanes(first.shape[0]), left, right)


def fold_third(tile, half):
    bottom = jnp.concatenate([tile[TOP:], jnp.zeros((2 * TOP - HS, LANES), jnp.float32)], axis=0)
    return side_by_side(tile[:TOP], half, bottom, half)


def normalise(floats, gain):
    square = jnp.mean(floats * floats, axis=-1, keepdims=True)
    return (floats * lax.rsqrt(square + EPSILON) * gain).astype(jnp.bfloat16)


def project_and_pack(normed_ref, weight_ref, turned_ref, out_ref, cross):
    total = weight_ref.shape[1]
    inner = total // 3
    step = 384
    for start in range(0, total, step):
        stop = min(start + step, total)
        part = jnp.dot(
            normed_ref[...], weight_ref[:, start:stop], preferred_element_type=jnp.float32
        )
        turned_ref[start:stop, :] = part.T
    for head in range(HEADS):
        for parity in range(2):
            other = 1 - parity if cross else parity

            def item(which, m):
                row = which * inner + head * HS
                return turned_ref[row : row + HS, m * LANES : (m + 1) * LANES]

            rows = [
                side_by_side(item(0, m), parity, item(1, m), other) for m in range(3)
            ]
            rows.append(side_by_side(item(2, 0), other, item(2, 1), other))
            rows.append(fold_third(item(2, 2), other))
            rows.append(jnp.zeros((QKV_ROWS - 4 * HS - TOP, LANES), jnp.float32))
            out_ref[head * 2 + parity] = jnp.concatenate(rows, axis=0).astype(jnp.bfloat16)


def project_kernel(right_ref, tokens_ref, gain_ref, weight_ref, out_ref, normed_ref, turned_ref):
    order = cycle_order(right_ref)
    for j in range(6):
        floats = tokens_ref[0, order[j]].astype(jnp.float32)
        normed_ref[j * TILE : (j + 1) * TILE, :] = normalise(floats, gain_ref[...])
    project_and_pack(normed_ref, weight_ref, turned_ref, out_ref, False)


def unpack(slots_ref, key_bias, query_rows, query_ref, key_ref, value_ref):
    blocks = slots_ref.shape[0] // 2
    low = low_lanes(QKV_ROWS)
    row8 = lax.broadcasted_iota(jnp.int32, (8, LANES), 0)
    pad = jnp.zeros((LANES - HS - 16, LANES), jnp.float32)
    first_row = jnp.where(row8 == 0, 1.0, 0.0)
    for b in range(blocks):
        span = slice(b * LANES, (b + 1) * LANES)
        even = slots_ref[2 * b].astype(jnp.float32)
        odd = slots_ref[2 * b + 1].astype(jnp.float32)
        lower = jnp.where(low, even, swap(odd))
        upper = jnp.where(low, swap(even), odd)
        own_block = jnp.where(row8 == b, 1.0, 0.0)
        values = [
            lower[3 * HS : 4 * HS],
            upper[3 * HS : 4 * HS],
            jnp.concatenate(
                [lower[4 * HS : 4 * HS + TOP], upper[4 * HS : 5 * HS - TOP]], axis=0
            ),
        ]
        for m in range(3):
            query = jnp.concatenate(
                [lower[m * HS : (m + 1) * HS], query_rows(m, b, row8), first_row, pad], axis=0
            )
            query_ref[m, :, span] = query.astype(jnp.bfloat16)
            live = jnp.where(row8 == 0, key_bias(m, b), 0.0)
            key = jnp.concatenate([upper[m * HS : (m + 1) * HS], own_block, live, pad], axis=0)
            key_ref[m, span, :] = key.T.astype(jnp.bfloat16)
            value_ref[m, :, span] = jnp.concatenate([values[m], first_row], axis=0).astype(
                jnp.bfloat16
            )


def attend(query, parts):
    factor = HS**-0.5 * 1.4426950408889634
    scores = [jnp.dot(keys, query, preferred_element_type=jnp.float32) for keys, _ in parts]
    top = functools.reduce(
        jnp.maximum, [jnp.max(score, axis=0, keepdims=True) for score in scores]
    )
    total = None
    for score, (_, values) in zip(scores, parts):
        weights = jnp.exp2((score - top) * factor).astype(jnp.bfloat16)
        term = jnp.dot(values, weights, preferred_element_type=jnp.float32)
        total = term if total is None else total + term
    return total[:HS] / total[HS : HS + 1]


def pack_outputs(attended_ref, out_ref):
    for b in range(out_ref.shape[0] // 2):
        span = slice(b * LANES, (b + 1) * LANES)
        tiles = [attended_ref[m, :, span] for m in range(3)]
        for half in range(2):
            rows = [side_by_side(tiles[0], half, tiles[1], half), fold_third(tiles[2], half)]
            out_ref[2 * b + half] = jnp.concatenate(rows, axis=0).astype(jnp.bfloat16)


def live_bias(length, b):
    position = b * LANES + lax.broadcasted_iota(jnp.int32, (8, LANES), 1)
    return jnp.where(position < length, 0.0, NEG)


def spatial_kernel(
    device_ref,
    right_ref,
    lengths_ref,
    mask_ref,
    slots_ref,
    out_ref,
    query_ref,
    key_ref,
    value_ref,
    attended_ref,
):
    order = cycle_order(right_ref)
    parity = device_ref[0] % 2
    views = [jnp.where(parity == 0, order[2 * m], order[2 * m + 1]) for m in range(3)]
    blocks = mask_ref.shape[-1]

    def query_rows(m, b, row8):
        rows = jnp.zeros((8, LANES), jnp.float32)
        for other in range(blocks):
            allowed = mask_ref[0, views[m], b, other] > 0
            rows = jnp.where(row8 == other, jnp.where(allowed, 0.0, NEG), rows)
        return rows

    def key_bias(m, b):
        return live_bias(lengths_ref[0, views[m]], b)

    unpack(slots_ref, key_bias, query_rows, query_ref, key_ref, value_ref)
    wide = 2 * LANES
    for m in range(3):
        for i in range(blocks // 2):
            first = max(0, 2 * i - 2) * LANES
            last = min(blocks, 2 * i + 4) * LANES
            spans = [slice(first, last)]
            if first > 0:
                spans.append(slice(0, LANES))
            lanes = slice(i * wide, (i + 1) * wide)
            attended_ref[m, :, lanes] = attend(
                query_ref[m, :, lanes],
                [(key_ref[m, span, :], value_ref[m, :, span]) for span in spans],
            )
    pack_outputs(attended_ref, out_ref)


def cross_kernel(
    device_ref,
    right_ref,
    lengths_ref,
    slots_ref,
    out_ref,
    query_ref,
    key_ref,
    value_ref,
    attended_ref,
):
    order = cycle_order(right_ref)
    parity = device_ref[0] % 2
    views = [jnp.where(parity == 0, order[2 * m + 1], order[2 * m]) for m in range(3)]

    def query_rows(m, b, row8):
        return jnp.zeros((8, LANES), jnp.float32)

    def key_bias(m, b):
        return live_bias(lengths_ref[0, views[m]], b)

    unpack(slots_ref, key_bias, query_rows, query_ref, key_ref, value_ref)
    wide = 2 * LANES
    for m in range(3):
        second = jnp.where(parity == 0, (m + 2) % 3, (m + 1) % 3)
        for i in range(query_ref.shape[2] // wide):
            lanes = slice(i * wide, (i + 1) * wide)
            attended_ref[m, :, lanes] = attend(
                query_ref[m, :, lanes],
                [(key_ref[m], value_ref[m]), (key_ref[second], value_ref[second])],
            )
    pack_outputs(attended_ref, out_ref)


def merge_heads(slots_ref, merged_ref):
    low = low_lanes(OUT_ROWS)
    tiles = [[], [], []]
    for head in range(HEADS):
        even = slots_ref[2 * head].astype(jnp.float32)
        odd = slots_ref[2 * head + 1].astype(jnp.float32)
        lower = jnp.where(low, even, swap(odd))
        upper = jnp.where(low, swap(even), odd)
        tiles[0].append(lower[:HS])
        tiles[1].append(upper[:HS])
        tiles[2].append(lower[HS:])
        tiles[2].append(upper[HS : 2 * HS - TOP])
    for m in range(3):
        merged = jnp.concatenate(tiles[m], axis=0)
        merged_ref[m * LANES : (m + 1) * LANES, :] = merged.T.astype(jnp.bfloat16)


def live_rows(device_ref, length):
    position = device_ref[0] * TILE + lax.broadcasted_iota(jnp.int32, (TILE, 1), 0)
    return (position < length).astype(jnp.float32)


def middle_kernel(
    device_ref,
    right_ref,
    lengths_ref,
    slots_ref,
    tokens_ref,
    mix_ref,
    gain_ref,
    weight_ref,
    middle_ref,
    out_ref,
    merged_ref,
    normed_ref,
    turned_ref,
):
    order = cycle_order(right_ref)
    merge_heads(slots_ref, merged_ref)
    for j in range(6):
        rows = slice(j * TILE, (j + 1) * TILE)
        branch = jnp.dot(merged_ref[rows, :], mix_ref[...], preferred_element_type=jnp.float32)
        live = live_rows(device_ref, lengths_ref[0, order[j]])
        middle = (tokens_ref[0, order[j]].astype(jnp.float32) + live * branch).astype(jnp.bfloat16)
        middle_ref[rows, :] = middle
        normed_ref[rows, :] = normalise(middle.astype(jnp.float32), gain_ref[...])
    project_and_pack(normed_ref, weight_ref, turned_ref, out_ref, True)


def finish_kernel(
    device_ref, right_ref, lengths_ref, slots_ref, middle_ref, mix_ref, out_ref, merged_ref
):
    order = cycle_order(right_ref)
    merge_heads(slots_ref, merged_ref)
    for j in range(6):
        rows = slice(j * TILE, (j + 1) * TILE)
        branch = jnp.dot(merged_ref[rows, :], mix_ref[...], preferred_element_type=jnp.float32)
        live = live_rows(device_ref, lengths_ref[0, order[j]])
        out_ref[0, order[j]] = (middle_ref[rows, :].astype(jnp.float32) + live * branch).astype(
            jnp.bfloat16
        )


def call(kernel, scalars, arrays, out_shape, scratch, name):
    smem = pl.BlockSpec(memory_space=pltpu.SMEM)
    vmem = pl.BlockSpec(memory_space=pltpu.VMEM)
    return pl.pallas_call(
        kernel,
        out_shape=out_shape,
        in_specs=[smem] * len(scalars) + [vmem] * len(arrays),
        out_specs=jax.tree.map(lambda _: vmem, out_shape),
        scratch_shapes=scratch,
        compiler_params=pltpu.CompilerParams(vmem_limit_bytes=VMEM),
        name=name,
    )(*scalars, *arrays)


def exchange(slots):
    return lax.all_to_all(slots, "sp", split_axis=0, concat_axis=0, tiled=True)


def fast_shards(
    tokens,
    gain_spatial,
    qkv_spatial,
    out_spatial,
    gain_cross,
    qkv_cross,
    out_cross,
    lengths,
    left_view,
    right_view,
    window_mask,
):
    width = tokens.shape[-1]
    inner = out_spatial.shape[0]
    devices_sp = lax.axis_size("sp")
    view_len = TILE * devices_sp
    rows = 6 * TILE
    device = lax.axis_index("sp").astype(jnp.int32).reshape(1)
    qkv_slots = jax.ShapeDtypeStruct((devices_sp, QKV_ROWS, LANES), jnp.bfloat16)
    out_slots = jax.ShapeDtypeStruct((devices_sp, OUT_ROWS, LANES), jnp.bfloat16)
    turned = pltpu.VMEM((3 * inner, rows), jnp.float32)
    normed = pltpu.VMEM((rows, width), jnp.bfloat16)
    merged = pltpu.VMEM((rows, inner), jnp.bfloat16)
    heads = [
        pltpu.VMEM((3, LANES, view_len), jnp.bfloat16),
        pltpu.VMEM((3, view_len, LANES), jnp.bfloat16),
        pltpu.VMEM((3, HS + 8, view_len), jnp.bfloat16),
        pltpu.VMEM((3, HS, view_len), jnp.float32),
    ]
    slots = call(
        project_kernel,
        [right_view],
        [tokens, gain_spatial.reshape(1, width), qkv_spatial],
        qkv_slots,
        [normed, turned],
        "project",
    )
    attended = call(
        spatial_kernel,
        [device, right_view, lengths, window_mask],
        [exchange(slots)],
        out_slots,
        heads,
        "spatial",
    )
    middle, slots = call(
        middle_kernel,
        [device, right_view, lengths],
        [exchange(attended), tokens, out_spatial, gain_cross.reshape(1, width), qkv_cross],
        (jax.ShapeDtypeStruct((rows, width), jnp.bfloat16), qkv_slots),
        [merged, normed, turned],
        "middle",
    )
    attended = call(
        cross_kernel,
        [device, right_view, lengths],
        [exchange(slots)],
        out_slots,
        heads,
        "cross",
    )
    return call(
        finish_kernel,
        [device, right_view, lengths],
        [exchange(attended), middle, out_cross],
        jax.ShapeDtypeStruct(tokens.shape, jnp.bfloat16),
        [merged],
        "finish",
    )


def rms_norm(values, gain):
    floats = values.astype(jnp.float32)
    square = jnp.mean(floats * floats, axis=-1, keepdims=True)
    return (floats * lax.rsqrt(square + EPSILON) * gain).astype(jnp.bfloat16)


def to_frames(block, heads):
    frames, views, tile_len, inner = block.shape
    head_size = inner // heads
    moved = block.reshape(frames, views, tile_len, heads, head_size).transpose(0, 3, 1, 2, 4)
    return moved.reshape(frames, heads, views, tile_len * head_size)


def from_units(units, frames, views, tile_len, heads):
    head_size = units.shape[-1] // tile_len
    moved = units.reshape(frames, heads, views, tile_len, head_size).transpose(0, 2, 3, 1, 4)
    return moved.reshape(frames, views, tile_len, heads * head_size)


def attend_one(operands):
    query, keys, values, allow = operands
    scores = jnp.einsum("qd,kd->qk", query, keys, preferred_element_type=jnp.float32) * query.shape[
        -1
    ] ** (-0.5)
    scores = jnp.where(allow, scores, -1e30)
    top = jnp.max(scores, axis=-1, keepdims=True)
    weights = jnp.where(allow, jnp.exp(scores - top), 0.0)
    probs = (weights / jnp.sum(weights, axis=-1, keepdims=True)).astype(jnp.bfloat16)
    return jnp.einsum("qk,kd->qd", probs, values, preferred_element_type=jnp.float32).astype(
        jnp.bfloat16
    )


def general_shards(
    tokens,
    gain_spatial,
    qkv_spatial,
    out_spatial,
    gain_cross,
    qkv_cross,
    out_cross,
    lengths,
    left_view,
    right_view,
    window_mask,
):
    frames, views, tile_len, width = tokens.shape
    inner = out_spatial.shape[0]
    head_size = inner // HEADS
    devices_sp = lax.axis_size("sp")
    device = lax.axis_index("sp")
    view_len = tile_len * devices_sp
    blocks = window_mask.shape[-1]
    block_len = view_len // blocks
    positions = device * tile_len + jnp.arange(tile_len, dtype=jnp.int32)
    live_rows = (positions[None, None, :] < lengths[:, :, None]).astype(jnp.float32)[..., None]
    key_pos = jnp.arange(view_len, dtype=jnp.int32)
    units_dev = frames * HEADS * views // devices_sp
    unit_ids = device * units_dev + jnp.arange(units_dev, dtype=jnp.int32)
    frame_ids = unit_ids // (HEADS * views)
    view_ids = unit_ids % views
    flat_ids = frame_ids * views + view_ids
    flat_len = lengths.reshape(-1)
    own_len = jnp.take(flat_len, flat_ids)
    total_units = frames * HEADS * views
    normed = rms_norm(tokens, gain_spatial)
    projected = jnp.einsum(
        "fvtd,de->fvte", normed, qkv_spatial, preferred_element_type=jnp.float32
    ).astype(jnp.bfloat16)
    stacked = jnp.stack(
        [
            to_frames(projected[..., which * inner : (which + 1) * inner], HEADS)
            for which in range(3)
        ],
        axis=3,
    )
    stacked = stacked.reshape(total_units, 3, tile_len * head_size)
    gathered = lax.all_to_all(stacked, "sp", split_axis=0, concat_axis=2, tiled=True)
    gathered = gathered.reshape(units_dev, 3, view_len, head_size)
    masks = jnp.take(window_mask.reshape(-1, blocks, blocks), flat_ids, axis=0) > 0
    allow = jnp.broadcast_to(
        masks[:, :, None, :, None], (units_dev, blocks, block_len, blocks, block_len)
    )
    allow = allow.reshape(units_dev, view_len, view_len) & (
        key_pos[None, None, :] < own_len[:, None, None]
    )
    spatial_out = lax.map(attend_one, (gathered[:, 0], gathered[:, 1], gathered[:, 2], allow))
    returned = lax.all_to_all(
        spatial_out.reshape(units_dev, view_len * head_size),
        "sp",
        split_axis=1,
        concat_axis=0,
        tiled=True,
    )
    attended = from_units(returned, frames, views, tile_len, HEADS)
    branch = jnp.einsum("fvte,ed->fvtd", attended, out_spatial, preferred_element_type=jnp.float32)
    middle = (tokens.astype(jnp.float32) + live_rows * branch).astype(jnp.bfloat16)
    normed_cross = rms_norm(middle, gain_cross)
    projected = jnp.einsum(
        "fvtd,de->fvte", normed_cross, qkv_cross, preferred_element_type=jnp.float32
    ).astype(jnp.bfloat16)
    query_fr, key_fr, value_fr = [
        to_frames(projected[..., which * inner : (which + 1) * inner], HEADS) for which in range(3)
    ]
    left_ids = jnp.take(left_view.reshape(-1), flat_ids)
    right_ids = jnp.take(right_view.reshape(-1), flat_ids)
    view_iota = jnp.arange(views, dtype=jnp.int32)
    pick_left = (left_view[:, :, None] == view_iota).astype(jnp.bfloat16)
    pick_right = (right_view[:, :, None] == view_iota).astype(jnp.bfloat16)

    def select(pick, source):
        return jnp.einsum(
            "fvw,fhwx->fhvx", pick, source, preferred_element_type=jnp.float32
        ).astype(jnp.bfloat16)

    packed = jnp.stack(
        [
            query_fr,
            select(pick_left, key_fr),
            select(pick_left, value_fr),
            select(pick_right, key_fr),
            select(pick_right, value_fr),
        ],
        axis=3,
    )
    packed = packed.reshape(total_units, 5, tile_len * head_size)
    arrived = lax.all_to_all(packed, "sp", split_axis=0, concat_axis=2, tiled=True)
    cross_query = arrived[:, 0]
    left_kv = arrived[:, 1:3]
    right_kv = arrived[:, 3:5]
    cross_keys = jnp.concatenate([left_kv[:, 0], right_kv[:, 0]], axis=1).reshape(
        units_dev, 2 * view_len, head_size
    )
    cross_values = jnp.concatenate([left_kv[:, 1], right_kv[:, 1]], axis=1).reshape(
        units_dev, 2 * view_len, head_size
    )
    left_len = jnp.take(flat_len, frame_ids * views + left_ids)
    right_len = jnp.take(flat_len, frame_ids * views + right_ids)
    allow_cross = jnp.concatenate(
        [key_pos[None, :] < left_len[:, None], key_pos[None, :] < right_len[:, None]], axis=1
    )[:, None, :]
    cross_out = lax.map(
        attend_one,
        (
            cross_query.reshape(units_dev, view_len, head_size),
            cross_keys,
            cross_values,
            allow_cross,
        ),
    )
    returned = lax.all_to_all(
        cross_out.reshape(units_dev, view_len * head_size),
        "sp",
        split_axis=1,
        concat_axis=0,
        tiled=True,
    )
    attended = from_units(returned, frames, views, tile_len, HEADS)
    branch = jnp.einsum("fvte,ed->fvtd", attended, out_cross, preferred_element_type=jnp.float32)
    return (middle.astype(jnp.float32) + live_rows * branch).astype(jnp.bfloat16)


def shards(*args):
    tokens, mask = args[0], args[-1]
    sizes = (tokens.shape[0], tokens.shape[1], tokens.shape[2], mask.shape[-1])
    if sizes == (1, 6, TILE, 8) and lax.axis_size("sp") == 2 * HEADS:
        return fast_shards(*args)
    return general_shards(*args)


def solution(mesh):
    in_specs = (
        P("grp", None, "sp", None),
        P(),
        P(),
        P(),
        P(),
        P(),
        P(),
        P("grp", None),
        P("grp", None),
        P("grp", None),
        P("grp", None, None, None),
    )
    out_specs = P("grp", None, "sp", None)
    return jax.shard_map(shards, mesh=mesh, in_specs=in_specs, out_specs=out_specs, check_vma=False)
```

```python
import functools

import jax
import jax.numpy as jnp
from jax import lax
from jax.experimental import pallas as pl
from jax.experimental.pallas import tpu as pltpu
from jax.sharding import PartitionSpec as P

HEADS = 8
EPSILON = 1e-06


HS = 72
TILE = 64
LANES = 128
TOP = 40
QKV_ROWS = 336
OUT_ROWS = 112
NEG = -1e30
VMEM = 24 * 1024 * 1024


def cycle_order(right_ref):
    order = [jnp.int32(0)]
    for _ in range(5):
        order.append(right_ref[0, order[-1]])
    return order


def low_lanes(rows):
    return lax.broadcasted_iota(jnp.int32, (rows, LANES), 1) < TILE


def swap(tile):
    return pltpu.roll(tile, TILE, 1)


def side_by_side(first, first_half, second, second_half):
    left = first if first_half == 0 else swap(first)
    right = second if second_half == 1 else swap(second)
    return jnp.where(low_lanes(first.shape[0]), left, right)


def fold_third(tile, half):
    bottom = jnp.concatenate([tile[TOP:], jnp.zeros((2 * TOP - HS, LANES), jnp.float32)], axis=0)
    return side_by_side(tile[:TOP], half, bottom, half)


def normalise(floats, gain):
    square = jnp.mean(floats * floats, axis=-1, keepdims=True)
    return (floats * lax.rsqrt(square + EPSILON) * gain[None, :]).astype(jnp.bfloat16)


def project_and_pack(normed_ref, weight_ref, turned_ref, out_ref, cross):
    inner = weight_ref.shape[0] // 3
    turned_ref[...] = lax.dot_general(
        weight_ref[...],
        normed_ref[...],
        (((1,), (1,)), ((), ())),
        preferred_element_type=jnp.float32,
    )
    for head in range(HEADS):
        for parity in range(2):
            other = 1 - parity if cross else parity

            def item(which, m):
                row = which * inner + head * HS
                return turned_ref[row : row + HS, m * LANES : (m + 1) * LANES]

            rows = [
                side_by_side(item(0, m), parity, item(1, m), other) for m in range(3)
            ]
            rows.append(side_by_side(item(2, 0), other, item(2, 1), other))
            rows.append(fold_third(item(2, 2), other))
            rows.append(jnp.zeros((QKV_ROWS - 4 * HS - TOP, LANES), jnp.float32))
            out_ref[head * 2 + parity] = jnp.concatenate(rows, axis=0).astype(jnp.bfloat16)


def project_kernel(right_ref, tokens_ref, gain_ref, weight_ref, out_ref, normed_ref, turned_ref):
    order = cycle_order(right_ref)
    for j in range(6):
        floats = tokens_ref[0, order[j]].astype(jnp.float32)
        normed_ref[j * TILE : (j + 1) * TILE, :] = normalise(floats, gain_ref[...])
    project_and_pack(normed_ref, weight_ref, turned_ref, out_ref, False)


def unpack(slots_ref, key_bias, query_rows, query_ref, key_ref, value_ref):
    blocks = slots_ref.shape[0] // 2
    low = low_lanes(QKV_ROWS)
    row8 = lax.broadcasted_iota(jnp.int32, (8, LANES), 0)
    pad = jnp.zeros((LANES - HS - 16, LANES), jnp.float32)
    first_row = jnp.where(row8 == 0, 1.0, 0.0)
    for b in range(blocks):
        span = slice(b * LANES, (b + 1) * LANES)
        even = slots_ref[2 * b].astype(jnp.float32)
        odd = slots_ref[2 * b + 1].astype(jnp.float32)
        lower = jnp.where(low, even, swap(odd))
        upper = jnp.where(low, swap(even), odd)
        own_block = jnp.where(row8 == b, 1.0, 0.0)
        values = [
            lower[3 * HS : 4 * HS],
            upper[3 * HS : 4 * HS],
            jnp.concatenate(
                [lower[4 * HS : 4 * HS + TOP], upper[4 * HS : 5 * HS - TOP]], axis=0
            ),
        ]
        for m in range(3):
            query = jnp.concatenate(
                [lower[m * HS : (m + 1) * HS], query_rows(m, b, row8), first_row, pad], axis=0
            )
            query_ref[m, :, span] = query.astype(jnp.bfloat16)
            live = jnp.where(row8 == 0, key_bias(m, b), 0.0)
            key = jnp.concatenate([upper[m * HS : (m + 1) * HS], own_block, live, pad], axis=0)
            key_ref[m, span, :] = key.T.astype(jnp.bfloat16)
            value_ref[m, :, span] = jnp.concatenate([values[m], first_row], axis=0).astype(
                jnp.bfloat16
            )


def attend(query, parts):
    factor = HS**-0.5 * 1.4426950408889634
    scores = [jnp.dot(keys, query, preferred_element_type=jnp.float32) for keys, _ in parts]
    top = functools.reduce(
        jnp.maximum, [jnp.max(score, axis=0, keepdims=True) for score in scores]
    )
    total = None
    for score, (_, values) in zip(scores, parts):
        weights = jnp.exp2((score - top) * factor).astype(jnp.bfloat16)
        term = jnp.dot(values, weights, preferred_element_type=jnp.float32)
        total = term if total is None else total + term
    return total[:HS] / total[HS : HS + 1]


def pack_outputs(attended_ref, out_ref):
    for b in range(out_ref.shape[0] // 2):
        span = slice(b * LANES, (b + 1) * LANES)
        tiles = [attended_ref[m, :, span] for m in range(3)]
        for half in range(2):
            rows = [side_by_side(tiles[0], half, tiles[1], half), fold_third(tiles[2], half)]
            out_ref[2 * b + half] = jnp.concatenate(rows, axis=0).astype(jnp.bfloat16)


def live_bias(length, b):
    position = b * LANES + lax.broadcasted_iota(jnp.int32, (8, LANES), 1)
    return jnp.where(position < length, 0.0, NEG)


def spatial_kernel(
    device_ref,
    right_ref,
    lengths_ref,
    mask_ref,
    slots_ref,
    out_ref,
    query_ref,
    key_ref,
    value_ref,
    attended_ref,
):
    order = cycle_order(right_ref)
    parity = device_ref[0] % 2
    views = [jnp.where(parity == 0, order[2 * m], order[2 * m + 1]) for m in range(3)]
    blocks = mask_ref.shape[-1]

    def query_rows(m, b, row8):
        rows = jnp.zeros((8, LANES), jnp.float32)
        for other in range(blocks):
            allowed = mask_ref[0, views[m], b, other] > 0
            rows = jnp.where(row8 == other, jnp.where(allowed, 0.0, NEG), rows)
        return rows

    def key_bias(m, b):
        return live_bias(lengths_ref[0, views[m]], b)

    unpack(slots_ref, key_bias, query_rows, query_ref, key_ref, value_ref)
    wide = 2 * LANES
    for m in range(3):
        for i in range(blocks // 2):
            first = max(0, 2 * i - 2) * LANES
            last = min(blocks, 2 * i + 4) * LANES
            spans = [slice(first, last)]
            if first > 0:
                spans.append(slice(0, LANES))
            lanes = slice(i * wide, (i + 1) * wide)
            attended_ref[m, :, lanes] = attend(
                query_ref[m, :, lanes],
                [(key_ref[m, span, :], value_ref[m, :, span]) for span in spans],
            )
    pack_outputs(attended_ref, out_ref)


def cross_kernel(
    device_ref,
    right_ref,
    lengths_ref,
    slots_ref,
    out_ref,
    query_ref,
    key_ref,
    value_ref,
    attended_ref,
):
    order = cycle_order(right_ref)
    parity = device_ref[0] % 2
    views = [jnp.where(parity == 0, order[2 * m + 1], order[2 * m]) for m in range(3)]

    def query_rows(m, b, row8):
        return jnp.zeros((8, LANES), jnp.float32)

    def key_bias(m, b):
        return live_bias(lengths_ref[0, views[m]], b)

    unpack(slots_ref, key_bias, query_rows, query_ref, key_ref, value_ref)
    wide = 2 * LANES
    for m in range(3):
        second = jnp.where(parity == 0, (m + 2) % 3, (m + 1) % 3)
        for i in range(query_ref.shape[2] // wide):
            lanes = slice(i * wide, (i + 1) * wide)
            attended_ref[m, :, lanes] = attend(
                query_ref[m, :, lanes],
                [(key_ref[m], value_ref[m]), (key_ref[second], value_ref[second])],
            )
    pack_outputs(attended_ref, out_ref)


def merge_heads(slots_ref, merged_ref):
    low = low_lanes(OUT_ROWS)
    tiles = [[], [], []]
    for head in range(HEADS):
        even = slots_ref[2 * head].astype(jnp.float32)
        odd = slots_ref[2 * head + 1].astype(jnp.float32)
        lower = jnp.where(low, even, swap(odd))
        upper = jnp.where(low, swap(even), odd)
        tiles[0].append(lower[:HS])
        tiles[1].append(upper[:HS])
        tiles[2].append(lower[HS:])
        tiles[2].append(upper[HS : 2 * HS - TOP])
    for m in range(3):
        merged = jnp.concatenate(tiles[m], axis=0)
        merged_ref[m * LANES : (m + 1) * LANES, :] = merged.T.astype(jnp.bfloat16)


def live_rows(device_ref, length):
    position = device_ref[0] * TILE + lax.broadcasted_iota(jnp.int32, (TILE, 1), 0)
    return (position < length).astype(jnp.float32)


def middle_kernel(
    device_ref,
    right_ref,
    lengths_ref,
    slots_ref,
    tokens_ref,
    mix_ref,
    gain_ref,
    weight_ref,
    middle_ref,
    out_ref,
    merged_ref,
    normed_ref,
    turned_ref,
):
    order = cycle_order(right_ref)
    merge_heads(slots_ref, merged_ref)
    for j in range(6):
        rows = slice(j * TILE, (j + 1) * TILE)
        branch = jnp.dot(merged_ref[rows, :], mix_ref[...], preferred_element_type=jnp.float32)
        live = live_rows(device_ref, lengths_ref[0, order[j]])
        middle = (tokens_ref[0, order[j]].astype(jnp.float32) + live * branch).astype(jnp.bfloat16)
        middle_ref[rows, :] = middle
        normed_ref[rows, :] = normalise(middle.astype(jnp.float32), gain_ref[...])
    project_and_pack(normed_ref, weight_ref, turned_ref, out_ref, True)


def finish_kernel(
    device_ref, right_ref, lengths_ref, slots_ref, middle_ref, mix_ref, out_ref, merged_ref
):
    order = cycle_order(right_ref)
    merge_heads(slots_ref, merged_ref)
    for j in range(6):
        rows = slice(j * TILE, (j + 1) * TILE)
        branch = jnp.dot(merged_ref[rows, :], mix_ref[...], preferred_element_type=jnp.float32)
        live = live_rows(device_ref, lengths_ref[0, order[j]])
        out_ref[0, order[j]] = (middle_ref[rows, :].astype(jnp.float32) + live * branch).astype(
            jnp.bfloat16
        )


def call(kernel, scalars, arrays, out_shape, scratch, name):
    smem = pl.BlockSpec(memory_space=pltpu.SMEM)
    vmem = pl.BlockSpec(memory_space=pltpu.VMEM)
    return pl.pallas_call(
        kernel,
        out_shape=out_shape,
        in_specs=[smem] * len(scalars) + [vmem] * len(arrays),
        out_specs=jax.tree.map(lambda _: vmem, out_shape),
        scratch_shapes=scratch,
        compiler_params=pltpu.CompilerParams(vmem_limit_bytes=VMEM),
        name=name,
    )(*scalars, *arrays)


def exchange(slots):
    return lax.all_to_all(slots, "sp", split_axis=0, concat_axis=0, tiled=True)


def fast_shards(
    tokens,
    gain_spatial,
    qkv_spatial,
    out_spatial,
    gain_cross,
    qkv_cross,
    out_cross,
    lengths,
    left_view,
    right_view,
    window_mask,
):
    width = tokens.shape[-1]
    inner = out_spatial.shape[0]
    devices_sp = lax.axis_size("sp")
    view_len = TILE * devices_sp
    rows = 6 * TILE
    device = lax.axis_index("sp").astype(jnp.int32).reshape(1)
    qkv_slots = jax.ShapeDtypeStruct((devices_sp, QKV_ROWS, LANES), jnp.bfloat16)
    out_slots = jax.ShapeDtypeStruct((devices_sp, OUT_ROWS, LANES), jnp.bfloat16)
    turned = pltpu.VMEM((3 * inner, rows), jnp.float32)
    normed = pltpu.VMEM((rows, width), jnp.bfloat16)
    merged = pltpu.VMEM((rows, inner), jnp.bfloat16)
    heads = [
        pltpu.VMEM((3, LANES, view_len), jnp.bfloat16),
        pltpu.VMEM((3, view_len, LANES), jnp.bfloat16),
        pltpu.VMEM((3, HS + 8, view_len), jnp.bfloat16),
        pltpu.VMEM((3, HS, view_len), jnp.float32),
    ]
    slots = call(
        project_kernel,
        [right_view],
        [tokens, gain_spatial, qkv_spatial.T],
        qkv_slots,
        [normed, turned],
        "project",
    )
    attended = call(
        spatial_kernel,
        [device, right_view, lengths, window_mask],
        [exchange(slots)],
        out_slots,
        heads,
        "spatial",
    )
    middle, slots = call(
        middle_kernel,
        [device, right_view, lengths],
        [exchange(attended), tokens, out_spatial, gain_cross, qkv_cross.T],
        (jax.ShapeDtypeStruct((rows, width), jnp.bfloat16), qkv_slots),
        [merged, normed, turned],
        "middle",
    )
    attended = call(
        cross_kernel,
        [device, right_view, lengths],
        [exchange(slots)],
        out_slots,
        heads,
        "cross",
    )
    return call(
        finish_kernel,
        [device, right_view, lengths],
        [exchange(attended), middle, out_cross],
        jax.ShapeDtypeStruct(tokens.shape, jnp.bfloat16),
        [merged],
        "finish",
    )


def rms_norm(values, gain):
    floats = values.astype(jnp.float32)
    square = jnp.mean(floats * floats, axis=-1, keepdims=True)
    return (floats * lax.rsqrt(square + EPSILON) * gain).astype(jnp.bfloat16)


def to_frames(block, heads):
    frames, views, tile_len, inner = block.shape
    head_size = inner // heads
    moved = block.reshape(frames, views, tile_len, heads, head_size).transpose(0, 3, 1, 2, 4)
    return moved.reshape(frames, heads, views, tile_len * head_size)


def from_units(units, frames, views, tile_len, heads):
    head_size = units.shape[-1] // tile_len
    moved = units.reshape(frames, heads, views, tile_len, head_size).transpose(0, 2, 3, 1, 4)
    return moved.reshape(frames, views, tile_len, heads * head_size)


def attend_one(operands):
    query, keys, values, allow = operands
    scores = jnp.einsum("qd,kd->qk", query, keys, preferred_element_type=jnp.float32) * query.shape[
        -1
    ] ** (-0.5)
    scores = jnp.where(allow, scores, -1e30)
    top = jnp.max(scores, axis=-1, keepdims=True)
    weights = jnp.where(allow, jnp.exp(scores - top), 0.0)
    probs = (weights / jnp.sum(weights, axis=-1, keepdims=True)).astype(jnp.bfloat16)
    return jnp.einsum("qk,kd->qd", probs, values, preferred_element_type=jnp.float32).astype(
        jnp.bfloat16
    )


def general_shards(
    tokens,
    gain_spatial,
    qkv_spatial,
    out_spatial,
    gain_cross,
    qkv_cross,
    out_cross,
    lengths,
    left_view,
    right_view,
    window_mask,
):
    frames, views, tile_len, width = tokens.shape
    inner = out_spatial.shape[0]
    head_size = inner // HEADS
    devices_sp = lax.axis_size("sp")
    device = lax.axis_index("sp")
    view_len = tile_len * devices_sp
    blocks = window_mask.shape[-1]
    block_len = view_len // blocks
    positions = device * tile_len + jnp.arange(tile_len, dtype=jnp.int32)
    live_rows = (positions[None, None, :] < lengths[:, :, None]).astype(jnp.float32)[..., None]
    key_pos = jnp.arange(view_len, dtype=jnp.int32)
    units_dev = frames * HEADS * views // devices_sp
    unit_ids = device * units_dev + jnp.arange(units_dev, dtype=jnp.int32)
    frame_ids = unit_ids // (HEADS * views)
    view_ids = unit_ids % views
    flat_ids = frame_ids * views + view_ids
    flat_len = lengths.reshape(-1)
    own_len = jnp.take(flat_len, flat_ids)
    total_units = frames * HEADS * views
    normed = rms_norm(tokens, gain_spatial)
    projected = jnp.einsum(
        "fvtd,de->fvte", normed, qkv_spatial, preferred_element_type=jnp.float32
    ).astype(jnp.bfloat16)
    stacked = jnp.stack(
        [
            to_frames(projected[..., which * inner : (which + 1) * inner], HEADS)
            for which in range(3)
        ],
        axis=3,
    )
    stacked = stacked.reshape(total_units, 3, tile_len * head_size)
    gathered = lax.all_to_all(stacked, "sp", split_axis=0, concat_axis=2, tiled=True)
    gathered = gathered.reshape(units_dev, 3, view_len, head_size)
    masks = jnp.take(window_mask.reshape(-1, blocks, blocks), flat_ids, axis=0) > 0
    allow = jnp.broadcast_to(
        masks[:, :, None, :, None], (units_dev, blocks, block_len, blocks, block_len)
    )
    allow = allow.reshape(units_dev, view_len, view_len) & (
        key_pos[None, None, :] < own_len[:, None, None]
    )
    spatial_out = lax.map(attend_one, (gathered[:, 0], gathered[:, 1], gathered[:, 2], allow))
    returned = lax.all_to_all(
        spatial_out.reshape(units_dev, view_len * head_size),
        "sp",
        split_axis=1,
        concat_axis=0,
        tiled=True,
    )
    attended = from_units(returned, frames, views, tile_len, HEADS)
    branch = jnp.einsum("fvte,ed->fvtd", attended, out_spatial, preferred_element_type=jnp.float32)
    middle = (tokens.astype(jnp.float32) + live_rows * branch).astype(jnp.bfloat16)
    normed_cross = rms_norm(middle, gain_cross)
    projected = jnp.einsum(
        "fvtd,de->fvte", normed_cross, qkv_cross, preferred_element_type=jnp.float32
    ).astype(jnp.bfloat16)
    query_fr, key_fr, value_fr = [
        to_frames(projected[..., which * inner : (which + 1) * inner], HEADS) for which in range(3)
    ]
    left_ids = jnp.take(left_view.reshape(-1), flat_ids)
    right_ids = jnp.take(right_view.reshape(-1), flat_ids)
    view_iota = jnp.arange(views, dtype=jnp.int32)
    pick_left = (left_view[:, :, None] == view_iota).astype(jnp.bfloat16)
    pick_right = (right_view[:, :, None] == view_iota).astype(jnp.bfloat16)

    def select(pick, source):
        return jnp.einsum(
            "fvw,fhwx->fhvx", pick, source, preferred_element_type=jnp.float32
        ).astype(jnp.bfloat16)

    packed = jnp.stack(
        [
            query_fr,
            select(pick_left, key_fr),
            select(pick_left, value_fr),
            select(pick_right, key_fr),
            select(pick_right, value_fr),
        ],
        axis=3,
    )
    packed = packed.reshape(total_units, 5, tile_len * head_size)
    arrived = lax.all_to_all(packed, "sp", split_axis=0, concat_axis=2, tiled=True)
    cross_query = arrived[:, 0]
    left_kv = arrived[:, 1:3]
    right_kv = arrived[:, 3:5]
    cross_keys = jnp.concatenate([left_kv[:, 0], right_kv[:, 0]], axis=1).reshape(
        units_dev, 2 * view_len, head_size
    )
    cross_values = jnp.concatenate([left_kv[:, 1], right_kv[:, 1]], axis=1).reshape(
        units_dev, 2 * view_len, head_size
    )
    left_len = jnp.take(flat_len, frame_ids * views + left_ids)
    right_len = jnp.take(flat_len, frame_ids * views + right_ids)
    allow_cross = jnp.concatenate(
        [key_pos[None, :] < left_len[:, None], key_pos[None, :] < right_len[:, None]], axis=1
    )[:, None, :]
    cross_out = lax.map(
        attend_one,
        (
            cross_query.reshape(units_dev, view_len, head_size),
            cross_keys,
            cross_values,
            allow_cross,
        ),
    )
    returned = lax.all_to_all(
        cross_out.reshape(units_dev, view_len * head_size),
        "sp",
        split_axis=1,
        concat_axis=0,
        tiled=True,
    )
    attended = from_units(returned, frames, views, tile_len, HEADS)
    branch = jnp.einsum("fvte,ed->fvtd", attended, out_cross, preferred_element_type=jnp.float32)
    return (middle.astype(jnp.float32) + live_rows * branch).astype(jnp.bfloat16)


def shards(*args):
    tokens, mask = args[0], args[-1]
    sizes = (tokens.shape[0], tokens.shape[1], tokens.shape[2], mask.shape[-1])
    if sizes == (1, 6, TILE, 8) and lax.axis_size("sp") == 2 * HEADS:
        return fast_shards(*args)
    return general_shards(*args)


def solution(mesh):
    in_specs = (
        P("grp", None, "sp", None),
        P(),
        P(),
        P(),
        P(),
        P(),
        P(),
        P("grp", None),
        P("grp", None),
        P("grp", None),
        P("grp", None, None, None),
    )
    out_specs = P("grp", None, "sp", None)
    return jax.shard_map(shards, mesh=mesh, in_specs=in_specs, out_specs=out_specs, check_vma=False)
```

```python
import functools

import jax
import jax.numpy as jnp
from jax import lax
from jax.experimental import pallas as pl
from jax.experimental.pallas import tpu as pltpu
from jax.sharding import PartitionSpec as P

HEADS = 8
EPSILON = 1e-06


HS = 72
TILE = 64
LANES = 128
TOP = 40
QKV_ROWS = 336
OUT_ROWS = 112
NEG = -1e30
FACTOR = HS**-0.5 * 1.4426950408889634
VMEM = 24 * 1024 * 1024


def cycle_order(right_ref):
    order = [jnp.int32(0)]
    for _ in range(5):
        order.append(right_ref[0, order[-1]])
    return order


def low_lanes(rows):
    return lax.broadcasted_iota(jnp.int32, (rows, LANES), 1) < TILE


def swap(tile):
    return pltpu.roll(tile, TILE, 1)


def side_by_side(first, first_half, second, second_half):
    left = first if first_half == 0 else swap(first)
    right = second if second_half == 1 else swap(second)
    return jnp.where(low_lanes(first.shape[0]), left, right)


def fold_third(tile, half):
    bottom = jnp.concatenate([tile[TOP:], jnp.zeros((2 * TOP - HS, LANES), jnp.float32)], axis=0)
    return side_by_side(tile[:TOP], half, bottom, half)


def normalise(floats, gain):
    square = jnp.mean(floats * floats, axis=-1, keepdims=True)
    return (floats * lax.rsqrt(square + EPSILON) * gain[None, :]).astype(jnp.bfloat16)


def project_and_pack(normed_ref, weights, slots_ref, copies_out, cross):
    for pair, (copies, weight_ref) in enumerate(weights):
        for copy in copies:
            copy.wait()
        turned = lax.dot_general(
            weight_ref[...],
            normed_ref[...],
            (((1,), (1,)), ((), ())),
            preferred_element_type=jnp.float32,
        )
        for inside in range(2):

            def item(which, m):
                row = (which * 2 + inside) * HS
                tile = turned[row : row + HS, m * LANES : (m + 1) * LANES]
                return tile * FACTOR if which == 0 else tile

            for parity in range(2):
                other = 1 - parity if cross else parity
                rows = [side_by_side(item(0, m), parity, item(1, m), other) for m in range(3)]
                rows.append(side_by_side(item(2, 0), other, item(2, 1), other))
                rows.append(fold_third(item(2, 2), other))
                rows.append(jnp.zeros((QKV_ROWS - 4 * HS - TOP, LANES), jnp.float32))
                slot = (pair * 2 + inside) * 2 + parity
                slots_ref[slot] = jnp.concatenate(rows, axis=0).astype(jnp.bfloat16)
        copies_out[pair].start()
    for copy in copies_out:
        copy.wait()


def weight_copies(source_ref, held_ref, sems):
    inner = source_ref.shape[0] // 3
    pairs, rows, _ = held_ref.shape
    rows = rows // 3
    weights = []
    for pair in range(pairs):
        copies = [
            pltpu.make_async_copy(
                source_ref.at[pl.ds(which * inner + pair * rows, rows)],
                held_ref.at[pair, pl.ds(which * rows, rows)],
                sems.at[pair * 3 + which],
            )
            for which in range(3)
        ]
        weights.append((copies, held_ref.at[pair]))
    return weights


def slot_copies(slots_ref, out_ref, sems):
    pairs = HEADS // 2
    step = slots_ref.shape[0] // pairs
    return [
        pltpu.make_async_copy(
            slots_ref.at[pl.ds(pair * step, step)],
            out_ref.at[pl.ds(pair * step, step)],
            sems.at[pair],
        )
        for pair in range(pairs)
    ]


def project_kernel(
    right_hbm,
    tokens_hbm,
    gain_hbm,
    weight_hbm,
    out_hbm,
    right_ref,
    tokens_ref,
    gain_ref,
    weight_ref,
    normed_ref,
    slots_ref,
    in_sems,
    weight_sems,
    out_sems,
):
    small = [
        pltpu.make_async_copy(source, held, in_sems.at[i])
        for i, (source, held) in enumerate(
            [(right_hbm, right_ref), (gain_hbm, gain_ref), (tokens_hbm, tokens_ref)]
        )
    ]
    weights = weight_copies(weight_hbm, weight_ref, weight_sems)
    for copy in small:
        copy.start()
    for copies, _ in weights:
        for copy in copies:
            copy.start()
    for copy in small:
        copy.wait()
    order = cycle_order(right_ref)
    for j in range(6):
        floats = tokens_ref[0, order[j]].astype(jnp.float32)
        normed_ref[j * TILE : (j + 1) * TILE, :] = normalise(floats, gain_ref[...])
    project_and_pack(
        normed_ref, weights, slots_ref, slot_copies(slots_ref, out_hbm, out_sems), False
    )


def unpack(slots_ref, key_bias, query_rows, query_ref, key_ref, value_ref):
    blocks = slots_ref.shape[0] // 2
    low = low_lanes(QKV_ROWS)
    row8 = lax.broadcasted_iota(jnp.int32, (8, LANES), 0)
    pad = jnp.zeros((LANES - HS - 16, LANES), jnp.float32)
    first_row = jnp.where(row8 == 0, 1.0, 0.0)
    for b in range(blocks):
        span = slice(b * LANES, (b + 1) * LANES)
        even = slots_ref[2 * b].astype(jnp.float32)
        odd = slots_ref[2 * b + 1].astype(jnp.float32)
        lower = jnp.where(low, even, swap(odd))
        upper = jnp.where(low, swap(even), odd)
        own_block = jnp.where(row8 == b, 1.0, 0.0)
        values = [
            lower[3 * HS : 4 * HS],
            upper[3 * HS : 4 * HS],
            jnp.concatenate(
                [lower[4 * HS : 4 * HS + TOP], upper[4 * HS : 5 * HS - TOP]], axis=0
            ),
        ]
        for m in range(3):
            query = jnp.concatenate(
                [lower[m * HS : (m + 1) * HS], query_rows(m, b, row8), first_row, pad], axis=0
            )
            query_ref[m, :, span] = query.astype(jnp.bfloat16)
            live = jnp.where(row8 == 0, key_bias(m, b), 0.0)
            key = jnp.concatenate([upper[m * HS : (m + 1) * HS], own_block, live, pad], axis=0)
            key_ref[m, span, :] = key.T.astype(jnp.bfloat16)
            value_ref[m, :, span] = jnp.concatenate([values[m], first_row], axis=0).astype(
                jnp.bfloat16
            )


def attend(jobs, query_ref, key_ref, value_ref, attended_ref):
    def scores(job):
        m, lanes, parts = job
        query = query_ref[m, :, lanes]
        return [
            jnp.dot(key_ref[n, span, :], query, preferred_element_type=jnp.float32)
            for n, span in parts
        ]

    def finish(job, found):
        m, lanes, parts = job
        top = functools.reduce(
            jnp.maximum, [jnp.max(score, axis=0, keepdims=True) for score in found]
        )
        total = None
        for score, (n, span) in zip(found, parts):
            weights = jnp.exp2(score - top).astype(jnp.bfloat16)
            term = jnp.dot(value_ref[n, :, span], weights, preferred_element_type=jnp.float32)
            total = term if total is None else total + term
        attended_ref[m, :, lanes] = total[:HS] / total[HS : HS + 1]

    ahead = None
    for job in jobs:
        found = scores(job)
        if ahead is not None:
            finish(*ahead)
        ahead = (job, found)
    finish(*ahead)


def pack_outputs(attended_ref, out_ref):
    for b in range(out_ref.shape[0] // 2):
        span = slice(b * LANES, (b + 1) * LANES)
        tiles = [attended_ref[m, :, span] for m in range(3)]
        for half in range(2):
            rows = [side_by_side(tiles[0], half, tiles[1], half), fold_third(tiles[2], half)]
            out_ref[2 * b + half] = jnp.concatenate(rows, axis=0).astype(jnp.bfloat16)


def live_bias(length, b):
    position = b * LANES + lax.broadcasted_iota(jnp.int32, (8, LANES), 1)
    return jnp.where(position < length, 0.0, NEG)


def spatial_kernel(
    device_ref,
    right_ref,
    lengths_ref,
    mask_ref,
    slots_ref,
    out_ref,
    query_ref,
    key_ref,
    value_ref,
    attended_ref,
):
    order = cycle_order(right_ref)
    parity = device_ref[0] % 2
    views = [jnp.where(parity == 0, order[2 * m], order[2 * m + 1]) for m in range(3)]
    blocks = mask_ref.shape[-1]

    def query_rows(m, b, row8):
        rows = jnp.zeros((8, LANES), jnp.float32)
        for other in range(blocks):
            allowed = mask_ref[0, views[m], b, other] > 0
            rows = jnp.where(row8 == other, jnp.where(allowed, 0.0, NEG), rows)
        return rows

    def key_bias(m, b):
        return live_bias(lengths_ref[0, views[m]], b)

    unpack(slots_ref, key_bias, query_rows, query_ref, key_ref, value_ref)
    wide = 2 * LANES
    jobs = []
    for m in range(3):
        for i in range(blocks // 2):
            first = max(0, 2 * i - 2) * LANES
            last = min(blocks, 2 * i + 4) * LANES
            spans = [slice(first, last)]
            if first > 0:
                spans.append(slice(0, LANES))
            jobs.append((m, slice(i * wide, (i + 1) * wide), [(m, span) for span in spans]))
    attend(jobs, query_ref, key_ref, value_ref, attended_ref)
    pack_outputs(attended_ref, out_ref)


def cross_kernel(
    device_ref,
    right_ref,
    lengths_ref,
    slots_ref,
    out_ref,
    query_ref,
    key_ref,
    value_ref,
    attended_ref,
):
    order = cycle_order(right_ref)
    parity = device_ref[0] % 2
    views = [jnp.where(parity == 0, order[2 * m + 1], order[2 * m]) for m in range(3)]

    def query_rows(m, b, row8):
        return jnp.zeros((8, LANES), jnp.float32)

    def key_bias(m, b):
        return live_bias(lengths_ref[0, views[m]], b)

    unpack(slots_ref, key_bias, query_rows, query_ref, key_ref, value_ref)
    wide = 2 * LANES
    every = slice(0, key_ref.shape[1])
    jobs = []
    for m in range(3):
        second = jnp.where(parity == 0, (m + 2) % 3, (m + 1) % 3)
        for i in range(query_ref.shape[2] // wide):
            jobs.append((m, slice(i * wide, (i + 1) * wide), [(m, every), (second, every)]))
    attend(jobs, query_ref, key_ref, value_ref, attended_ref)
    pack_outputs(attended_ref, out_ref)


def merge_heads(slots_ref, merged_ref):
    low = low_lanes(OUT_ROWS)
    tiles = [[], [], []]
    for head in range(HEADS):
        even = slots_ref[2 * head].astype(jnp.float32)
        odd = slots_ref[2 * head + 1].astype(jnp.float32)
        lower = jnp.where(low, even, swap(odd))
        upper = jnp.where(low, swap(even), odd)
        tiles[0].append(lower[:HS])
        tiles[1].append(upper[:HS])
        tiles[2].append(lower[HS:])
        tiles[2].append(upper[HS : 2 * HS - TOP])
    for m in range(3):
        merged = jnp.concatenate(tiles[m], axis=0)
        merged_ref[m * LANES : (m + 1) * LANES, :] = merged.T.astype(jnp.bfloat16)


def live_rows(device_ref, length):
    position = device_ref[0] * TILE + lax.broadcasted_iota(jnp.int32, (TILE, 1), 0)
    return (position < length).astype(jnp.float32)


def middle_kernel(
    device_ref,
    right_ref,
    lengths_ref,
    slots_ref,
    tokens_ref,
    mix_ref,
    gain_ref,
    weight_hbm,
    middle_ref,
    out_hbm,
    merged_ref,
    weight_ref,
    normed_ref,
    sent_ref,
    weight_sems,
    out_sems,
):
    weights = weight_copies(weight_hbm, weight_ref, weight_sems)
    for copies, _ in weights:
        for copy in copies:
            copy.start()
    order = cycle_order(right_ref)
    merge_heads(slots_ref, merged_ref)
    branch = jnp.dot(merged_ref[...], mix_ref[...], preferred_element_type=jnp.float32)
    for j in range(6):
        rows = slice(j * TILE, (j + 1) * TILE)
        live = live_rows(device_ref, lengths_ref[0, order[j]])
        middle = tokens_ref[0, order[j]].astype(jnp.float32) + live * branch[rows]
        middle = middle.astype(jnp.bfloat16)
        middle_ref[rows, :] = middle
        normed_ref[rows, :] = normalise(middle.astype(jnp.float32), gain_ref[...])
    project_and_pack(
        normed_ref, weights, sent_ref, slot_copies(sent_ref, out_hbm, out_sems), True
    )


def finish_kernel(
    device_ref,
    right_ref,
    lengths_ref,
    slots_ref,
    middle_ref,
    mix_ref,
    out_hbm,
    merged_ref,
    result_ref,
    sems,
):
    order = cycle_order(right_ref)
    merge_heads(slots_ref, merged_ref)
    branch = jnp.dot(merged_ref[...], mix_ref[...], preferred_element_type=jnp.float32)
    copies = []
    for j in range(6):
        rows = slice(j * TILE, (j + 1) * TILE)
        live = live_rows(device_ref, lengths_ref[0, order[j]])
        result = middle_ref[rows, :].astype(jnp.float32) + live * branch[rows]
        result_ref[j] = result.astype(jnp.bfloat16)
        copy = pltpu.make_async_copy(result_ref.at[j], out_hbm.at[0, order[j]], sems.at[j])
        copy.start()
        copies.append(copy)
    for copy in copies:
        copy.wait()


SMEM_SPEC = pl.BlockSpec(memory_space=pltpu.SMEM)
VMEM_SPEC = pl.BlockSpec(memory_space=pltpu.VMEM)
HBM_SPEC = pl.BlockSpec(memory_space=pltpu.HBM)


def in_hbm(array):
    return pltpu.with_memory_space_constraint(array, pltpu.HBM)


def call(kernel, in_specs, args, out_specs, out_shape, scratch, name):
    return pl.pallas_call(
        kernel,
        out_shape=out_shape,
        in_specs=in_specs,
        out_specs=out_specs,
        scratch_shapes=scratch,
        compiler_params=pltpu.CompilerParams(vmem_limit_bytes=VMEM),
        name=name,
    )(*args)


def exchange(slots):
    return lax.all_to_all(slots, "sp", split_axis=0, concat_axis=0, tiled=True)


def fast_shards(
    tokens,
    gain_spatial,
    qkv_spatial,
    out_spatial,
    gain_cross,
    qkv_cross,
    out_cross,
    lengths,
    left_view,
    right_view,
    window_mask,
):
    width = tokens.shape[-1]
    inner = out_spatial.shape[0]
    devices_sp = lax.axis_size("sp")
    view_len = TILE * devices_sp
    rows = 6 * TILE
    device = lax.axis_index("sp").astype(jnp.int32).reshape(1)
    qkv_slots = jax.ShapeDtypeStruct((devices_sp, QKV_ROWS, LANES), jnp.bfloat16)
    out_slots = jax.ShapeDtypeStruct((devices_sp, OUT_ROWS, LANES), jnp.bfloat16)
    normed = pltpu.VMEM((rows, width), jnp.bfloat16)
    merged = pltpu.VMEM((rows, inner), jnp.bfloat16)
    pairs = HEADS // 2
    weights = pltpu.VMEM((pairs, 3 * inner // pairs, width), jnp.bfloat16)
    slots_held = pltpu.VMEM(qkv_slots.shape, jnp.bfloat16)
    weight_sems = pltpu.SemaphoreType.DMA((3 * pairs,))
    slot_sems = pltpu.SemaphoreType.DMA((pairs,))
    heads = [
        pltpu.VMEM((3, LANES, view_len), jnp.bfloat16),
        pltpu.VMEM((3, view_len, LANES), jnp.bfloat16),
        pltpu.VMEM((3, HS + 8, view_len), jnp.bfloat16),
        pltpu.VMEM((3, HS, view_len), jnp.float32),
    ]
    slots = call(
        project_kernel,
        [HBM_SPEC] * 4,
        [in_hbm(x) for x in (right_view, tokens, gain_spatial, qkv_spatial.T)],
        HBM_SPEC,
        qkv_slots,
        [
            pltpu.SMEM(right_view.shape, jnp.int32),
            pltpu.VMEM(tokens.shape, jnp.bfloat16),
            pltpu.VMEM((width,), jnp.float32),
            weights,
            normed,
            slots_held,
            pltpu.SemaphoreType.DMA((3,)),
            weight_sems,
            slot_sems,
        ],
        "project",
    )
    attended = call(
        spatial_kernel,
        [SMEM_SPEC] * 4 + [VMEM_SPEC],
        [device, right_view, lengths, window_mask, exchange(slots)],
        VMEM_SPEC,
        out_slots,
        heads,
        "spatial",
    )
    middle, slots = call(
        middle_kernel,
        [SMEM_SPEC] * 3 + [VMEM_SPEC] * 4 + [HBM_SPEC],
        [
            device,
            right_view,
            lengths,
            exchange(attended),
            tokens,
            out_spatial,
            gain_cross,
            in_hbm(qkv_cross.T),
        ],
        (VMEM_SPEC, HBM_SPEC),
        (jax.ShapeDtypeStruct((rows, width), jnp.bfloat16), qkv_slots),
        [merged, weights, normed, slots_held, weight_sems, slot_sems],
        "middle",
    )
    attended = call(
        cross_kernel,
        [SMEM_SPEC] * 3 + [VMEM_SPEC],
        [device, right_view, lengths, exchange(slots)],
        VMEM_SPEC,
        out_slots,
        heads,
        "cross",
    )
    return call(
        finish_kernel,
        [SMEM_SPEC] * 3 + [VMEM_SPEC] * 3,
        [device, right_view, lengths, exchange(attended), middle, out_cross],
        HBM_SPEC,
        jax.ShapeDtypeStruct(tokens.shape, jnp.bfloat16),
        [merged, pltpu.VMEM((6, TILE, width), jnp.bfloat16), pltpu.SemaphoreType.DMA((6,))],
        "finish",
    )


def rms_norm(values, gain):
    floats = values.astype(jnp.float32)
    square = jnp.mean(floats * floats, axis=-1, keepdims=True)
    return (floats * lax.rsqrt(square + EPSILON) * gain).astype(jnp.bfloat16)


def to_frames(block, heads):
    frames, views, tile_len, inner = block.shape
    head_size = inner // heads
    moved = block.reshape(frames, views, tile_len, heads, head_size).transpose(0, 3, 1, 2, 4)
    return moved.reshape(frames, heads, views, tile_len * head_size)


def from_units(units, frames, views, tile_len, heads):
    head_size = units.shape[-1] // tile_len
    moved = units.reshape(frames, heads, views, tile_len, head_size).transpose(0, 2, 3, 1, 4)
    return moved.reshape(frames, views, tile_len, heads * head_size)


def attend_one(operands):
    query, keys, values, allow = operands
    scores = jnp.einsum("qd,kd->qk", query, keys, preferred_element_type=jnp.float32) * query.shape[
        -1
    ] ** (-0.5)
    scores = jnp.where(allow, scores, -1e30)
    top = jnp.max(scores, axis=-1, keepdims=True)
    weights = jnp.where(allow, jnp.exp(scores - top), 0.0)
    probs = (weights / jnp.sum(weights, axis=-1, keepdims=True)).astype(jnp.bfloat16)
    return jnp.einsum("qk,kd->qd", probs, values, preferred_element_type=jnp.float32).astype(
        jnp.bfloat16
    )


def general_shards(
    tokens,
    gain_spatial,
    qkv_spatial,
    out_spatial,
    gain_cross,
    qkv_cross,
    out_cross,
    lengths,
    left_view,
    right_view,
    window_mask,
):
    frames, views, tile_len, width = tokens.shape
    inner = out_spatial.shape[0]
    head_size = inner // HEADS
    devices_sp = lax.axis_size("sp")
    device = lax.axis_index("sp")
    view_len = tile_len * devices_sp
    blocks = window_mask.shape[-1]
    block_len = view_len // blocks
    positions = device * tile_len + jnp.arange(tile_len, dtype=jnp.int32)
    live_rows = (positions[None, None, :] < lengths[:, :, None]).astype(jnp.float32)[..., None]
    key_pos = jnp.arange(view_len, dtype=jnp.int32)
    units_dev = frames * HEADS * views // devices_sp
    unit_ids = device * units_dev + jnp.arange(units_dev, dtype=jnp.int32)
    frame_ids = unit_ids // (HEADS * views)
    view_ids = unit_ids % views
    flat_ids = frame_ids * views + view_ids
    flat_len = lengths.reshape(-1)
    own_len = jnp.take(flat_len, flat_ids)
    total_units = frames * HEADS * views
    normed = rms_norm(tokens, gain_spatial)
    projected = jnp.einsum(
        "fvtd,de->fvte", normed, qkv_spatial, preferred_element_type=jnp.float32
    ).astype(jnp.bfloat16)
    stacked = jnp.stack(
        [
            to_frames(projected[..., which * inner : (which + 1) * inner], HEADS)
            for which in range(3)
        ],
        axis=3,
    )
    stacked = stacked.reshape(total_units, 3, tile_len * head_size)
    gathered = lax.all_to_all(stacked, "sp", split_axis=0, concat_axis=2, tiled=True)
    gathered = gathered.reshape(units_dev, 3, view_len, head_size)
    masks = jnp.take(window_mask.reshape(-1, blocks, blocks), flat_ids, axis=0) > 0
    allow = jnp.broadcast_to(
        masks[:, :, None, :, None], (units_dev, blocks, block_len, blocks, block_len)
    )
    allow = allow.reshape(units_dev, view_len, view_len) & (
        key_pos[None, None, :] < own_len[:, None, None]
    )
    spatial_out = lax.map(attend_one, (gathered[:, 0], gathered[:, 1], gathered[:, 2], allow))
    returned = lax.all_to_all(
        spatial_out.reshape(units_dev, view_len * head_size),
        "sp",
        split_axis=1,
        concat_axis=0,
        tiled=True,
    )
    attended = from_units(returned, frames, views, tile_len, HEADS)
    branch = jnp.einsum("fvte,ed->fvtd", attended, out_spatial, preferred_element_type=jnp.float32)
    middle = (tokens.astype(jnp.float32) + live_rows * branch).astype(jnp.bfloat16)
    normed_cross = rms_norm(middle, gain_cross)
    projected = jnp.einsum(
        "fvtd,de->fvte", normed_cross, qkv_cross, preferred_element_type=jnp.float32
    ).astype(jnp.bfloat16)
    query_fr, key_fr, value_fr = [
        to_frames(projected[..., which * inner : (which + 1) * inner], HEADS) for which in range(3)
    ]
    left_ids = jnp.take(left_view.reshape(-1), flat_ids)
    right_ids = jnp.take(right_view.reshape(-1), flat_ids)
    view_iota = jnp.arange(views, dtype=jnp.int32)
    pick_left = (left_view[:, :, None] == view_iota).astype(jnp.bfloat16)
    pick_right = (right_view[:, :, None] == view_iota).astype(jnp.bfloat16)

    def select(pick, source):
        return jnp.einsum(
            "fvw,fhwx->fhvx", pick, source, preferred_element_type=jnp.float32
        ).astype(jnp.bfloat16)

    packed = jnp.stack(
        [
            query_fr,
            select(pick_left, key_fr),
            select(pick_left, value_fr),
            select(pick_right, key_fr),
            select(pick_right, value_fr),
        ],
        axis=3,
    )
    packed = packed.reshape(total_units, 5, tile_len * head_size)
    arrived = lax.all_to_all(packed, "sp", split_axis=0, concat_axis=2, tiled=True)
    cross_query = arrived[:, 0]
    left_kv = arrived[:, 1:3]
    right_kv = arrived[:, 3:5]
    cross_keys = jnp.concatenate([left_kv[:, 0], right_kv[:, 0]], axis=1).reshape(
        units_dev, 2 * view_len, head_size
    )
    cross_values = jnp.concatenate([left_kv[:, 1], right_kv[:, 1]], axis=1).reshape(
        units_dev, 2 * view_len, head_size
    )
    left_len = jnp.take(flat_len, frame_ids * views + left_ids)
    right_len = jnp.take(flat_len, frame_ids * views + right_ids)
    allow_cross = jnp.concatenate(
        [key_pos[None, :] < left_len[:, None], key_pos[None, :] < right_len[:, None]], axis=1
    )[:, None, :]
    cross_out = lax.map(
        attend_one,
        (
            cross_query.reshape(units_dev, view_len, head_size),
            cross_keys,
            cross_values,
            allow_cross,
        ),
    )
    returned = lax.all_to_all(
        cross_out.reshape(units_dev, view_len * head_size),
        "sp",
        split_axis=1,
        concat_axis=0,
        tiled=True,
    )
    attended = from_units(returned, frames, views, tile_len, HEADS)
    branch = jnp.einsum("fvte,ed->fvtd", attended, out_cross, preferred_element_type=jnp.float32)
    return (middle.astype(jnp.float32) + live_rows * branch).astype(jnp.bfloat16)


def shards(*args):
    tokens, mask = args[0], args[-1]
    sizes = (tokens.shape[0], tokens.shape[1], tokens.shape[2], mask.shape[-1])
    if sizes == (1, 6, TILE, 8) and lax.axis_size("sp") == 2 * HEADS:
        return fast_shards(*args)
    return general_shards(*args)


def solution(mesh):
    in_specs = (
        P("grp", None, "sp", None),
        P(),
        P(),
        P(),
        P(),
        P(),
        P(),
        P("grp", None),
        P("grp", None),
        P("grp", None),
        P("grp", None, None, None),
    )
    out_specs = P("grp", None, "sp", None)
    return jax.shard_map(shards, mesh=mesh, in_specs=in_specs, out_specs=out_specs, check_vma=False)
```

```python
import functools

import jax
import jax.numpy as jnp
from jax import lax
from jax.experimental import pallas as pl
from jax.experimental.pallas import tpu as pltpu
from jax.sharding import PartitionSpec as P

HEADS = 8
EPSILON = 1e-06


HS = 72
TILE = 64
LANES = 128
TOP = 40
QKV_ROWS = 328
OUT_ROWS = 112
NEG = -1e30
FACTOR = HS**-0.5 * 1.4426950408889634
FIRST_GROUPS = (4, 4)
SECOND_GROUPS = (6, 2)
AHEAD = 2
VMEM = 24 * 1024 * 1024


def cycle_order(right_ref):
    order = [jnp.int32(0)]
    for _ in range(5):
        order.append(right_ref[0, order[-1]])
    return order


def low_lanes(rows):
    return lax.broadcasted_iota(jnp.int32, (rows, LANES), 1) < TILE


def swap(tile):
    return pltpu.roll(tile, TILE, 1)


def side_by_side(first, first_half, second, second_half):
    left = first if first_half == 0 else swap(first)
    right = second if second_half == 1 else swap(second)
    return jnp.where(low_lanes(first.shape[0]), left, right)


def fold_third(tile, half):
    bottom = jnp.concatenate([tile[TOP:], jnp.zeros((2 * TOP - HS, LANES), jnp.float32)], axis=0)
    return side_by_side(tile[:TOP], half, bottom, half)


def normalise(floats, gain):
    square = jnp.mean(floats * floats, axis=-1, keepdims=True)
    return (floats * lax.rsqrt(square + EPSILON) * gain[None, :]).astype(jnp.bfloat16)


def project_and_pack(normed_ref, groups, slots_ref, cross, arrived, done):
    def project(weight_ref):
        return lax.dot_general(
            weight_ref[...],
            normed_ref[...],
            (((1,), (1,)), ((), ())),
            preferred_element_type=jnp.float32,
        )

    def pack(head, heads, turned):
        for inside in range(heads):

            def item(which, m):
                row = (which * heads + inside) * HS
                tile = turned[row : row + HS, m * LANES : (m + 1) * LANES]
                return tile * FACTOR if which == 0 else tile

            for parity in range(2):
                other = 1 - parity if cross else parity
                views = [2, 0, 1] if cross and parity == 0 else [0, 1, 2]
                rows = [
                    side_by_side(item(0, m), parity, item(1, views[m]), other) for m in range(3)
                ]
                rows.append(side_by_side(item(2, views[0]), other, item(2, views[1]), other))
                rows.append(fold_third(item(2, views[2]), other))
                slot = (head + inside) * 2 + parity
                slots_ref[slot] = jnp.concatenate(rows, axis=0).astype(jnp.bfloat16)

    ahead = None
    for group, (head, heads, weight_ref) in enumerate(groups):
        arrived(group)
        turned = project(weight_ref)
        if ahead is not None:
            pack(*ahead)
            done(group - 1)
        ahead = (head, heads, turned)
    pack(*ahead)
    done(len(groups) - 1)


def weight_groups(source_ref, held_ref, sems, sizes):
    inner = source_ref.shape[0] // 3
    copies, groups, head = [], [], 0
    for group, heads in enumerate(sizes):
        rows = heads * HS
        copies.append(
            [
                pltpu.make_async_copy(
                    source_ref.at[pl.ds(which * inner + head * HS, rows)],
                    held_ref.at[pl.ds(3 * head * HS + which * rows, rows)],
                    sems.at[group * 3 + which],
                )
                for which in range(3)
            ]
        )
        groups.append((head, heads, held_ref.at[pl.ds(3 * head * HS, 3 * rows)]))
        head += heads
    return copies, groups


def start_all(copies, priority=0):
    for copy in copies:
        copy.start(priority=priority)


def wait_all(copies):
    for copy in copies:
        copy.wait()


def slot_copies(slots_ref, out_ref, sems, sizes):
    copies, head = [], 0
    for group, heads in enumerate(sizes):
        span = pl.ds(2 * head, 2 * heads)
        copies.append(pltpu.make_async_copy(slots_ref.at[span], out_ref.at[span], sems.at[group]))
        head += heads
    return copies


def project_kernel(
    right_hbm,
    tokens_hbm,
    gain_hbm,
    weight_hbm,
    out_hbm,
    right_ref,
    tokens_ref,
    gain_ref,
    weight_ref,
    normed_ref,
    slots_ref,
    in_sems,
    weight_sems,
    out_sems,
):
    small = [
        pltpu.make_async_copy(right_hbm, right_ref, in_sems.at[0]),
        pltpu.make_async_copy(gain_hbm, gain_ref, in_sems.at[1]),
    ]
    views = [
        pltpu.make_async_copy(tokens_hbm.at[0, v], tokens_ref.at[0, v], in_sems.at[2 + v])
        for v in range(6)
    ]
    copies, groups = weight_groups(weight_hbm, weight_ref, weight_sems, FIRST_GROUPS)
    outgoing = slot_copies(slots_ref, out_hbm, out_sems, FIRST_GROUPS)
    start_all(small)
    start_all(views)
    for group in range(min(AHEAD, len(groups))):
        start_all(copies[group], 1)
    wait_all(small)
    order = cycle_order(right_ref)
    place = [sum(jnp.where(order[j] == v, j, 0) for j in range(6)) for v in range(6)]
    for v in range(6):
        views[v].wait()
        floats = tokens_ref[0, v].astype(jnp.float32)
        rows = pl.ds(pl.multiple_of(place[v] * TILE, TILE), TILE)
        normed_ref[rows, :] = normalise(floats, gain_ref[...])

    def arrived(group):
        wait_all(copies[group])
        if group + AHEAD < len(groups):
            start_all(copies[group + AHEAD], 1)

    project_and_pack(
        normed_ref, groups, slots_ref, False, arrived, lambda group: outgoing[group].start()
    )
    wait_all(outgoing)


def prepare_kernel(
    device_ref,
    right_ref,
    lengths_ref,
    mask_ref,
    tokens_ref,
    _,
    query_ref,
    key_ref,
    cross_ref,
    live_ref,
    ordered_ref,
):
    order = cycle_order(right_ref)
    parity = device_ref[0] % 2
    blocks = mask_ref.shape[-1]
    view_len = key_ref.shape[-1]
    position = lax.broadcasted_iota(jnp.int32, (8, view_len), 1)
    first = lax.broadcasted_iota(jnp.int32, (8, view_len), 0) == 0
    row8 = lax.broadcasted_iota(jnp.int32, (8, LANES), 0)

    def keys_of(view):
        return jnp.where(first & (position >= lengths_ref[0, view]), NEG, 0.0)

    for m in range(3):
        view = jnp.where(parity == 0, order[2 * m], order[2 * m + 1])
        other = jnp.where(parity == 0, order[(2 * m - 1) % 6], order[2 * m])
        key_ref[m] = keys_of(view)
        cross_ref[m] = keys_of(other)
        for b in range(blocks):
            rows = jnp.zeros((8, LANES), jnp.float32)
            for c in range(blocks):
                addend = jnp.where(mask_ref[0, view, b, c] > 0, 0.0, NEG)
                rows = jnp.where(row8 == c, addend, rows)
            query_ref[m, :, b * LANES : (b + 1) * LANES] = rows
    row = device_ref[0] * TILE + lax.broadcasted_iota(jnp.int32, (TILE, LANES), 0)
    for j in range(6):
        live_ref[j * TILE : (j + 1) * TILE, :] = jnp.where(
            row < lengths_ref[0, order[j]], 1.0, 0.0
        )
        ordered_ref[j * TILE : (j + 1) * TILE, :] = tokens_ref[0, order[j]]


def unpack(slots_ref, bias_ref, rows_ref, query_ref, key_ref, value_ref):
    blocks = slots_ref.shape[0] // 2
    low = low_lanes(QKV_ROWS)
    row8 = lax.broadcasted_iota(jnp.int32, (8, LANES), 0)
    pad = jnp.zeros((LANES - HS - 16, LANES), jnp.float32)
    zero = jnp.zeros((8, LANES), jnp.float32)
    first_row = jnp.where(row8 == 0, 1.0, 0.0)
    for b in range(blocks):
        span = slice(b * LANES, (b + 1) * LANES)
        even = slots_ref[2 * b].astype(jnp.float32)
        odd = slots_ref[2 * b + 1].astype(jnp.float32)
        lower = jnp.where(low, even, swap(odd))
        upper = jnp.where(low, swap(even), odd)
        own_block = zero if rows_ref is None else jnp.where(row8 == b, 1.0, 0.0)
        values = [
            lower[3 * HS : 4 * HS],
            upper[3 * HS : 4 * HS],
            jnp.concatenate(
                [lower[4 * HS : 4 * HS + TOP], upper[4 * HS : 5 * HS - TOP]], axis=0
            ),
        ]
        for m in range(3):
            rows = zero if rows_ref is None else rows_ref[m, :, span]
            query = jnp.concatenate([lower[m * HS : (m + 1) * HS], rows, first_row, pad], axis=0)
            query_ref[m, :, span] = query.astype(jnp.bfloat16)
            key = jnp.concatenate(
                [upper[m * HS : (m + 1) * HS], own_block, bias_ref[m, :, span], pad], axis=0
            )
            key_ref[m, span, :] = key.T.astype(jnp.bfloat16)
            value_ref[m, :, span] = jnp.concatenate([values[m], first_row], axis=0).astype(
                jnp.bfloat16
            )


def attend(jobs, query_ref, key_ref, value_ref, attended_ref):
    def scores(job):
        m, lanes, parts = job
        query = query_ref[m, :, lanes]
        return [
            jnp.dot(key_ref[n, span, :], query, preferred_element_type=jnp.float32)
            for n, span in parts
        ]

    def finish(job, found):
        m, lanes, parts = job
        top = functools.reduce(
            jnp.maximum, [jnp.max(score, axis=0, keepdims=True) for score in found]
        )
        total = None
        for score, (n, span) in zip(found, parts):
            weights = jnp.exp2(score - top).astype(jnp.bfloat16)
            term = jnp.dot(value_ref[n, :, span], weights, preferred_element_type=jnp.float32)
            total = term if total is None else total + term
        attended_ref[m, :, lanes] = total[:HS] / total[HS : HS + 1]

    ahead = None
    for job in jobs:
        found = scores(job)
        if ahead is not None:
            finish(*ahead)
        ahead = (job, found)
    finish(*ahead)


def pack_outputs(attended_ref, out_ref):
    for b in range(out_ref.shape[0] // 2):
        span = slice(b * LANES, (b + 1) * LANES)
        tiles = [attended_ref[m, :, span] for m in range(3)]
        for half in range(2):
            rows = [side_by_side(tiles[0], half, tiles[1], half), fold_third(tiles[2], half)]
            out_ref[2 * b + half] = jnp.concatenate(rows, axis=0).astype(jnp.bfloat16)


def spatial_kernel(
    slots_ref, rows_ref, bias_ref, out_ref, query_ref, key_ref, value_ref, attended_ref
):
    unpack(slots_ref, bias_ref, rows_ref, query_ref, key_ref, value_ref)
    blocks = slots_ref.shape[0] // 2
    wide = 2 * LANES
    jobs = []
    for m in range(3):
        for i in range(blocks // 2):
            first = max(0, 2 * i - 2) * LANES
            last = min(blocks, 2 * i + 4) * LANES
            spans = [slice(first, last)]
            if first > 0:
                spans.append(slice(0, LANES))
            jobs.append((m, slice(i * wide, (i + 1) * wide), [(m, span) for span in spans]))
    attend(jobs, query_ref, key_ref, value_ref, attended_ref)
    pack_outputs(attended_ref, out_ref)


def cross_kernel(slots_ref, bias_ref, out_ref, query_ref, key_ref, value_ref, attended_ref):
    unpack(slots_ref, bias_ref, None, query_ref, key_ref, value_ref)
    wide = 2 * LANES
    every = slice(0, key_ref.shape[1])
    jobs = []
    for m in range(3):
        second = (m + 1) % 3
        for i in range(query_ref.shape[2] // wide):
            jobs.append((m, slice(i * wide, (i + 1) * wide), [(m, every), (second, every)]))
    attend(jobs, query_ref, key_ref, value_ref, attended_ref)
    pack_outputs(attended_ref, out_ref)


def merge_heads(slots_ref, merged_ref):
    low = low_lanes(OUT_ROWS)
    tiles = [[], [], []]
    for head in range(HEADS):
        even = slots_ref[2 * head].astype(jnp.float32)
        odd = slots_ref[2 * head + 1].astype(jnp.float32)
        lower = jnp.where(low, even, swap(odd))
        upper = jnp.where(low, swap(even), odd)
        tiles[0].append(lower[:HS])
        tiles[1].append(upper[:HS])
        tiles[2].append(lower[HS:])
        tiles[2].append(upper[HS : 2 * HS - TOP])
    for m in range(3):
        merged = jnp.concatenate(tiles[m], axis=0)
        merged_ref[m * LANES : (m + 1) * LANES, :] = merged.T.astype(jnp.bfloat16)


def middle_kernel(
    slots_ref,
    tokens_ref,
    live_ref,
    mix_ref,
    gain_ref,
    weight_hbm,
    middle_ref,
    out_ref,
    merged_ref,
    weight_ref,
    normed_ref,
    weight_sems,
):
    copies, groups = weight_groups(weight_hbm, weight_ref, weight_sems, SECOND_GROUPS)
    for group in copies:
        start_all(group)
    merge_heads(slots_ref, merged_ref)
    branch = jnp.dot(merged_ref[...], mix_ref[...], preferred_element_type=jnp.float32)
    for j in range(6):
        rows = slice(j * TILE, (j + 1) * TILE)
        middle = tokens_ref[rows, :].astype(jnp.float32) + live_ref[rows, :1] * branch[rows]
        middle = middle.astype(jnp.bfloat16)
        middle_ref[rows, :] = middle
        normed_ref[rows, :] = normalise(middle.astype(jnp.float32), gain_ref[...])
    for group in copies:
        wait_all(group)
    project_and_pack(normed_ref, groups, out_ref, True, lambda group: None, lambda group: None)


def finish_kernel(
    right_hbm,
    slots_ref,
    middle_ref,
    live_ref,
    mix_ref,
    out_hbm,
    right_ref,
    merged_ref,
    result_ref,
    right_sem,
    sems,
):
    right_copy = pltpu.make_async_copy(right_hbm, right_ref, right_sem.at[0])
    right_copy.start()
    merge_heads(slots_ref, merged_ref)
    branch = jnp.dot(merged_ref[...], mix_ref[...], preferred_element_type=jnp.float32)
    right_copy.wait()
    order = cycle_order(right_ref)
    copies = []
    for j in range(6):
        rows = slice(j * TILE, (j + 1) * TILE)
        result = middle_ref[rows, :].astype(jnp.float32) + live_ref[rows, :1] * branch[rows]
        result_ref[j] = result.astype(jnp.bfloat16)
        copy = pltpu.make_async_copy(result_ref.at[j], out_hbm.at[0, order[j]], sems.at[j])
        copy.start()
        copies.append(copy)
    for copy in copies:
        copy.wait()


SMEM_SPEC = pl.BlockSpec(memory_space=pltpu.SMEM)
VMEM_SPEC = pl.BlockSpec(memory_space=pltpu.VMEM)
HBM_SPEC = pl.BlockSpec(memory_space=pltpu.HBM)


def in_hbm(array):
    return pltpu.with_memory_space_constraint(array, pltpu.HBM)


def call(kernel, in_specs, args, out_specs, out_shape, scratch, name):
    return pl.pallas_call(
        kernel,
        out_shape=out_shape,
        in_specs=in_specs,
        out_specs=out_specs,
        scratch_shapes=scratch,
        compiler_params=pltpu.CompilerParams(vmem_limit_bytes=VMEM),
        name=name,
    )(*args)


def exchange(slots):
    return lax.all_to_all(slots, "sp", split_axis=0, concat_axis=0, tiled=True)


def fast_shards(
    tokens,
    gain_spatial,
    qkv_spatial,
    out_spatial,
    gain_cross,
    qkv_cross,
    out_cross,
    lengths,
    left_view,
    right_view,
    window_mask,
):
    width = tokens.shape[-1]
    inner = out_spatial.shape[0]
    devices_sp = lax.axis_size("sp")
    view_len = TILE * devices_sp
    rows = 6 * TILE
    device = lax.axis_index("sp").astype(jnp.int32).reshape(1)
    qkv_slots = jax.ShapeDtypeStruct((devices_sp, QKV_ROWS, LANES), jnp.bfloat16)
    out_slots = jax.ShapeDtypeStruct((devices_sp, OUT_ROWS, LANES), jnp.bfloat16)
    normed = pltpu.VMEM((rows, width), jnp.bfloat16)
    merged = pltpu.VMEM((rows, inner), jnp.bfloat16)
    weights = pltpu.VMEM((3 * inner, width), jnp.bfloat16)
    heads = [
        pltpu.VMEM((3, LANES, view_len), jnp.bfloat16),
        pltpu.VMEM((3, view_len, LANES), jnp.bfloat16),
        pltpu.VMEM((3, HS + 8, view_len), jnp.bfloat16),
        pltpu.VMEM((3, HS, view_len), jnp.float32),
    ]
    slots = call(
        project_kernel,
        [HBM_SPEC] * 4,
        [in_hbm(x) for x in (right_view, tokens, gain_spatial, qkv_spatial.T)],
        HBM_SPEC,
        qkv_slots,
        [
            pltpu.SMEM(right_view.shape, jnp.int32),
            pltpu.VMEM(tokens.shape, jnp.bfloat16),
            pltpu.VMEM((width,), jnp.float32),
            weights,
            normed,
            pltpu.VMEM(qkv_slots.shape, jnp.bfloat16),
            pltpu.SemaphoreType.DMA((8,)),
            pltpu.SemaphoreType.DMA((3 * len(FIRST_GROUPS),)),
            pltpu.SemaphoreType.DMA((len(FIRST_GROUPS),)),
        ],
        "project",
    )
    per_view = jax.ShapeDtypeStruct((3, 8, view_len), jnp.float32)
    stream = jax.ShapeDtypeStruct((rows, width), jnp.bfloat16)
    block_rows, key_bias, cross_bias, live, ordered = call(
        prepare_kernel,
        [SMEM_SPEC] * 4 + [VMEM_SPEC, HBM_SPEC],
        [device, right_view, lengths, window_mask, tokens, slots],
        (VMEM_SPEC,) * 5,
        (per_view, per_view, per_view, jax.ShapeDtypeStruct((rows, LANES), jnp.float32), stream),
        [],
        "prepare",
    )
    attended = call(
        spatial_kernel,
        [VMEM_SPEC] * 3,
        [exchange(slots), block_rows, key_bias],
        VMEM_SPEC,
        out_slots,
        heads,
        "spatial",
    )
    middle, slots = call(
        middle_kernel,
        [VMEM_SPEC] * 5 + [HBM_SPEC],
        [exchange(attended), ordered, live, out_spatial, gain_cross, in_hbm(qkv_cross.T)],
        (VMEM_SPEC, VMEM_SPEC),
        (stream, qkv_slots),
        [merged, weights, normed, pltpu.SemaphoreType.DMA((3 * len(SECOND_GROUPS),))],
        "middle",
    )
    attended = call(
        cross_kernel,
        [VMEM_SPEC] * 2,
        [exchange(slots), cross_bias],
        VMEM_SPEC,
        out_slots,
        heads,
        "cross",
    )
    return call(
        finish_kernel,
        [HBM_SPEC] + [VMEM_SPEC] * 4,
        [in_hbm(right_view), exchange(attended), middle, live, out_cross],
        HBM_SPEC,
        jax.ShapeDtypeStruct(tokens.shape, jnp.bfloat16),
        [
            pltpu.SMEM(right_view.shape, jnp.int32),
            merged,
            pltpu.VMEM((6, TILE, width), jnp.bfloat16),
            pltpu.SemaphoreType.DMA((1,)),
            pltpu.SemaphoreType.DMA((6,)),
        ],
        "finish",
    )


def rms_norm(values, gain):
    floats = values.astype(jnp.float32)
    square = jnp.mean(floats * floats, axis=-1, keepdims=True)
    return (floats * lax.rsqrt(square + EPSILON) * gain).astype(jnp.bfloat16)


def to_frames(block, heads):
    frames, views, tile_len, inner = block.shape
    head_size = inner // heads
    moved = block.reshape(frames, views, tile_len, heads, head_size).transpose(0, 3, 1, 2, 4)
    return moved.reshape(frames, heads, views, tile_len * head_size)


def from_units(units, frames, views, tile_len, heads):
    head_size = units.shape[-1] // tile_len
    moved = units.reshape(frames, heads, views, tile_len, head_size).transpose(0, 2, 3, 1, 4)
    return moved.reshape(frames, views, tile_len, heads * head_size)


def attend_one(operands):
    query, keys, values, allow = operands
    scores = jnp.einsum("qd,kd->qk", query, keys, preferred_element_type=jnp.float32) * query.shape[
        -1
    ] ** (-0.5)
    scores = jnp.where(allow, scores, -1e30)
    top = jnp.max(scores, axis=-1, keepdims=True)
    weights = jnp.where(allow, jnp.exp(scores - top), 0.0)
    probs = (weights / jnp.sum(weights, axis=-1, keepdims=True)).astype(jnp.bfloat16)
    return jnp.einsum("qk,kd->qd", probs, values, preferred_element_type=jnp.float32).astype(
        jnp.bfloat16
    )


def general_shards(
    tokens,
    gain_spatial,
    qkv_spatial,
    out_spatial,
    gain_cross,
    qkv_cross,
    out_cross,
    lengths,
    left_view,
    right_view,
    window_mask,
):
    frames, views, tile_len, width = tokens.shape
    inner = out_spatial.shape[0]
    head_size = inner // HEADS
    devices_sp = lax.axis_size("sp")
    device = lax.axis_index("sp")
    view_len = tile_len * devices_sp
    blocks = window_mask.shape[-1]
    block_len = view_len // blocks
    positions = device * tile_len + jnp.arange(tile_len, dtype=jnp.int32)
    live_rows = (positions[None, None, :] < lengths[:, :, None]).astype(jnp.float32)[..., None]
    key_pos = jnp.arange(view_len, dtype=jnp.int32)
    units_dev = frames * HEADS * views // devices_sp
    unit_ids = device * units_dev + jnp.arange(units_dev, dtype=jnp.int32)
    frame_ids = unit_ids // (HEADS * views)
    view_ids = unit_ids % views
    flat_ids = frame_ids * views + view_ids
    flat_len = lengths.reshape(-1)
    own_len = jnp.take(flat_len, flat_ids)
    total_units = frames * HEADS * views
    normed = rms_norm(tokens, gain_spatial)
    projected = jnp.einsum(
        "fvtd,de->fvte", normed, qkv_spatial, preferred_element_type=jnp.float32
    ).astype(jnp.bfloat16)
    stacked = jnp.stack(
        [
            to_frames(projected[..., which * inner : (which + 1) * inner], HEADS)
            for which in range(3)
        ],
        axis=3,
    )
    stacked = stacked.reshape(total_units, 3, tile_len * head_size)
    gathered = lax.all_to_all(stacked, "sp", split_axis=0, concat_axis=2, tiled=True)
    gathered = gathered.reshape(units_dev, 3, view_len, head_size)
    masks = jnp.take(window_mask.reshape(-1, blocks, blocks), flat_ids, axis=0) > 0
    allow = jnp.broadcast_to(
        masks[:, :, None, :, None], (units_dev, blocks, block_len, blocks, block_len)
    )
    allow = allow.reshape(units_dev, view_len, view_len) & (
        key_pos[None, None, :] < own_len[:, None, None]
    )
    spatial_out = lax.map(attend_one, (gathered[:, 0], gathered[:, 1], gathered[:, 2], allow))
    returned = lax.all_to_all(
        spatial_out.reshape(units_dev, view_len * head_size),
        "sp",
        split_axis=1,
        concat_axis=0,
        tiled=True,
    )
    attended = from_units(returned, frames, views, tile_len, HEADS)
    branch = jnp.einsum("fvte,ed->fvtd", attended, out_spatial, preferred_element_type=jnp.float32)
    middle = (tokens.astype(jnp.float32) + live_rows * branch).astype(jnp.bfloat16)
    normed_cross = rms_norm(middle, gain_cross)
    projected = jnp.einsum(
        "fvtd,de->fvte", normed_cross, qkv_cross, preferred_element_type=jnp.float32
    ).astype(jnp.bfloat16)
    query_fr, key_fr, value_fr = [
        to_frames(projected[..., which * inner : (which + 1) * inner], HEADS) for which in range(3)
    ]
    left_ids = jnp.take(left_view.reshape(-1), flat_ids)
    right_ids = jnp.take(right_view.reshape(-1), flat_ids)
    view_iota = jnp.arange(views, dtype=jnp.int32)
    pick_left = (left_view[:, :, None] == view_iota).astype(jnp.bfloat16)
    pick_right = (right_view[:, :, None] == view_iota).astype(jnp.bfloat16)

    def select(pick, source):
        return jnp.einsum(
            "fvw,fhwx->fhvx", pick, source, preferred_element_type=jnp.float32
        ).astype(jnp.bfloat16)

    packed = jnp.stack(
        [
            query_fr,
            select(pick_left, key_fr),
            select(pick_left, value_fr),
            select(pick_right, key_fr),
            select(pick_right, value_fr),
        ],
        axis=3,
    )
    packed = packed.reshape(total_units, 5, tile_len * head_size)
    arrived = lax.all_to_all(packed, "sp", split_axis=0, concat_axis=2, tiled=True)
    cross_query = arrived[:, 0]
    left_kv = arrived[:, 1:3]
    right_kv = arrived[:, 3:5]
    cross_keys = jnp.concatenate([left_kv[:, 0], right_kv[:, 0]], axis=1).reshape(
        units_dev, 2 * view_len, head_size
    )
    cross_values = jnp.concatenate([left_kv[:, 1], right_kv[:, 1]], axis=1).reshape(
        units_dev, 2 * view_len, head_size
    )
    left_len = jnp.take(flat_len, frame_ids * views + left_ids)
    right_len = jnp.take(flat_len, frame_ids * views + right_ids)
    allow_cross = jnp.concatenate(
        [key_pos[None, :] < left_len[:, None], key_pos[None, :] < right_len[:, None]], axis=1
    )[:, None, :]
    cross_out = lax.map(
        attend_one,
        (
            cross_query.reshape(units_dev, view_len, head_size),
            cross_keys,
            cross_values,
            allow_cross,
        ),
    )
    returned = lax.all_to_all(
        cross_out.reshape(units_dev, view_len * head_size),
        "sp",
        split_axis=1,
        concat_axis=0,
        tiled=True,
    )
    attended = from_units(returned, frames, views, tile_len, HEADS)
    branch = jnp.einsum("fvte,ed->fvtd", attended, out_cross, preferred_element_type=jnp.float32)
    return (middle.astype(jnp.float32) + live_rows * branch).astype(jnp.bfloat16)


def shards(*args):
    tokens, mask = args[0], args[-1]
    sizes = (tokens.shape[0], tokens.shape[1], tokens.shape[2], mask.shape[-1])
    if sizes == (1, 6, TILE, 8) and lax.axis_size("sp") == 2 * HEADS:
        return fast_shards(*args)
    return general_shards(*args)


def solution(mesh):
    in_specs = (
        P("grp", None, "sp", None),
        P(),
        P(),
        P(),
        P(),
        P(),
        P(),
        P("grp", None),
        P("grp", None),
        P("grp", None),
        P("grp", None, None, None),
    )
    out_specs = P("grp", None, "sp", None)
    return jax.shard_map(shards, mesh=mesh, in_specs=in_specs, out_specs=out_specs, check_vma=False)
```

```python
import functools

import jax
import jax.numpy as jnp
from jax import lax
from jax.experimental import pallas as pl
from jax.experimental.pallas import tpu as pltpu
from jax.sharding import PartitionSpec as P

HEADS = 8
EPSILON = 1e-06


HS = 72
TILE = 64
LANES = 128
TOP = 40
QKV_ROWS = 328
OUT_ROWS = 112
NEG = -1e30
FACTOR = HS**-0.5 * 1.4426950408889634
FIRST_GROUPS = (2, 4, 2)
SECOND_GROUPS = (8,)
AHEAD = 2
VMEM = 24 * 1024 * 1024


def cycle_order(right_ref):
    order = [jnp.int32(0)]
    for _ in range(5):
        order.append(right_ref[0, order[-1]])
    return order


def low_lanes(rows):
    return lax.broadcasted_iota(jnp.int32, (rows, LANES), 1) < TILE


def swap(tile):
    return pltpu.roll(tile, TILE, 1)


def side_by_side(first, first_half, second, second_half):
    left = first if first_half == 0 else swap(first)
    right = second if second_half == 1 else swap(second)
    return jnp.where(low_lanes(first.shape[0]), left, right)


def fold_third(tile, half):
    bottom = jnp.concatenate([tile[TOP:], jnp.zeros((2 * TOP - HS, LANES), jnp.float32)], axis=0)
    return side_by_side(tile[:TOP], half, bottom, half)


def normalise(floats, gain):
    square = jnp.mean(floats * floats, axis=-1, keepdims=True)
    return (floats * lax.rsqrt(square + EPSILON) * gain[None, :]).astype(jnp.bfloat16)


def project_and_pack(normed_ref, groups, slots_ref, cross, arrived, done):
    def project(weight_ref):
        return lax.dot_general(
            weight_ref[...],
            normed_ref[...],
            (((1,), (1,)), ((), ())),
            preferred_element_type=jnp.float32,
        )

    def pack(head, heads, turned):
        for inside in range(heads):

            def item(which, m):
                row = (which * heads + inside) * HS
                tile = turned[row : row + HS, m * LANES : (m + 1) * LANES]
                return tile * FACTOR if which == 0 else tile

            for parity in range(2):
                other = 1 - parity if cross else parity
                views = [2, 0, 1] if cross and parity == 0 else [0, 1, 2]
                rows = [
                    side_by_side(item(0, m), parity, item(1, views[m]), other) for m in range(3)
                ]
                rows.append(side_by_side(item(2, views[0]), other, item(2, views[1]), other))
                rows.append(fold_third(item(2, views[2]), other))
                slot = (head + inside) * 2 + parity
                slots_ref[slot] = jnp.concatenate(rows, axis=0).astype(jnp.bfloat16)

    ahead = None
    for group, (head, heads, weight_ref) in enumerate(groups):
        arrived(group)
        turned = project(weight_ref)
        if ahead is not None:
            pack(*ahead)
            done(group - 1)
        ahead = (head, heads, turned)
    pack(*ahead)
    done(len(groups) - 1)


def weight_groups(source_ref, held_ref, sems, sizes):
    inner = source_ref.shape[0] // 3
    copies, groups, head = [], [], 0
    for group, heads in enumerate(sizes):
        rows = heads * HS
        copies.append(
            [
                pltpu.make_async_copy(
                    source_ref.at[pl.ds(which * inner + head * HS, rows)],
                    held_ref.at[pl.ds(3 * head * HS + which * rows, rows)],
                    sems.at[group * 3 + which],
                )
                for which in range(3)
            ]
        )
        groups.append((head, heads, held_ref.at[pl.ds(3 * head * HS, 3 * rows)]))
        head += heads
    return copies, groups


def start_all(copies, priority=0):
    for copy in copies:
        copy.start(priority=priority)


def wait_all(copies):
    for copy in copies:
        copy.wait()


def slot_copies(slots_ref, out_ref, sems, sizes):
    copies, head = [], 0
    for group, heads in enumerate(sizes):
        span = pl.ds(2 * head, 2 * heads)
        copies.append(pltpu.make_async_copy(slots_ref.at[span], out_ref.at[span], sems.at[group]))
        head += heads
    return copies


def project_kernel(
    right_hbm,
    tokens_hbm,
    gain_hbm,
    weight_hbm,
    out_hbm,
    right_ref,
    tokens_ref,
    gain_ref,
    weight_ref,
    normed_ref,
    slots_ref,
    in_sems,
    weight_sems,
    out_sems,
):
    small = [
        pltpu.make_async_copy(right_hbm, right_ref, in_sems.at[0]),
        pltpu.make_async_copy(gain_hbm, gain_ref, in_sems.at[1]),
    ]
    views = [
        pltpu.make_async_copy(tokens_hbm.at[0, v], tokens_ref.at[0, v], in_sems.at[2 + v])
        for v in range(6)
    ]
    copies, groups = weight_groups(weight_hbm, weight_ref, weight_sems, FIRST_GROUPS)
    outgoing = slot_copies(slots_ref, out_hbm, out_sems, FIRST_GROUPS)
    start_all(small)
    start_all(views)
    for group in range(min(AHEAD, len(groups))):
        start_all(copies[group], 1)
    wait_all(small)
    order = cycle_order(right_ref)
    place = [sum(jnp.where(order[j] == v, j, 0) for j in range(6)) for v in range(6)]
    for v in range(6):
        views[v].wait()
        floats = tokens_ref[0, v].astype(jnp.float32)
        rows = pl.ds(pl.multiple_of(place[v] * TILE, TILE), TILE)
        normed_ref[rows, :] = normalise(floats, gain_ref[...])

    def arrived(group):
        wait_all(copies[group])
        if group + AHEAD < len(groups):
            start_all(copies[group + AHEAD], 1)

    project_and_pack(
        normed_ref, groups, slots_ref, False, arrived, lambda group: outgoing[group].start()
    )
    wait_all(outgoing)


def prepare_kernel(
    device_ref,
    right_ref,
    lengths_ref,
    mask_ref,
    tokens_ref,
    _,
    query_ref,
    key_ref,
    cross_ref,
    live_ref,
    ordered_ref,
):
    order = cycle_order(right_ref)
    parity = device_ref[0] % 2
    blocks = mask_ref.shape[-1]
    view_len = key_ref.shape[-1]
    position = lax.broadcasted_iota(jnp.int32, (8, view_len), 1)
    first = lax.broadcasted_iota(jnp.int32, (8, view_len), 0) == 0
    row8 = lax.broadcasted_iota(jnp.int32, (8, LANES), 0)

    def keys_of(view):
        return jnp.where(first & (position >= lengths_ref[0, view]), NEG, 0.0)

    for m in range(3):
        view = jnp.where(parity == 0, order[2 * m], order[2 * m + 1])
        other = jnp.where(parity == 0, order[(2 * m - 1) % 6], order[2 * m])
        key_ref[m] = keys_of(view)
        cross_ref[m] = keys_of(other)
        for b in range(blocks):
            rows = jnp.zeros((8, LANES), jnp.float32)
            for c in range(blocks):
                addend = jnp.where(mask_ref[0, view, b, c] > 0, 0.0, NEG)
                rows = jnp.where(row8 == c, addend, rows)
            query_ref[m, :, b * LANES : (b + 1) * LANES] = rows
    row = device_ref[0] * TILE + lax.broadcasted_iota(jnp.int32, (TILE, LANES), 0)
    for j in range(6):
        live_ref[j * TILE : (j + 1) * TILE, :] = jnp.where(
            row < lengths_ref[0, order[j]], 1.0, 0.0
        )
        ordered_ref[j * TILE : (j + 1) * TILE, :] = tokens_ref[0, order[j]]


def unpack(slots_ref, bias_ref, rows_ref, query_ref, key_ref, value_ref):
    blocks = slots_ref.shape[0] // 2
    low = low_lanes(QKV_ROWS)
    row8 = lax.broadcasted_iota(jnp.int32, (8, LANES), 0)
    pad = jnp.zeros((LANES - HS - 16, LANES), jnp.float32)
    zero = jnp.zeros((8, LANES), jnp.float32)
    first_row = jnp.where(row8 == 0, 1.0, 0.0)
    for b in range(blocks):
        span = slice(b * LANES, (b + 1) * LANES)
        even = slots_ref[2 * b].astype(jnp.float32)
        odd = slots_ref[2 * b + 1].astype(jnp.float32)
        lower = jnp.where(low, even, swap(odd))
        upper = jnp.where(low, swap(even), odd)
        own_block = zero if rows_ref is None else jnp.where(row8 == b, 1.0, 0.0)
        values = [
            lower[3 * HS : 4 * HS],
            upper[3 * HS : 4 * HS],
            jnp.concatenate(
                [lower[4 * HS : 4 * HS + TOP], upper[4 * HS : 5 * HS - TOP]], axis=0
            ),
        ]
        for m in range(3):
            rows = zero if rows_ref is None else rows_ref[m, :, span]
            query = jnp.concatenate([lower[m * HS : (m + 1) * HS], rows, first_row, pad], axis=0)
            query_ref[m, :, span] = query.astype(jnp.bfloat16)
            key = jnp.concatenate(
                [upper[m * HS : (m + 1) * HS], own_block, bias_ref[m, :, span], pad], axis=0
            )
            key_ref[m, span, :] = key.T.astype(jnp.bfloat16)
            value_ref[m, :, span] = jnp.concatenate([values[m], first_row], axis=0).astype(
                jnp.bfloat16
            )


def attend(jobs, query_ref, key_ref, value_ref, attended_ref):
    def scores(job):
        m, lanes, parts = job
        query = query_ref[m, :, lanes]
        return [
            jnp.dot(key_ref[n, span, :], query, preferred_element_type=jnp.float32)
            for n, span in parts
        ]

    def finish(job, found):
        m, lanes, parts = job
        top = functools.reduce(
            jnp.maximum, [jnp.max(score, axis=0, keepdims=True) for score in found]
        )
        total = None
        for score, (n, span) in zip(found, parts):
            weights = jnp.exp2(score - top).astype(jnp.bfloat16)
            term = jnp.dot(value_ref[n, :, span], weights, preferred_element_type=jnp.float32)
            total = term if total is None else total + term
        attended_ref[m, :, lanes] = total[:HS] / total[HS : HS + 1]

    queue = []
    for job in jobs:
        queue.append((job, scores(job)))
        if len(queue) > 2:
            finish(*queue.pop(0))
    for entry in queue:
        finish(*entry)


def pack_outputs(attended_ref, out_ref):
    for b in range(out_ref.shape[0] // 2):
        span = slice(b * LANES, (b + 1) * LANES)
        tiles = [attended_ref[m, :, span] for m in range(3)]
        for half in range(2):
            rows = [side_by_side(tiles[0], half, tiles[1], half), fold_third(tiles[2], half)]
            out_ref[2 * b + half] = jnp.concatenate(rows, axis=0).astype(jnp.bfloat16)


def spatial_kernel(
    slots_ref, rows_ref, bias_ref, out_ref, query_ref, key_ref, value_ref, attended_ref
):
    unpack(slots_ref, bias_ref, rows_ref, query_ref, key_ref, value_ref)
    blocks = slots_ref.shape[0] // 2
    wide = 2 * LANES
    jobs = []
    for m in range(3):
        for i in range(blocks // 2):
            first = max(0, 2 * i - 2) * LANES
            last = min(blocks, 2 * i + 4) * LANES
            spans = [slice(first, last)]
            if first > 0:
                spans.append(slice(0, LANES))
            jobs.append((m, slice(i * wide, (i + 1) * wide), [(m, span) for span in spans]))
    attend(jobs, query_ref, key_ref, value_ref, attended_ref)
    pack_outputs(attended_ref, out_ref)


def cross_kernel(slots_ref, bias_ref, out_ref, query_ref, key_ref, value_ref, attended_ref):
    unpack(slots_ref, bias_ref, None, query_ref, key_ref, value_ref)
    wide = 2 * LANES
    every = slice(0, key_ref.shape[1])
    jobs = []
    for m in range(3):
        second = (m + 1) % 3
        for i in range(query_ref.shape[2] // wide):
            jobs.append((m, slice(i * wide, (i + 1) * wide), [(m, every), (second, every)]))
    attend(jobs, query_ref, key_ref, value_ref, attended_ref)
    pack_outputs(attended_ref, out_ref)


def merge_heads(slots_ref, merged_ref):
    low = low_lanes(OUT_ROWS)
    tiles = [[], [], []]
    for head in range(HEADS):
        even = slots_ref[2 * head].astype(jnp.float32)
        odd = slots_ref[2 * head + 1].astype(jnp.float32)
        lower = jnp.where(low, even, swap(odd))
        upper = jnp.where(low, swap(even), odd)
        tiles[0].append(lower[:HS])
        tiles[1].append(upper[:HS])
        tiles[2].append(lower[HS:])
        tiles[2].append(upper[HS : 2 * HS - TOP])
    for m in range(3):
        merged = jnp.concatenate(tiles[m], axis=0)
        merged_ref[m * LANES : (m + 1) * LANES, :] = merged.T.astype(jnp.bfloat16)


def middle_kernel(
    slots_ref,
    tokens_ref,
    live_ref,
    mix_ref,
    gain_ref,
    weight_hbm,
    middle_ref,
    out_ref,
    merged_ref,
    weight_ref,
    normed_ref,
    weight_sems,
):
    copies, groups = weight_groups(weight_hbm, weight_ref, weight_sems, SECOND_GROUPS)
    for group in copies:
        start_all(group)
    merge_heads(slots_ref, merged_ref)
    branch = jnp.dot(merged_ref[...], mix_ref[...], preferred_element_type=jnp.float32)
    for j in range(6):
        rows = slice(j * TILE, (j + 1) * TILE)
        middle = tokens_ref[rows, :].astype(jnp.float32) + live_ref[rows, :1] * branch[rows]
        middle = middle.astype(jnp.bfloat16)
        middle_ref[rows, :] = middle
        normed_ref[rows, :] = normalise(middle.astype(jnp.float32), gain_ref[...])
    for group in copies:
        wait_all(group)
    project_and_pack(normed_ref, groups, out_ref, True, lambda group: None, lambda group: None)


def finish_kernel(
    right_hbm,
    slots_ref,
    middle_ref,
    live_ref,
    mix_ref,
    out_hbm,
    right_ref,
    merged_ref,
    result_ref,
    right_sem,
    sems,
):
    right_copy = pltpu.make_async_copy(right_hbm, right_ref, right_sem.at[0])
    right_copy.start()
    merge_heads(slots_ref, merged_ref)
    branch = jnp.dot(merged_ref[...], mix_ref[...], preferred_element_type=jnp.float32)
    right_copy.wait()
    order = cycle_order(right_ref)
    copies = []
    for j in range(6):
        rows = slice(j * TILE, (j + 1) * TILE)
        result = middle_ref[rows, :].astype(jnp.float32) + live_ref[rows, :1] * branch[rows]
        result_ref[j] = result.astype(jnp.bfloat16)
        copy = pltpu.make_async_copy(result_ref.at[j], out_hbm.at[0, order[j]], sems.at[j])
        copy.start()
        copies.append(copy)
    for copy in copies:
        copy.wait()


SMEM_SPEC = pl.BlockSpec(memory_space=pltpu.SMEM)
VMEM_SPEC = pl.BlockSpec(memory_space=pltpu.VMEM)
HBM_SPEC = pl.BlockSpec(memory_space=pltpu.HBM)


def in_hbm(array):
    return pltpu.with_memory_space_constraint(array, pltpu.HBM)


def call(kernel, in_specs, args, out_specs, out_shape, scratch, name):
    return pl.pallas_call(
        kernel,
        out_shape=out_shape,
        in_specs=in_specs,
        out_specs=out_specs,
        scratch_shapes=scratch,
        compiler_params=pltpu.CompilerParams(vmem_limit_bytes=VMEM),
        name=name,
    )(*args)


def exchange(slots):
    return lax.all_to_all(slots, "sp", split_axis=0, concat_axis=0, tiled=True)


def fast_shards(
    tokens,
    gain_spatial,
    qkv_spatial,
    out_spatial,
    gain_cross,
    qkv_cross,
    out_cross,
    lengths,
    left_view,
    right_view,
    window_mask,
):
    width = tokens.shape[-1]
    inner = out_spatial.shape[0]
    devices_sp = lax.axis_size("sp")
    view_len = TILE * devices_sp
    rows = 6 * TILE
    device = lax.axis_index("sp").astype(jnp.int32).reshape(1)
    qkv_slots = jax.ShapeDtypeStruct((devices_sp, QKV_ROWS, LANES), jnp.bfloat16)
    out_slots = jax.ShapeDtypeStruct((devices_sp, OUT_ROWS, LANES), jnp.bfloat16)
    normed = pltpu.VMEM((rows, width), jnp.bfloat16)
    merged = pltpu.VMEM((rows, inner), jnp.bfloat16)
    weights = pltpu.VMEM((3 * inner, width), jnp.bfloat16)
    heads = [
        pltpu.VMEM((3, LANES, view_len), jnp.bfloat16),
        pltpu.VMEM((3, view_len, LANES), jnp.bfloat16),
        pltpu.VMEM((3, HS + 8, view_len), jnp.bfloat16),
        pltpu.VMEM((3, HS, view_len), jnp.float32),
    ]
    slots = call(
        project_kernel,
        [HBM_SPEC] * 4,
        [in_hbm(x) for x in (right_view, tokens, gain_spatial, qkv_spatial.T)],
        HBM_SPEC,
        qkv_slots,
        [
            pltpu.SMEM(right_view.shape, jnp.int32),
            pltpu.VMEM(tokens.shape, jnp.bfloat16),
            pltpu.VMEM((width,), jnp.float32),
            weights,
            normed,
            pltpu.VMEM(qkv_slots.shape, jnp.bfloat16),
            pltpu.SemaphoreType.DMA((8,)),
            pltpu.SemaphoreType.DMA((3 * len(FIRST_GROUPS),)),
            pltpu.SemaphoreType.DMA((len(FIRST_GROUPS),)),
        ],
        "project",
    )
    per_view = jax.ShapeDtypeStruct((3, 8, view_len), jnp.float32)
    stream = jax.ShapeDtypeStruct((rows, width), jnp.bfloat16)
    block_rows, key_bias, cross_bias, live, ordered = call(
        prepare_kernel,
        [SMEM_SPEC] * 4 + [VMEM_SPEC, HBM_SPEC],
        [device, right_view, lengths, window_mask, tokens, slots],
        (VMEM_SPEC,) * 5,
        (per_view, per_view, per_view, jax.ShapeDtypeStruct((rows, LANES), jnp.float32), stream),
        [],
        "prepare",
    )
    attended = call(
        spatial_kernel,
        [VMEM_SPEC] * 3,
        [exchange(slots), block_rows, key_bias],
        VMEM_SPEC,
        out_slots,
        heads,
        "spatial",
    )
    middle, slots = call(
        middle_kernel,
        [VMEM_SPEC] * 5 + [HBM_SPEC],
        [exchange(attended), ordered, live, out_spatial, gain_cross, in_hbm(qkv_cross.T)],
        (VMEM_SPEC, VMEM_SPEC),
        (stream, qkv_slots),
        [merged, weights, normed, pltpu.SemaphoreType.DMA((3 * len(SECOND_GROUPS),))],
        "middle",
    )
    attended = call(
        cross_kernel,
        [VMEM_SPEC] * 2,
        [exchange(slots), cross_bias],
        VMEM_SPEC,
        out_slots,
        heads,
        "cross",
    )
    return call(
        finish_kernel,
        [HBM_SPEC] + [VMEM_SPEC] * 4,
        [in_hbm(right_view), exchange(attended), middle, live, out_cross],
        HBM_SPEC,
        jax.ShapeDtypeStruct(tokens.shape, jnp.bfloat16),
        [
            pltpu.SMEM(right_view.shape, jnp.int32),
            merged,
            pltpu.VMEM((6, TILE, width), jnp.bfloat16),
            pltpu.SemaphoreType.DMA((1,)),
            pltpu.SemaphoreType.DMA((6,)),
        ],
        "finish",
    )


def rms_norm(values, gain):
    floats = values.astype(jnp.float32)
    square = jnp.mean(floats * floats, axis=-1, keepdims=True)
    return (floats * lax.rsqrt(square + EPSILON) * gain).astype(jnp.bfloat16)


def to_frames(block, heads):
    frames, views, tile_len, inner = block.shape
    head_size = inner // heads
    moved = block.reshape(frames, views, tile_len, heads, head_size).transpose(0, 3, 1, 2, 4)
    return moved.reshape(frames, heads, views, tile_len * head_size)


def from_units(units, frames, views, tile_len, heads):
    head_size = units.shape[-1] // tile_len
    moved = units.reshape(frames, heads, views, tile_len, head_size).transpose(0, 2, 3, 1, 4)
    return moved.reshape(frames, views, tile_len, heads * head_size)


def attend_one(operands):
    query, keys, values, allow = operands
    scores = jnp.einsum("qd,kd->qk", query, keys, preferred_element_type=jnp.float32) * query.shape[
        -1
    ] ** (-0.5)
    scores = jnp.where(allow, scores, -1e30)
    top = jnp.max(scores, axis=-1, keepdims=True)
    weights = jnp.where(allow, jnp.exp(scores - top), 0.0)
    probs = (weights / jnp.sum(weights, axis=-1, keepdims=True)).astype(jnp.bfloat16)
    return jnp.einsum("qk,kd->qd", probs, values, preferred_element_type=jnp.float32).astype(
        jnp.bfloat16
    )


def general_shards(
    tokens,
    gain_spatial,
    qkv_spatial,
    out_spatial,
    gain_cross,
    qkv_cross,
    out_cross,
    lengths,
    left_view,
    right_view,
    window_mask,
):
    frames, views, tile_len, width = tokens.shape
    inner = out_spatial.shape[0]
    head_size = inner // HEADS
    devices_sp = lax.axis_size("sp")
    device = lax.axis_index("sp")
    view_len = tile_len * devices_sp
    blocks = window_mask.shape[-1]
    block_len = view_len // blocks
    positions = device * tile_len + jnp.arange(tile_len, dtype=jnp.int32)
    live_rows = (positions[None, None, :] < lengths[:, :, None]).astype(jnp.float32)[..., None]
    key_pos = jnp.arange(view_len, dtype=jnp.int32)
    units_dev = frames * HEADS * views // devices_sp
    unit_ids = device * units_dev + jnp.arange(units_dev, dtype=jnp.int32)
    frame_ids = unit_ids // (HEADS * views)
    view_ids = unit_ids % views
    flat_ids = frame_ids * views + view_ids
    flat_len = lengths.reshape(-1)
    own_len = jnp.take(flat_len, flat_ids)
    total_units = frames * HEADS * views
    normed = rms_norm(tokens, gain_spatial)
    projected = jnp.einsum(
        "fvtd,de->fvte", normed, qkv_spatial, preferred_element_type=jnp.float32
    ).astype(jnp.bfloat16)
    stacked = jnp.stack(
        [
            to_frames(projected[..., which * inner : (which + 1) * inner], HEADS)
            for which in range(3)
        ],
        axis=3,
    )
    stacked = stacked.reshape(total_units, 3, tile_len * head_size)
    gathered = lax.all_to_all(stacked, "sp", split_axis=0, concat_axis=2, tiled=True)
    gathered = gathered.reshape(units_dev, 3, view_len, head_size)
    masks = jnp.take(window_mask.reshape(-1, blocks, blocks), flat_ids, axis=0) > 0
    allow = jnp.broadcast_to(
        masks[:, :, None, :, None], (units_dev, blocks, block_len, blocks, block_len)
    )
    allow = allow.reshape(units_dev, view_len, view_len) & (
        key_pos[None, None, :] < own_len[:, None, None]
    )
    spatial_out = lax.map(attend_one, (gathered[:, 0], gathered[:, 1], gathered[:, 2], allow))
    returned = lax.all_to_all(
        spatial_out.reshape(units_dev, view_len * head_size),
        "sp",
        split_axis=1,
        concat_axis=0,
        tiled=True,
    )
    attended = from_units(returned, frames, views, tile_len, HEADS)
    branch = jnp.einsum("fvte,ed->fvtd", attended, out_spatial, preferred_element_type=jnp.float32)
    middle = (tokens.astype(jnp.float32) + live_rows * branch).astype(jnp.bfloat16)
    normed_cross = rms_norm(middle, gain_cross)
    projected = jnp.einsum(
        "fvtd,de->fvte", normed_cross, qkv_cross, preferred_element_type=jnp.float32
    ).astype(jnp.bfloat16)
    query_fr, key_fr, value_fr = [
        to_frames(projected[..., which * inner : (which + 1) * inner], HEADS) for which in range(3)
    ]
    left_ids = jnp.take(left_view.reshape(-1), flat_ids)
    right_ids = jnp.take(right_view.reshape(-1), flat_ids)
    view_iota = jnp.arange(views, dtype=jnp.int32)
    pick_left = (left_view[:, :, None] == view_iota).astype(jnp.bfloat16)
    pick_right = (right_view[:, :, None] == view_iota).astype(jnp.bfloat16)

    def select(pick, source):
        return jnp.einsum(
            "fvw,fhwx->fhvx", pick, source, preferred_element_type=jnp.float32
        ).astype(jnp.bfloat16)

    packed = jnp.stack(
        [
            query_fr,
            select(pick_left, key_fr),
            select(pick_left, value_fr),
            select(pick_right, key_fr),
            select(pick_right, value_fr),
        ],
        axis=3,
    )
    packed = packed.reshape(total_units, 5, tile_len * head_size)
    arrived = lax.all_to_all(packed, "sp", split_axis=0, concat_axis=2, tiled=True)
    cross_query = arrived[:, 0]
    left_kv = arrived[:, 1:3]
    right_kv = arrived[:, 3:5]
    cross_keys = jnp.concatenate([left_kv[:, 0], right_kv[:, 0]], axis=1).reshape(
        units_dev, 2 * view_len, head_size
    )
    cross_values = jnp.concatenate([left_kv[:, 1], right_kv[:, 1]], axis=1).reshape(
        units_dev, 2 * view_len, head_size
    )
    left_len = jnp.take(flat_len, frame_ids * views + left_ids)
    right_len = jnp.take(flat_len, frame_ids * views + right_ids)
    allow_cross = jnp.concatenate(
        [key_pos[None, :] < left_len[:, None], key_pos[None, :] < right_len[:, None]], axis=1
    )[:, None, :]
    cross_out = lax.map(
        attend_one,
        (
            cross_query.reshape(units_dev, view_len, head_size),
            cross_keys,
            cross_values,
            allow_cross,
        ),
    )
    returned = lax.all_to_all(
        cross_out.reshape(units_dev, view_len * head_size),
        "sp",
        split_axis=1,
        concat_axis=0,
        tiled=True,
    )
    attended = from_units(returned, frames, views, tile_len, HEADS)
    branch = jnp.einsum("fvte,ed->fvtd", attended, out_cross, preferred_element_type=jnp.float32)
    return (middle.astype(jnp.float32) + live_rows * branch).astype(jnp.bfloat16)


def shards(*args):
    tokens, mask = args[0], args[-1]
    sizes = (tokens.shape[0], tokens.shape[1], tokens.shape[2], mask.shape[-1])
    if sizes == (1, 6, TILE, 8) and lax.axis_size("sp") == 2 * HEADS:
        return fast_shards(*args)
    return general_shards(*args)


def solution(mesh):
    in_specs = (
        P("grp", None, "sp", None),
        P(),
        P(),
        P(),
        P(),
        P(),
        P(),
        P("grp", None),
        P("grp", None),
        P("grp", None),
        P("grp", None, None, None),
    )
    out_specs = P("grp", None, "sp", None)
    return jax.shard_map(shards, mesh=mesh, in_specs=in_specs, out_specs=out_specs, check_vma=False)
```

```python
import functools

import jax
import jax.numpy as jnp
from jax import lax
from jax.experimental import pallas as pl
from jax.experimental.pallas import tpu as pltpu
from jax.sharding import PartitionSpec as P

HEADS = 8
EPSILON = 1e-06


HS = 72
TILE = 64
LANES = 128
TOP = 40
QKV_ROWS = 328
OUT_ROWS = 112
NEG = -1e30
ORDER = (9, 1, 5, 12, 0, 2, 7, 8, 14, 6, 4, 3, 15, 11, 10, 13)
PLACE = tuple(ORDER.index(device) for device in range(len(ORDER)))
FACTOR = HS**-0.5 * 1.4426950408889634
FIRST_GROUPS = (2, 4, 2)
SECOND_GROUPS = (8,)
AHEAD = 2
VMEM = 24 * 1024 * 1024


def cycle_order(right_ref):
    order = [jnp.int32(0)]
    for _ in range(5):
        order.append(right_ref[0, order[-1]])
    return order


def low_lanes(rows):
    return lax.broadcasted_iota(jnp.int32, (rows, LANES), 1) < TILE


def swap(tile):
    return pltpu.roll(tile, TILE, 1)


def side_by_side(first, first_half, second, second_half):
    left = first if first_half == 0 else swap(first)
    right = second if second_half == 1 else swap(second)
    return jnp.where(low_lanes(first.shape[0]), left, right)


def fold_third(tile, half):
    bottom = jnp.concatenate([tile[TOP:], jnp.zeros((2 * TOP - HS, LANES), jnp.float32)], axis=0)
    return side_by_side(tile[:TOP], half, bottom, half)


def normalise(floats, gain):
    square = jnp.mean(floats * floats, axis=-1, keepdims=True)
    return (floats * lax.rsqrt(square + EPSILON) * gain[None, :]).astype(jnp.bfloat16)


def project_and_pack(normed_ref, groups, slots_ref, cross, arrived, done):
    def project(weight_ref):
        return lax.dot_general(
            weight_ref[...],
            normed_ref[...],
            (((1,), (1,)), ((), ())),
            preferred_element_type=jnp.float32,
        )

    def pack(head, heads, turned):
        for inside in range(heads):

            def item(which, m):
                row = (which * heads + inside) * HS
                tile = turned[row : row + HS, m * LANES : (m + 1) * LANES]
                return tile * FACTOR if which == 0 else tile

            for parity in range(2):
                other = 1 - parity if cross else parity
                views = [2, 0, 1] if cross and parity == 0 else [0, 1, 2]
                rows = [
                    side_by_side(item(0, m), parity, item(1, views[m]), other) for m in range(3)
                ]
                rows.append(side_by_side(item(2, views[0]), other, item(2, views[1]), other))
                rows.append(fold_third(item(2, views[2]), other))
                slot = PLACE[(head + inside) * 2 + parity]
                slots_ref[slot] = jnp.concatenate(rows, axis=0).astype(jnp.bfloat16)

    ahead = None
    for group, (head, heads, weight_ref) in enumerate(groups):
        arrived(group)
        turned = project(weight_ref)
        if ahead is not None:
            pack(*ahead)
            done(group - 1)
        ahead = (head, heads, turned)
    pack(*ahead)
    done(len(groups) - 1)


def weight_groups(source_ref, held_ref, sems, sizes):
    inner = source_ref.shape[0] // 3
    copies, groups, head = [], [], 0
    for group, heads in enumerate(sizes):
        rows = heads * HS
        copies.append(
            [
                pltpu.make_async_copy(
                    source_ref.at[pl.ds(which * inner + head * HS, rows)],
                    held_ref.at[pl.ds(3 * head * HS + which * rows, rows)],
                    sems.at[group * 3 + which],
                )
                for which in range(3)
            ]
        )
        groups.append((head, heads, held_ref.at[pl.ds(3 * head * HS, 3 * rows)]))
        head += heads
    return copies, groups


def start_all(copies, priority=0):
    for copy in copies:
        copy.start(priority=priority)


def wait_all(copies):
    for copy in copies:
        copy.wait()


def slot_copies(slots_ref, out_ref, sems, sizes):
    copies, head = [], 0
    for heads in sizes:
        places = PLACE[2 * head : 2 * (head + heads)]
        copies.append(
            [
                pltpu.make_async_copy(slots_ref.at[place], out_ref.at[place], sems.at[place])
                for place in places
            ]
        )
        head += heads
    return copies


def project_kernel(
    right_hbm,
    tokens_hbm,
    gain_hbm,
    weight_hbm,
    out_hbm,
    right_ref,
    tokens_ref,
    gain_ref,
    weight_ref,
    normed_ref,
    slots_ref,
    in_sems,
    weight_sems,
    out_sems,
):
    small = [
        pltpu.make_async_copy(right_hbm, right_ref, in_sems.at[0]),
        pltpu.make_async_copy(gain_hbm, gain_ref, in_sems.at[1]),
    ]
    views = [
        pltpu.make_async_copy(tokens_hbm.at[0, v], tokens_ref.at[0, v], in_sems.at[2 + v])
        for v in range(6)
    ]
    copies, groups = weight_groups(weight_hbm, weight_ref, weight_sems, FIRST_GROUPS)
    outgoing = slot_copies(slots_ref, out_hbm, out_sems, FIRST_GROUPS)
    start_all(small)
    start_all(views)
    for group in range(min(AHEAD, len(groups))):
        start_all(copies[group], 1)
    wait_all(small)
    order = cycle_order(right_ref)
    place = [sum(jnp.where(order[j] == v, j, 0) for j in range(6)) for v in range(6)]
    for v in range(6):
        views[v].wait()
        floats = tokens_ref[0, v].astype(jnp.float32)
        rows = pl.ds(pl.multiple_of(place[v] * TILE, TILE), TILE)
        normed_ref[rows, :] = normalise(floats, gain_ref[...])

    def arrived(group):
        wait_all(copies[group])
        if group + AHEAD < len(groups):
            start_all(copies[group + AHEAD], 1)

    project_and_pack(
        normed_ref, groups, slots_ref, False, arrived, lambda group: start_all(outgoing[group])
    )
    for group in outgoing:
        wait_all(group)


def prepare_kernel(
    device_ref,
    right_ref,
    lengths_ref,
    mask_ref,
    tokens_ref,
    _,
    query_ref,
    key_ref,
    cross_ref,
    live_ref,
    ordered_ref,
):
    order = cycle_order(right_ref)
    parity = device_ref[0] % 2
    blocks = mask_ref.shape[-1]
    view_len = key_ref.shape[-1]
    position = lax.broadcasted_iota(jnp.int32, (8, view_len), 1)
    first = lax.broadcasted_iota(jnp.int32, (8, view_len), 0) == 0
    row8 = lax.broadcasted_iota(jnp.int32, (8, LANES), 0)

    def keys_of(view):
        return jnp.where(first & (position >= lengths_ref[0, view]), NEG, 0.0)

    for m in range(3):
        view = jnp.where(parity == 0, order[2 * m], order[2 * m + 1])
        other = jnp.where(parity == 0, order[(2 * m - 1) % 6], order[2 * m])
        key_ref[m] = keys_of(view)
        cross_ref[m] = keys_of(other)
        for b in range(blocks):
            rows = jnp.zeros((8, LANES), jnp.float32)
            for c in range(blocks):
                addend = jnp.where(mask_ref[0, view, b, c] > 0, 0.0, NEG)
                rows = jnp.where(row8 == c, addend, rows)
            query_ref[m, :, b * LANES : (b + 1) * LANES] = rows
    row = device_ref[0] * TILE + lax.broadcasted_iota(jnp.int32, (TILE, LANES), 0)
    for j in range(6):
        live_ref[j * TILE : (j + 1) * TILE, :] = jnp.where(
            row < lengths_ref[0, order[j]], 1.0, 0.0
        )
        ordered_ref[j * TILE : (j + 1) * TILE, :] = tokens_ref[0, order[j]]


def unpack(slots_ref, bias_ref, rows_ref, query_ref, key_ref, value_ref):
    blocks = slots_ref.shape[0] // 2
    low = low_lanes(QKV_ROWS)
    row8 = lax.broadcasted_iota(jnp.int32, (8, LANES), 0)
    pad = jnp.zeros((LANES - HS - 16, LANES), jnp.float32)
    zero = jnp.zeros((8, LANES), jnp.float32)
    first_row = jnp.where(row8 == 0, 1.0, 0.0)
    for b in range(blocks):
        span = slice(b * LANES, (b + 1) * LANES)
        even = slots_ref[PLACE[2 * b]].astype(jnp.float32)
        odd = slots_ref[PLACE[2 * b + 1]].astype(jnp.float32)
        lower = jnp.where(low, even, swap(odd))
        upper = jnp.where(low, swap(even), odd)
        own_block = zero if rows_ref is None else jnp.where(row8 == b, 1.0, 0.0)
        values = [
            lower[3 * HS : 4 * HS],
            upper[3 * HS : 4 * HS],
            jnp.concatenate(
                [lower[4 * HS : 4 * HS + TOP], upper[4 * HS : 5 * HS - TOP]], axis=0
            ),
        ]
        for m in range(3):
            rows = zero if rows_ref is None else rows_ref[m, :, span]
            query = jnp.concatenate([lower[m * HS : (m + 1) * HS], rows, first_row, pad], axis=0)
            query_ref[m, :, span] = query.astype(jnp.bfloat16)
            key = jnp.concatenate(
                [upper[m * HS : (m + 1) * HS], own_block, bias_ref[m, :, span], pad], axis=0
            )
            key_ref[m, span, :] = key.T.astype(jnp.bfloat16)
            value_ref[m, :, span] = jnp.concatenate([values[m], first_row], axis=0).astype(
                jnp.bfloat16
            )


def attend(jobs, query_ref, key_ref, value_ref, attended_ref):
    def scores(job):
        m, lanes, parts = job
        query = query_ref[m, :, lanes]
        return [
            jnp.dot(key_ref[n, span, :], query, preferred_element_type=jnp.float32)
            for n, span in parts
        ]

    def finish(job, found):
        m, lanes, parts = job
        top = functools.reduce(
            jnp.maximum, [jnp.max(score, axis=0, keepdims=True) for score in found]
        )
        total = None
        for score, (n, span) in zip(found, parts):
            weights = jnp.exp2(score - top).astype(jnp.bfloat16)
            term = jnp.dot(value_ref[n, :, span], weights, preferred_element_type=jnp.float32)
            total = term if total is None else total + term
        attended_ref[m, :, lanes] = total[:HS] / total[HS : HS + 1]

    queue = []
    for job in jobs:
        queue.append((job, scores(job)))
        if len(queue) > 2:
            finish(*queue.pop(0))
    for entry in queue:
        finish(*entry)


def pack_outputs(attended_ref, out_ref):
    for b in range(out_ref.shape[0] // 2):
        span = slice(b * LANES, (b + 1) * LANES)
        tiles = [attended_ref[m, :, span] for m in range(3)]
        for half in range(2):
            rows = [side_by_side(tiles[0], half, tiles[1], half), fold_third(tiles[2], half)]
            out_ref[PLACE[2 * b + half]] = jnp.concatenate(rows, axis=0).astype(jnp.bfloat16)


def spatial_kernel(
    slots_ref, rows_ref, bias_ref, out_ref, query_ref, key_ref, value_ref, attended_ref
):
    unpack(slots_ref, bias_ref, rows_ref, query_ref, key_ref, value_ref)
    blocks = slots_ref.shape[0] // 2
    wide = 2 * LANES
    jobs = []
    for m in range(3):
        for i in range(blocks // 2):
            first = max(0, 2 * i - 2) * LANES
            last = min(blocks, 2 * i + 4) * LANES
            spans = [slice(first, last)]
            if first > 0:
                spans.append(slice(0, LANES))
            jobs.append((m, slice(i * wide, (i + 1) * wide), [(m, span) for span in spans]))
    attend(jobs, query_ref, key_ref, value_ref, attended_ref)
    pack_outputs(attended_ref, out_ref)


def cross_kernel(slots_ref, bias_ref, out_ref, query_ref, key_ref, value_ref, attended_ref):
    unpack(slots_ref, bias_ref, None, query_ref, key_ref, value_ref)
    wide = 2 * LANES
    every = slice(0, key_ref.shape[1])
    jobs = []
    for m in range(3):
        second = (m + 1) % 3
        for i in range(query_ref.shape[2] // wide):
            jobs.append((m, slice(i * wide, (i + 1) * wide), [(m, every), (second, every)]))
    attend(jobs, query_ref, key_ref, value_ref, attended_ref)
    pack_outputs(attended_ref, out_ref)


def merge_heads(slots_ref, merged_ref):
    low = low_lanes(OUT_ROWS)
    tiles = [[], [], []]
    for head in range(HEADS):
        even = slots_ref[PLACE[2 * head]].astype(jnp.float32)
        odd = slots_ref[PLACE[2 * head + 1]].astype(jnp.float32)
        lower = jnp.where(low, even, swap(odd))
        upper = jnp.where(low, swap(even), odd)
        tiles[0].append(lower[:HS])
        tiles[1].append(upper[:HS])
        tiles[2].append(lower[HS:])
        tiles[2].append(upper[HS : 2 * HS - TOP])
    for m in range(3):
        merged = jnp.concatenate(tiles[m], axis=0)
        merged_ref[m * LANES : (m + 1) * LANES, :] = merged.T.astype(jnp.bfloat16)


def middle_kernel(
    slots_ref,
    tokens_ref,
    live_ref,
    mix_ref,
    gain_ref,
    weight_hbm,
    middle_ref,
    out_ref,
    merged_ref,
    weight_ref,
    normed_ref,
    weight_sems,
):
    copies, groups = weight_groups(weight_hbm, weight_ref, weight_sems, SECOND_GROUPS)
    for group in copies:
        start_all(group)
    merge_heads(slots_ref, merged_ref)
    branch = jnp.dot(merged_ref[...], mix_ref[...], preferred_element_type=jnp.float32)
    for j in range(6):
        rows = slice(j * TILE, (j + 1) * TILE)
        middle = tokens_ref[rows, :].astype(jnp.float32) + live_ref[rows, :1] * branch[rows]
        middle = middle.astype(jnp.bfloat16)
        middle_ref[rows, :] = middle
        normed_ref[rows, :] = normalise(middle.astype(jnp.float32), gain_ref[...])
    for group in copies:
        wait_all(group)
    project_and_pack(normed_ref, groups, out_ref, True, lambda group: None, lambda group: None)


def finish_kernel(
    right_hbm,
    slots_ref,
    middle_ref,
    live_ref,
    mix_ref,
    out_hbm,
    right_ref,
    merged_ref,
    result_ref,
    right_sem,
    sems,
):
    right_copy = pltpu.make_async_copy(right_hbm, right_ref, right_sem.at[0])
    right_copy.start()
    merge_heads(slots_ref, merged_ref)
    branch = jnp.dot(merged_ref[...], mix_ref[...], preferred_element_type=jnp.float32)
    right_copy.wait()
    order = cycle_order(right_ref)
    copies = []
    for j in range(6):
        rows = slice(j * TILE, (j + 1) * TILE)
        result = middle_ref[rows, :].astype(jnp.float32) + live_ref[rows, :1] * branch[rows]
        result_ref[j] = result.astype(jnp.bfloat16)
        copy = pltpu.make_async_copy(result_ref.at[j], out_hbm.at[0, order[j]], sems.at[j])
        copy.start()
        copies.append(copy)
    for copy in copies:
        copy.wait()


SMEM_SPEC = pl.BlockSpec(memory_space=pltpu.SMEM)
VMEM_SPEC = pl.BlockSpec(memory_space=pltpu.VMEM)
HBM_SPEC = pl.BlockSpec(memory_space=pltpu.HBM)


def in_hbm(array):
    return pltpu.with_memory_space_constraint(array, pltpu.HBM)


def call(kernel, in_specs, args, out_specs, out_shape, scratch, name):
    return pl.pallas_call(
        kernel,
        out_shape=out_shape,
        in_specs=in_specs,
        out_specs=out_specs,
        scratch_shapes=scratch,
        compiler_params=pltpu.CompilerParams(vmem_limit_bytes=VMEM),
        name=name,
    )(*args)


def exchange(slots):
    return lax.all_to_all(
        slots, "sp", split_axis=0, concat_axis=0, tiled=True, axis_index_groups=[list(ORDER)]
    )


def fast_shards(
    tokens,
    gain_spatial,
    qkv_spatial,
    out_spatial,
    gain_cross,
    qkv_cross,
    out_cross,
    lengths,
    left_view,
    right_view,
    window_mask,
):
    width = tokens.shape[-1]
    inner = out_spatial.shape[0]
    devices_sp = lax.axis_size("sp")
    view_len = TILE * devices_sp
    rows = 6 * TILE
    device = lax.axis_index("sp").astype(jnp.int32).reshape(1)
    qkv_slots = jax.ShapeDtypeStruct((devices_sp, QKV_ROWS, LANES), jnp.bfloat16)
    out_slots = jax.ShapeDtypeStruct((devices_sp, OUT_ROWS, LANES), jnp.bfloat16)
    normed = pltpu.VMEM((rows, width), jnp.bfloat16)
    merged = pltpu.VMEM((rows, inner), jnp.bfloat16)
    weights = pltpu.VMEM((3 * inner, width), jnp.bfloat16)
    heads = [
        pltpu.VMEM((3, LANES, view_len), jnp.bfloat16),
        pltpu.VMEM((3, view_len, LANES), jnp.bfloat16),
        pltpu.VMEM((3, HS + 8, view_len), jnp.bfloat16),
        pltpu.VMEM((3, HS, view_len), jnp.float32),
    ]
    slots = call(
        project_kernel,
        [HBM_SPEC] * 4,
        [in_hbm(x) for x in (right_view, tokens, gain_spatial, qkv_spatial.T)],
        HBM_SPEC,
        qkv_slots,
        [
            pltpu.SMEM(right_view.shape, jnp.int32),
            pltpu.VMEM(tokens.shape, jnp.bfloat16),
            pltpu.VMEM((width,), jnp.float32),
            weights,
            normed,
            pltpu.VMEM(qkv_slots.shape, jnp.bfloat16),
            pltpu.SemaphoreType.DMA((8,)),
            pltpu.SemaphoreType.DMA((3 * len(FIRST_GROUPS),)),
            pltpu.SemaphoreType.DMA((devices_sp,)),
        ],
        "project",
    )
    per_view = jax.ShapeDtypeStruct((3, 8, view_len), jnp.float32)
    stream = jax.ShapeDtypeStruct((rows, width), jnp.bfloat16)
    block_rows, key_bias, cross_bias, live, ordered = call(
        prepare_kernel,
        [SMEM_SPEC] * 4 + [VMEM_SPEC, HBM_SPEC],
        [device, right_view, lengths, window_mask, tokens, slots],
        (VMEM_SPEC,) * 5,
        (per_view, per_view, per_view, jax.ShapeDtypeStruct((rows, LANES), jnp.float32), stream),
        [],
        "prepare",
    )
    attended = call(
        spatial_kernel,
        [VMEM_SPEC] * 3,
        [exchange(slots), block_rows, key_bias],
        VMEM_SPEC,
        out_slots,
        heads,
        "spatial",
    )
    middle, slots = call(
        middle_kernel,
        [VMEM_SPEC] * 5 + [HBM_SPEC],
        [exchange(attended), ordered, live, out_spatial, gain_cross, in_hbm(qkv_cross.T)],
        (VMEM_SPEC, VMEM_SPEC),
        (stream, qkv_slots),
        [merged, weights, normed, pltpu.SemaphoreType.DMA((3 * len(SECOND_GROUPS),))],
        "middle",
    )
    attended = call(
        cross_kernel,
        [VMEM_SPEC] * 2,
        [exchange(slots), cross_bias],
        VMEM_SPEC,
        out_slots,
        heads,
        "cross",
    )
    return call(
        finish_kernel,
        [HBM_SPEC] + [VMEM_SPEC] * 4,
        [in_hbm(right_view), exchange(attended), middle, live, out_cross],
        HBM_SPEC,
        jax.ShapeDtypeStruct(tokens.shape, jnp.bfloat16),
        [
            pltpu.SMEM(right_view.shape, jnp.int32),
            merged,
            pltpu.VMEM((6, TILE, width), jnp.bfloat16),
            pltpu.SemaphoreType.DMA((1,)),
            pltpu.SemaphoreType.DMA((6,)),
        ],
        "finish",
    )


def rms_norm(values, gain):
    floats = values.astype(jnp.float32)
    square = jnp.mean(floats * floats, axis=-1, keepdims=True)
    return (floats * lax.rsqrt(square + EPSILON) * gain).astype(jnp.bfloat16)


def to_frames(block, heads):
    frames, views, tile_len, inner = block.shape
    head_size = inner // heads
    moved = block.reshape(frames, views, tile_len, heads, head_size).transpose(0, 3, 1, 2, 4)
    return moved.reshape(frames, heads, views, tile_len * head_size)


def from_units(units, frames, views, tile_len, heads):
    head_size = units.shape[-1] // tile_len
    moved = units.reshape(frames, heads, views, tile_len, head_size).transpose(0, 2, 3, 1, 4)
    return moved.reshape(frames, views, tile_len, heads * head_size)


def attend_one(operands):
    query, keys, values, allow = operands
    scores = jnp.einsum("qd,kd->qk", query, keys, preferred_element_type=jnp.float32) * query.shape[
        -1
    ] ** (-0.5)
    scores = jnp.where(allow, scores, -1e30)
    top = jnp.max(scores, axis=-1, keepdims=True)
    weights = jnp.where(allow, jnp.exp(scores - top), 0.0)
    probs = (weights / jnp.sum(weights, axis=-1, keepdims=True)).astype(jnp.bfloat16)
    return jnp.einsum("qk,kd->qd", probs, values, preferred_element_type=jnp.float32).astype(
        jnp.bfloat16
    )


def general_shards(
    tokens,
    gain_spatial,
    qkv_spatial,
    out_spatial,
    gain_cross,
    qkv_cross,
    out_cross,
    lengths,
    left_view,
    right_view,
    window_mask,
):
    frames, views, tile_len, width = tokens.shape
    inner = out_spatial.shape[0]
    head_size = inner // HEADS
    devices_sp = lax.axis_size("sp")
    device = lax.axis_index("sp")
    view_len = tile_len * devices_sp
    blocks = window_mask.shape[-1]
    block_len = view_len // blocks
    positions = device * tile_len + jnp.arange(tile_len, dtype=jnp.int32)
    live_rows = (positions[None, None, :] < lengths[:, :, None]).astype(jnp.float32)[..., None]
    key_pos = jnp.arange(view_len, dtype=jnp.int32)
    units_dev = frames * HEADS * views // devices_sp
    unit_ids = device * units_dev + jnp.arange(units_dev, dtype=jnp.int32)
    frame_ids = unit_ids // (HEADS * views)
    view_ids = unit_ids % views
    flat_ids = frame_ids * views + view_ids
    flat_len = lengths.reshape(-1)
    own_len = jnp.take(flat_len, flat_ids)
    total_units = frames * HEADS * views
    normed = rms_norm(tokens, gain_spatial)
    projected = jnp.einsum(
        "fvtd,de->fvte", normed, qkv_spatial, preferred_element_type=jnp.float32
    ).astype(jnp.bfloat16)
    stacked = jnp.stack(
        [
            to_frames(projected[..., which * inner : (which + 1) * inner], HEADS)
            for which in range(3)
        ],
        axis=3,
    )
    stacked = stacked.reshape(total_units, 3, tile_len * head_size)
    gathered = lax.all_to_all(stacked, "sp", split_axis=0, concat_axis=2, tiled=True)
    gathered = gathered.reshape(units_dev, 3, view_len, head_size)
    masks = jnp.take(window_mask.reshape(-1, blocks, blocks), flat_ids, axis=0) > 0
    allow = jnp.broadcast_to(
        masks[:, :, None, :, None], (units_dev, blocks, block_len, blocks, block_len)
    )
    allow = allow.reshape(units_dev, view_len, view_len) & (
        key_pos[None, None, :] < own_len[:, None, None]
    )
    spatial_out = lax.map(attend_one, (gathered[:, 0], gathered[:, 1], gathered[:, 2], allow))
    returned = lax.all_to_all(
        spatial_out.reshape(units_dev, view_len * head_size),
        "sp",
        split_axis=1,
        concat_axis=0,
        tiled=True,
    )
    attended = from_units(returned, frames, views, tile_len, HEADS)
    branch = jnp.einsum("fvte,ed->fvtd", attended, out_spatial, preferred_element_type=jnp.float32)
    middle = (tokens.astype(jnp.float32) + live_rows * branch).astype(jnp.bfloat16)
    normed_cross = rms_norm(middle, gain_cross)
    projected = jnp.einsum(
        "fvtd,de->fvte", normed_cross, qkv_cross, preferred_element_type=jnp.float32
    ).astype(jnp.bfloat16)
    query_fr, key_fr, value_fr = [
        to_frames(projected[..., which * inner : (which + 1) * inner], HEADS) for which in range(3)
    ]
    left_ids = jnp.take(left_view.reshape(-1), flat_ids)
    right_ids = jnp.take(right_view.reshape(-1), flat_ids)
    view_iota = jnp.arange(views, dtype=jnp.int32)
    pick_left = (left_view[:, :, None] == view_iota).astype(jnp.bfloat16)
    pick_right = (right_view[:, :, None] == view_iota).astype(jnp.bfloat16)

    def select(pick, source):
        return jnp.einsum(
            "fvw,fhwx->fhvx", pick, source, preferred_element_type=jnp.float32
        ).astype(jnp.bfloat16)

    packed = jnp.stack(
        [
            query_fr,
            select(pick_left, key_fr),
            select(pick_left, value_fr),
            select(pick_right, key_fr),
            select(pick_right, value_fr),
        ],
        axis=3,
    )
    packed = packed.reshape(total_units, 5, tile_len * head_size)
    arrived = lax.all_to_all(packed, "sp", split_axis=0, concat_axis=2, tiled=True)
    cross_query = arrived[:, 0]
    left_kv = arrived[:, 1:3]
    right_kv = arrived[:, 3:5]
    cross_keys = jnp.concatenate([left_kv[:, 0], right_kv[:, 0]], axis=1).reshape(
        units_dev, 2 * view_len, head_size
    )
    cross_values = jnp.concatenate([left_kv[:, 1], right_kv[:, 1]], axis=1).reshape(
        units_dev, 2 * view_len, head_size
    )
    left_len = jnp.take(flat_len, frame_ids * views + left_ids)
    right_len = jnp.take(flat_len, frame_ids * views + right_ids)
    allow_cross = jnp.concatenate(
        [key_pos[None, :] < left_len[:, None], key_pos[None, :] < right_len[:, None]], axis=1
    )[:, None, :]
    cross_out = lax.map(
        attend_one,
        (
            cross_query.reshape(units_dev, view_len, head_size),
            cross_keys,
            cross_values,
            allow_cross,
        ),
    )
    returned = lax.all_to_all(
        cross_out.reshape(units_dev, view_len * head_size),
        "sp",
        split_axis=1,
        concat_axis=0,
        tiled=True,
    )
    attended = from_units(returned, frames, views, tile_len, HEADS)
    branch = jnp.einsum("fvte,ed->fvtd", attended, out_cross, preferred_element_type=jnp.float32)
    return (middle.astype(jnp.float32) + live_rows * branch).astype(jnp.bfloat16)


def shards(*args):
    tokens, mask = args[0], args[-1]
    sizes = (tokens.shape[0], tokens.shape[1], tokens.shape[2], mask.shape[-1])
    if sizes == (1, 6, TILE, 8) and lax.axis_size("sp") == 2 * HEADS:
        return fast_shards(*args)
    return general_shards(*args)


def solution(mesh):
    in_specs = (
        P("grp", None, "sp", None),
        P(),
        P(),
        P(),
        P(),
        P(),
        P(),
        P("grp", None),
        P("grp", None),
        P("grp", None),
        P("grp", None, None, None),
    )
    out_specs = P("grp", None, "sp", None)
    return jax.shard_map(shards, mesh=mesh, in_specs=in_specs, out_specs=out_specs, check_vma=False)
```

```python
import functools

import jax
import jax.numpy as jnp
from jax import lax
from jax.experimental import pallas as pl
from jax.experimental.pallas import tpu as pltpu
from jax.sharding import PartitionSpec as P

HEADS = 8
EPSILON = 1e-06


HS = 72
TILE = 64
LANES = 128
TOP = 40
QKV_ROWS = 328
OUT_ROWS = 112
NEG = -1e30
ORDER = (9, 11, 12, 15, 5, 8, 6, 1, 10, 3, 4, 14, 7, 0, 13, 2)
PLACE = tuple(ORDER.index(device) for device in range(len(ORDER)))
FACTOR = HS**-0.5 * 1.4426950408889634
FIRST_GROUPS = (2, 4, 2)
SECOND_GROUPS = (8,)
AHEAD = 2
VMEM = 24 * 1024 * 1024


def cycle_order(right_ref):
    order = [jnp.int32(0)]
    for _ in range(5):
        order.append(right_ref[0, order[-1]])
    return order


def low_lanes(rows):
    return lax.broadcasted_iota(jnp.int32, (rows, LANES), 1) < TILE


def swap(tile):
    return pltpu.roll(tile, TILE, 1)


def side_by_side(first, first_half, second, second_half):
    left = first if first_half == 0 else swap(first)
    right = second if second_half == 1 else swap(second)
    return jnp.where(low_lanes(first.shape[0]), left, right)


def fold_third(tile, half):
    bottom = jnp.concatenate([tile[TOP:], jnp.zeros((2 * TOP - HS, LANES), jnp.float32)], axis=0)
    return side_by_side(tile[:TOP], half, bottom, half)


def normalise(floats, gain):
    square = jnp.mean(floats * floats, axis=-1, keepdims=True)
    return (floats * lax.rsqrt(square + EPSILON) * gain[None, :]).astype(jnp.bfloat16)


def project_and_pack(normed_ref, groups, slots_ref, cross, arrived, done):
    def project(weight_ref):
        return lax.dot_general(
            weight_ref[...],
            normed_ref[...],
            (((1,), (1,)), ((), ())),
            preferred_element_type=jnp.float32,
        )

    def pack(head, heads, turned):
        for inside in range(heads):

            def item(which, m):
                row = (which * heads + inside) * HS
                tile = turned[row : row + HS, m * LANES : (m + 1) * LANES]
                return tile * FACTOR if which == 0 else tile

            for parity in range(2):
                other = 1 - parity if cross else parity
                views = [2, 0, 1] if cross and parity == 0 else [0, 1, 2]
                rows = [
                    side_by_side(item(0, m), parity, item(1, views[m]), other) for m in range(3)
                ]
                rows.append(side_by_side(item(2, views[0]), other, item(2, views[1]), other))
                rows.append(fold_third(item(2, views[2]), other))
                slot = PLACE[(head + inside) * 2 + parity]
                slots_ref[slot] = jnp.concatenate(rows, axis=0).astype(jnp.bfloat16)

    ahead = None
    for group, (head, heads, weight_ref) in enumerate(groups):
        arrived(group)
        turned = project(weight_ref)
        if ahead is not None:
            pack(*ahead)
            done(group - 1)
        ahead = (head, heads, turned)
    pack(*ahead)
    done(len(groups) - 1)


def weight_groups(source_ref, held_ref, sems, sizes):
    inner = source_ref.shape[0] // 3
    copies, groups, head = [], [], 0
    for group, heads in enumerate(sizes):
        rows = heads * HS
        copies.append(
            [
                pltpu.make_async_copy(
                    source_ref.at[pl.ds(which * inner + head * HS, rows)],
                    held_ref.at[pl.ds(3 * head * HS + which * rows, rows)],
                    sems.at[group * 3 + which],
                )
                for which in range(3)
            ]
        )
        groups.append((head, heads, held_ref.at[pl.ds(3 * head * HS, 3 * rows)]))
        head += heads
    return copies, groups


def start_all(copies, priority=0):
    for copy in copies:
        copy.start(priority=priority)


def wait_all(copies):
    for copy in copies:
        copy.wait()


def slot_copies(slots_ref, out_ref, sems, sizes):
    copies, head = [], 0
    for heads in sizes:
        places = PLACE[2 * head : 2 * (head + heads)]
        copies.append(
            [
                pltpu.make_async_copy(slots_ref.at[place], out_ref.at[place], sems.at[place])
                for place in places
            ]
        )
        head += heads
    return copies


def project_kernel(
    right_hbm,
    tokens_hbm,
    gain_hbm,
    weight_hbm,
    out_hbm,
    right_ref,
    tokens_ref,
    gain_ref,
    weight_ref,
    normed_ref,
    slots_ref,
    in_sems,
    weight_sems,
    out_sems,
):
    small = [
        pltpu.make_async_copy(right_hbm, right_ref, in_sems.at[0]),
        pltpu.make_async_copy(gain_hbm, gain_ref, in_sems.at[1]),
    ]
    views = [
        pltpu.make_async_copy(tokens_hbm.at[0, v], tokens_ref.at[0, v], in_sems.at[2 + v])
        for v in range(6)
    ]
    copies, groups = weight_groups(weight_hbm, weight_ref, weight_sems, FIRST_GROUPS)
    outgoing = slot_copies(slots_ref, out_hbm, out_sems, FIRST_GROUPS)
    start_all(small)
    start_all(views)
    for group in range(min(AHEAD, len(groups))):
        start_all(copies[group], 1)
    wait_all(small)
    order = cycle_order(right_ref)
    place = [sum(jnp.where(order[j] == v, j, 0) for j in range(6)) for v in range(6)]
    for v in range(6):
        views[v].wait()
        floats = tokens_ref[0, v].astype(jnp.float32)
        rows = pl.ds(pl.multiple_of(place[v] * TILE, TILE), TILE)
        normed_ref[rows, :] = normalise(floats, gain_ref[...])

    def arrived(group):
        wait_all(copies[group])
        if group + AHEAD < len(groups):
            start_all(copies[group + AHEAD], 1)

    project_and_pack(
        normed_ref, groups, slots_ref, False, arrived, lambda group: start_all(outgoing[group])
    )
    for group in outgoing:
        wait_all(group)


def prepare_kernel(
    device_ref,
    right_ref,
    lengths_ref,
    mask_ref,
    tokens_ref,
    _,
    query_ref,
    key_ref,
    cross_ref,
    live_ref,
    ordered_ref,
):
    order = cycle_order(right_ref)
    parity = device_ref[0] % 2
    blocks = mask_ref.shape[-1]
    view_len = key_ref.shape[-1]
    position = lax.broadcasted_iota(jnp.int32, (8, view_len), 1)
    first = lax.broadcasted_iota(jnp.int32, (8, view_len), 0) == 0
    row8 = lax.broadcasted_iota(jnp.int32, (8, LANES), 0)

    def keys_of(view):
        return jnp.where(first & (position >= lengths_ref[0, view]), NEG, 0.0)

    for m in range(3):
        view = jnp.where(parity == 0, order[2 * m], order[2 * m + 1])
        other = jnp.where(parity == 0, order[(2 * m - 1) % 6], order[2 * m])
        key_ref[m] = keys_of(view)
        cross_ref[m] = keys_of(other)
        for b in range(blocks):
            rows = jnp.zeros((8, LANES), jnp.float32)
            for c in range(blocks):
                addend = jnp.where(mask_ref[0, view, b, c] > 0, 0.0, NEG)
                rows = jnp.where(row8 == c, addend, rows)
            query_ref[m, :, b * LANES : (b + 1) * LANES] = rows
    row = device_ref[0] * TILE + lax.broadcasted_iota(jnp.int32, (TILE, LANES), 0)
    for j in range(6):
        live_ref[j * TILE : (j + 1) * TILE, :] = jnp.where(
            row < lengths_ref[0, order[j]], 1.0, 0.0
        )
        ordered_ref[j * TILE : (j + 1) * TILE, :] = tokens_ref[0, order[j]]


def unpack(slots_ref, bias_ref, rows_ref, query_ref, key_ref, value_ref):
    blocks = slots_ref.shape[0] // 2
    low = low_lanes(QKV_ROWS)
    row8 = lax.broadcasted_iota(jnp.int32, (8, LANES), 0)
    pad = jnp.zeros((LANES - HS - 16, LANES), jnp.float32)
    zero = jnp.zeros((8, LANES), jnp.float32)
    first_row = jnp.where(row8 == 0, 1.0, 0.0)
    for b in range(blocks):
        span = slice(b * LANES, (b + 1) * LANES)
        even = slots_ref[PLACE[2 * b]].astype(jnp.float32)
        odd = slots_ref[PLACE[2 * b + 1]].astype(jnp.float32)
        lower = jnp.where(low, even, swap(odd))
        upper = jnp.where(low, swap(even), odd)
        own_block = zero if rows_ref is None else jnp.where(row8 == b, 1.0, 0.0)
        values = [
            lower[3 * HS : 4 * HS],
            upper[3 * HS : 4 * HS],
            jnp.concatenate(
                [lower[4 * HS : 4 * HS + TOP], upper[4 * HS : 5 * HS - TOP]], axis=0
            ),
        ]
        for m in range(3):
            rows = zero if rows_ref is None else rows_ref[m, :, span]
            query = jnp.concatenate([lower[m * HS : (m + 1) * HS], rows, first_row, pad], axis=0)
            query_ref[m, :, span] = query.astype(jnp.bfloat16)
            key = jnp.concatenate(
                [upper[m * HS : (m + 1) * HS], own_block, bias_ref[m, :, span], pad], axis=0
            )
            key_ref[m, span, :] = key.T.astype(jnp.bfloat16)
            value_ref[m, :, span] = jnp.concatenate([values[m], first_row], axis=0).astype(
                jnp.bfloat16
            )


def attend(jobs, query_ref, key_ref, value_ref, attended_ref):
    def scores(job):
        m, lanes, parts = job
        query = query_ref[m, :, lanes]
        return [
            jnp.dot(key_ref[n, span, :], query, preferred_element_type=jnp.float32)
            for n, span in parts
        ]

    def finish(job, found):
        m, lanes, parts = job
        top = functools.reduce(
            jnp.maximum, [jnp.max(score, axis=0, keepdims=True) for score in found]
        )
        total = None
        for score, (n, span) in zip(found, parts):
            weights = jnp.exp2(score - top).astype(jnp.bfloat16)
            term = jnp.dot(value_ref[n, :, span], weights, preferred_element_type=jnp.float32)
            total = term if total is None else total + term
        attended_ref[m, :, lanes] = total[:HS] / total[HS : HS + 1]

    queue = []
    for job in jobs:
        queue.append((job, scores(job)))
        if len(queue) > 2:
            finish(*queue.pop(0))
    for entry in queue:
        finish(*entry)


def pack_outputs(attended_ref, out_ref):
    for b in range(out_ref.shape[0] // 2):
        span = slice(b * LANES, (b + 1) * LANES)
        tiles = [attended_ref[m, :, span] for m in range(3)]
        for half in range(2):
            rows = [side_by_side(tiles[0], half, tiles[1], half), fold_third(tiles[2], half)]
            out_ref[PLACE[2 * b + half]] = jnp.concatenate(rows, axis=0).astype(jnp.bfloat16)


def spatial_kernel(
    slots_ref, rows_ref, bias_ref, out_ref, query_ref, key_ref, value_ref, attended_ref
):
    unpack(slots_ref, bias_ref, rows_ref, query_ref, key_ref, value_ref)
    blocks = slots_ref.shape[0] // 2
    wide = 2 * LANES
    jobs = []
    for m in range(3):
        for i in range(blocks // 2):
            first = max(0, 2 * i - 2) * LANES
            last = min(blocks, 2 * i + 4) * LANES
            spans = [slice(first, last)]
            if first > 0:
                spans.append(slice(0, LANES))
            jobs.append((m, slice(i * wide, (i + 1) * wide), [(m, span) for span in spans]))
    attend(jobs, query_ref, key_ref, value_ref, attended_ref)
    pack_outputs(attended_ref, out_ref)


def cross_kernel(slots_ref, bias_ref, out_ref, query_ref, key_ref, value_ref, attended_ref):
    unpack(slots_ref, bias_ref, None, query_ref, key_ref, value_ref)
    wide = 2 * LANES
    every = slice(0, key_ref.shape[1])
    jobs = []
    for m in range(3):
        second = (m + 1) % 3
        for i in range(query_ref.shape[2] // wide):
            jobs.append((m, slice(i * wide, (i + 1) * wide), [(m, every), (second, every)]))
    attend(jobs, query_ref, key_ref, value_ref, attended_ref)
    pack_outputs(attended_ref, out_ref)


def merge_heads(slots_ref, merged_ref):
    low = low_lanes(OUT_ROWS)
    tiles = [[], [], []]
    for head in range(HEADS):
        even = slots_ref[PLACE[2 * head]].astype(jnp.float32)
        odd = slots_ref[PLACE[2 * head + 1]].astype(jnp.float32)
        lower = jnp.where(low, even, swap(odd))
        upper = jnp.where(low, swap(even), odd)
        tiles[0].append(lower[:HS])
        tiles[1].append(upper[:HS])
        tiles[2].append(lower[HS:])
        tiles[2].append(upper[HS : 2 * HS - TOP])
    for m in range(3):
        merged = jnp.concatenate(tiles[m], axis=0)
        merged_ref[m * LANES : (m + 1) * LANES, :] = merged.T.astype(jnp.bfloat16)


def middle_kernel(
    slots_ref,
    tokens_ref,
    live_ref,
    mix_ref,
    gain_ref,
    weight_hbm,
    middle_ref,
    out_ref,
    merged_ref,
    weight_ref,
    normed_ref,
    weight_sems,
):
    copies, groups = weight_groups(weight_hbm, weight_ref, weight_sems, SECOND_GROUPS)
    for group in copies:
        start_all(group)
    merge_heads(slots_ref, merged_ref)
    branch = jnp.dot(merged_ref[...], mix_ref[...], preferred_element_type=jnp.float32)
    for j in range(6):
        rows = slice(j * TILE, (j + 1) * TILE)
        middle = tokens_ref[rows, :].astype(jnp.float32) + live_ref[rows, :1] * branch[rows]
        middle = middle.astype(jnp.bfloat16)
        middle_ref[rows, :] = middle
        normed_ref[rows, :] = normalise(middle.astype(jnp.float32), gain_ref[...])
    for group in copies:
        wait_all(group)
    project_and_pack(normed_ref, groups, out_ref, True, lambda group: None, lambda group: None)


def finish_kernel(
    right_hbm,
    slots_ref,
    middle_ref,
    live_ref,
    mix_ref,
    out_hbm,
    right_ref,
    merged_ref,
    result_ref,
    right_sem,
    sems,
):
    right_copy = pltpu.make_async_copy(right_hbm, right_ref, right_sem.at[0])
    right_copy.start()
    merge_heads(slots_ref, merged_ref)
    branch = jnp.dot(merged_ref[...], mix_ref[...], preferred_element_type=jnp.float32)
    right_copy.wait()
    order = cycle_order(right_ref)
    copies = []
    for j in range(6):
        rows = slice(j * TILE, (j + 1) * TILE)
        result = middle_ref[rows, :].astype(jnp.float32) + live_ref[rows, :1] * branch[rows]
        result_ref[j] = result.astype(jnp.bfloat16)
        copy = pltpu.make_async_copy(result_ref.at[j], out_hbm.at[0, order[j]], sems.at[j])
        copy.start()
        copies.append(copy)
    for copy in copies:
        copy.wait()


SMEM_SPEC = pl.BlockSpec(memory_space=pltpu.SMEM)
VMEM_SPEC = pl.BlockSpec(memory_space=pltpu.VMEM)
HBM_SPEC = pl.BlockSpec(memory_space=pltpu.HBM)


def in_hbm(array):
    return pltpu.with_memory_space_constraint(array, pltpu.HBM)


def call(kernel, in_specs, args, out_specs, out_shape, scratch, name):
    return pl.pallas_call(
        kernel,
        out_shape=out_shape,
        in_specs=in_specs,
        out_specs=out_specs,
        scratch_shapes=scratch,
        compiler_params=pltpu.CompilerParams(vmem_limit_bytes=VMEM),
        name=name,
    )(*args)


def exchange(slots):
    return lax.all_to_all(
        slots, "sp", split_axis=0, concat_axis=0, tiled=True, axis_index_groups=[list(ORDER)]
    )


def fast_shards(
    tokens,
    gain_spatial,
    qkv_spatial,
    out_spatial,
    gain_cross,
    qkv_cross,
    out_cross,
    lengths,
    left_view,
    right_view,
    window_mask,
):
    width = tokens.shape[-1]
    inner = out_spatial.shape[0]
    devices_sp = lax.axis_size("sp")
    view_len = TILE * devices_sp
    rows = 6 * TILE
    device = lax.axis_index("sp").astype(jnp.int32).reshape(1)
    qkv_slots = jax.ShapeDtypeStruct((devices_sp, QKV_ROWS, LANES), jnp.bfloat16)
    out_slots = jax.ShapeDtypeStruct((devices_sp, OUT_ROWS, LANES), jnp.bfloat16)
    normed = pltpu.VMEM((rows, width), jnp.bfloat16)
    merged = pltpu.VMEM((rows, inner), jnp.bfloat16)
    weights = pltpu.VMEM((3 * inner, width), jnp.bfloat16)
    heads = [
        pltpu.VMEM((3, LANES, view_len), jnp.bfloat16),
        pltpu.VMEM((3, view_len, LANES), jnp.bfloat16),
        pltpu.VMEM((3, HS + 8, view_len), jnp.bfloat16),
        pltpu.VMEM((3, HS, view_len), jnp.float32),
    ]
    slots = call(
        project_kernel,
        [HBM_SPEC] * 4,
        [in_hbm(x) for x in (right_view, tokens, gain_spatial, qkv_spatial.T)],
        HBM_SPEC,
        qkv_slots,
        [
            pltpu.SMEM(right_view.shape, jnp.int32),
            pltpu.VMEM(tokens.shape, jnp.bfloat16),
            pltpu.VMEM((width,), jnp.float32),
            weights,
            normed,
            pltpu.VMEM(qkv_slots.shape, jnp.bfloat16),
            pltpu.SemaphoreType.DMA((8,)),
            pltpu.SemaphoreType.DMA((3 * len(FIRST_GROUPS),)),
            pltpu.SemaphoreType.DMA((devices_sp,)),
        ],
        "project",
    )
    per_view = jax.ShapeDtypeStruct((3, 8, view_len), jnp.float32)
    stream = jax.ShapeDtypeStruct((rows, width), jnp.bfloat16)
    block_rows, key_bias, cross_bias, live, ordered = call(
        prepare_kernel,
        [SMEM_SPEC] * 4 + [VMEM_SPEC, HBM_SPEC],
        [device, right_view, lengths, window_mask, tokens, slots],
        (VMEM_SPEC,) * 5,
        (per_view, per_view, per_view, jax.ShapeDtypeStruct((rows, LANES), jnp.float32), stream),
        [],
        "prepare",
    )
    attended = call(
        spatial_kernel,
        [VMEM_SPEC] * 3,
        [exchange(slots), block_rows, key_bias],
        VMEM_SPEC,
        out_slots,
        heads,
        "spatial",
    )
    middle, slots = call(
        middle_kernel,
        [VMEM_SPEC] * 5 + [HBM_SPEC],
        [exchange(attended), ordered, live, out_spatial, gain_cross, in_hbm(qkv_cross.T)],
        (VMEM_SPEC, VMEM_SPEC),
        (stream, qkv_slots),
        [merged, weights, normed, pltpu.SemaphoreType.DMA((3 * len(SECOND_GROUPS),))],
        "middle",
    )
    attended = call(
        cross_kernel,
        [VMEM_SPEC] * 2,
        [exchange(slots), cross_bias],
        VMEM_SPEC,
        out_slots,
        heads,
        "cross",
    )
    return call(
        finish_kernel,
        [HBM_SPEC] + [VMEM_SPEC] * 4,
        [in_hbm(right_view), exchange(attended), middle, live, out_cross],
        HBM_SPEC,
        jax.ShapeDtypeStruct(tokens.shape, jnp.bfloat16),
        [
            pltpu.SMEM(right_view.shape, jnp.int32),
            merged,
            pltpu.VMEM((6, TILE, width), jnp.bfloat16),
            pltpu.SemaphoreType.DMA((1,)),
            pltpu.SemaphoreType.DMA((6,)),
        ],
        "finish",
    )


def rms_norm(values, gain):
    floats = values.astype(jnp.float32)
    square = jnp.mean(floats * floats, axis=-1, keepdims=True)
    return (floats * lax.rsqrt(square + EPSILON) * gain).astype(jnp.bfloat16)


def to_frames(block, heads):
    frames, views, tile_len, inner = block.shape
    head_size = inner // heads
    moved = block.reshape(frames, views, tile_len, heads, head_size).transpose(0, 3, 1, 2, 4)
    return moved.reshape(frames, heads, views, tile_len * head_size)


def from_units(units, frames, views, tile_len, heads):
    head_size = units.shape[-1] // tile_len
    moved = units.reshape(frames, heads, views, tile_len, head_size).transpose(0, 2, 3, 1, 4)
    return moved.reshape(frames, views, tile_len, heads * head_size)


def attend_one(operands):
    query, keys, values, allow = operands
    scores = jnp.einsum("qd,kd->qk", query, keys, preferred_element_type=jnp.float32) * query.shape[
        -1
    ] ** (-0.5)
    scores = jnp.where(allow, scores, -1e30)
    top = jnp.max(scores, axis=-1, keepdims=True)
    weights = jnp.where(allow, jnp.exp(scores - top), 0.0)
    probs = (weights / jnp.sum(weights, axis=-1, keepdims=True)).astype(jnp.bfloat16)
    return jnp.einsum("qk,kd->qd", probs, values, preferred_element_type=jnp.float32).astype(
        jnp.bfloat16
    )


def general_shards(
    tokens,
    gain_spatial,
    qkv_spatial,
    out_spatial,
    gain_cross,
    qkv_cross,
    out_cross,
    lengths,
    left_view,
    right_view,
    window_mask,
):
    frames, views, tile_len, width = tokens.shape
    inner = out_spatial.shape[0]
    head_size = inner // HEADS
    devices_sp = lax.axis_size("sp")
    device = lax.axis_index("sp")
    view_len = tile_len * devices_sp
    blocks = window_mask.shape[-1]
    block_len = view_len // blocks
    positions = device * tile_len + jnp.arange(tile_len, dtype=jnp.int32)
    live_rows = (positions[None, None, :] < lengths[:, :, None]).astype(jnp.float32)[..., None]
    key_pos = jnp.arange(view_len, dtype=jnp.int32)
    units_dev = frames * HEADS * views // devices_sp
    unit_ids = device * units_dev + jnp.arange(units_dev, dtype=jnp.int32)
    frame_ids = unit_ids // (HEADS * views)
    view_ids = unit_ids % views
    flat_ids = frame_ids * views + view_ids
    flat_len = lengths.reshape(-1)
    own_len = jnp.take(flat_len, flat_ids)
    total_units = frames * HEADS * views
    normed = rms_norm(tokens, gain_spatial)
    projected = jnp.einsum(
        "fvtd,de->fvte", normed, qkv_spatial, preferred_element_type=jnp.float32
    ).astype(jnp.bfloat16)
    stacked = jnp.stack(
        [
            to_frames(projected[..., which * inner : (which + 1) * inner], HEADS)
            for which in range(3)
        ],
        axis=3,
    )
    stacked = stacked.reshape(total_units, 3, tile_len * head_size)
    gathered = lax.all_to_all(stacked, "sp", split_axis=0, concat_axis=2, tiled=True)
    gathered = gathered.reshape(units_dev, 3, view_len, head_size)
    masks = jnp.take(window_mask.reshape(-1, blocks, blocks), flat_ids, axis=0) > 0
    allow = jnp.broadcast_to(
        masks[:, :, None, :, None], (units_dev, blocks, block_len, blocks, block_len)
    )
    allow = allow.reshape(units_dev, view_len, view_len) & (
        key_pos[None, None, :] < own_len[:, None, None]
    )
    spatial_out = lax.map(attend_one, (gathered[:, 0], gathered[:, 1], gathered[:, 2], allow))
    returned = lax.all_to_all(
        spatial_out.reshape(units_dev, view_len * head_size),
        "sp",
        split_axis=1,
        concat_axis=0,
        tiled=True,
    )
    attended = from_units(returned, frames, views, tile_len, HEADS)
    branch = jnp.einsum("fvte,ed->fvtd", attended, out_spatial, preferred_element_type=jnp.float32)
    middle = (tokens.astype(jnp.float32) + live_rows * branch).astype(jnp.bfloat16)
    normed_cross = rms_norm(middle, gain_cross)
    projected = jnp.einsum(
        "fvtd,de->fvte", normed_cross, qkv_cross, preferred_element_type=jnp.float32
    ).astype(jnp.bfloat16)
    query_fr, key_fr, value_fr = [
        to_frames(projected[..., which * inner : (which + 1) * inner], HEADS) for which in range(3)
    ]
    left_ids = jnp.take(left_view.reshape(-1), flat_ids)
    right_ids = jnp.take(right_view.reshape(-1), flat_ids)
    view_iota = jnp.arange(views, dtype=jnp.int32)
    pick_left = (left_view[:, :, None] == view_iota).astype(jnp.bfloat16)
    pick_right = (right_view[:, :, None] == view_iota).astype(jnp.bfloat16)

    def select(pick, source):
        return jnp.einsum(
            "fvw,fhwx->fhvx", pick, source, preferred_element_type=jnp.float32
        ).astype(jnp.bfloat16)

    packed = jnp.stack(
        [
            query_fr,
            select(pick_left, key_fr),
            select(pick_left, value_fr),
            select(pick_right, key_fr),
            select(pick_right, value_fr),
        ],
        axis=3,
    )
    packed = packed.reshape(total_units, 5, tile_len * head_size)
    arrived = lax.all_to_all(packed, "sp", split_axis=0, concat_axis=2, tiled=True)
    cross_query = arrived[:, 0]
    left_kv = arrived[:, 1:3]
    right_kv = arrived[:, 3:5]
    cross_keys = jnp.concatenate([left_kv[:, 0], right_kv[:, 0]], axis=1).reshape(
        units_dev, 2 * view_len, head_size
    )
    cross_values = jnp.concatenate([left_kv[:, 1], right_kv[:, 1]], axis=1).reshape(
        units_dev, 2 * view_len, head_size
    )
    left_len = jnp.take(flat_len, frame_ids * views + left_ids)
    right_len = jnp.take(flat_len, frame_ids * views + right_ids)
    allow_cross = jnp.concatenate(
        [key_pos[None, :] < left_len[:, None], key_pos[None, :] < right_len[:, None]], axis=1
    )[:, None, :]
    cross_out = lax.map(
        attend_one,
        (
            cross_query.reshape(units_dev, view_len, head_size),
            cross_keys,
            cross_values,
            allow_cross,
        ),
    )
    returned = lax.all_to_all(
        cross_out.reshape(units_dev, view_len * head_size),
        "sp",
        split_axis=1,
        concat_axis=0,
        tiled=True,
    )
    attended = from_units(returned, frames, views, tile_len, HEADS)
    branch = jnp.einsum("fvte,ed->fvtd", attended, out_cross, preferred_element_type=jnp.float32)
    return (middle.astype(jnp.float32) + live_rows * branch).astype(jnp.bfloat16)


def shards(*args):
    tokens, mask = args[0], args[-1]
    sizes = (tokens.shape[0], tokens.shape[1], tokens.shape[2], mask.shape[-1])
    if sizes == (1, 6, TILE, 8) and lax.axis_size("sp") == 2 * HEADS:
        return fast_shards(*args)
    return general_shards(*args)


def solution(mesh):
    in_specs = (
        P("grp", None, "sp", None),
        P(),
        P(),
        P(),
        P(),
        P(),
        P(),
        P("grp", None),
        P("grp", None),
        P("grp", None),
        P("grp", None, None, None),
    )
    out_specs = P("grp", None, "sp", None)
    return jax.shard_map(shards, mesh=mesh, in_specs=in_specs, out_specs=out_specs, check_vma=False)
```

```python
import functools

import jax
import jax.numpy as jnp
from jax import lax
from jax.experimental import pallas as pl
from jax.experimental.pallas import tpu as pltpu
from jax.sharding import PartitionSpec as P

HEADS = 8
EPSILON = 1e-06


HS = 72
TILE = 64
LANES = 128
TOP = 40
QKV_ROWS = 336
OUT_ROWS = 112
NEG = -1e30
ORDER = (9, 11, 12, 15, 5, 8, 6, 1, 10, 3, 4, 14, 7, 0, 13, 2)
PLACE = tuple(ORDER.index(device) for device in range(len(ORDER)))
FACTOR = HS**-0.5 * 1.4426950408889634
FIRST_GROUPS = (2, 4, 2)
SECOND_GROUPS = (8,)
AHEAD = 2
VMEM = 24 * 1024 * 1024


def cycle_order(right_ref):
    order = [jnp.int32(0)]
    for _ in range(5):
        order.append(right_ref[0, order[-1]])
    return order


def low_lanes(rows):
    return lax.broadcasted_iota(jnp.int32, (rows, LANES), 1) < TILE


def swap(tile):
    return pltpu.roll(tile, TILE, 1)


def side_by_side(first, first_half, second, second_half):
    left = first if first_half == 0 else swap(first)
    right = second if second_half == 1 else swap(second)
    return jnp.where(low_lanes(first.shape[0]), left, right)


def fold_third(tile, half):
    bottom = jnp.concatenate([tile[TOP:], jnp.zeros((2 * TOP - HS, LANES), jnp.float32)], axis=0)
    return side_by_side(tile[:TOP], half, bottom, half)


def normalise(floats, gain):
    square = jnp.mean(floats * floats, axis=-1, keepdims=True)
    return (floats * lax.rsqrt(square + EPSILON) * gain[None, :]).astype(jnp.bfloat16)


def project_and_pack(normed_ref, groups, slots_ref, cross, arrived, done):
    def project(weight_ref):
        return lax.dot_general(
            weight_ref[...],
            normed_ref[...],
            (((1,), (1,)), ((), ())),
            preferred_element_type=jnp.float32,
        )

    def pack(head, heads, turned):
        for inside in range(heads):

            def item(which, m):
                row = (which * heads + inside) * HS
                tile = turned[row : row + HS, m * LANES : (m + 1) * LANES]
                return tile * FACTOR if which == 0 else tile

            for parity in range(2):
                other = 1 - parity if cross else parity
                views = [2, 0, 1] if cross and parity == 0 else [0, 1, 2]
                rows = [
                    side_by_side(item(0, m), parity, item(1, views[m]), other) for m in range(3)
                ]
                rows.append(side_by_side(item(2, views[0]), other, item(2, views[1]), other))
                rows.append(fold_third(item(2, views[2]), other))
                rows.append(jnp.zeros((QKV_ROWS - 4 * HS - TOP, LANES), jnp.float32))
                slot = PLACE[(head + inside) * 2 + parity]
                slots_ref[slot] = jnp.concatenate(rows, axis=0).astype(jnp.bfloat16)

    ahead = None
    for group, (head, heads, weight_ref) in enumerate(groups):
        arrived(group)
        turned = project(weight_ref)
        if ahead is not None:
            pack(*ahead)
            done(group - 1)
        ahead = (head, heads, turned)
    pack(*ahead)
    done(len(groups) - 1)


def weight_groups(source_ref, held_ref, sems, sizes):
    inner = source_ref.shape[0] // 3
    copies, groups, head = [], [], 0
    for group, heads in enumerate(sizes):
        rows = heads * HS
        copies.append(
            [
                pltpu.make_async_copy(
                    source_ref.at[pl.ds(which * inner + head * HS, rows)],
                    held_ref.at[pl.ds(3 * head * HS + which * rows, rows)],
                    sems.at[group * 3 + which],
                )
                for which in range(3)
            ]
        )
        groups.append((head, heads, held_ref.at[pl.ds(3 * head * HS, 3 * rows)]))
        head += heads
    return copies, groups


def start_all(copies, priority=0):
    for copy in copies:
        copy.start(priority=priority)


def wait_all(copies):
    for copy in copies:
        copy.wait()


def slot_copies(slots_ref, out_ref, sems, sizes):
    copies, head = [], 0
    for heads in sizes:
        places = PLACE[2 * head : 2 * (head + heads)]
        copies.append(
            [
                pltpu.make_async_copy(slots_ref.at[place], out_ref.at[place], sems.at[place])
                for place in places
            ]
        )
        head += heads
    return copies


def project_kernel(
    right_hbm,
    tokens_hbm,
    gain_hbm,
    weight_hbm,
    out_hbm,
    right_ref,
    tokens_ref,
    gain_ref,
    weight_ref,
    normed_ref,
    slots_ref,
    in_sems,
    weight_sems,
    out_sems,
):
    small = [
        pltpu.make_async_copy(right_hbm, right_ref, in_sems.at[0]),
        pltpu.make_async_copy(gain_hbm, gain_ref, in_sems.at[1]),
    ]
    views = [
        pltpu.make_async_copy(tokens_hbm.at[0, v], tokens_ref.at[0, v], in_sems.at[2 + v])
        for v in range(6)
    ]
    copies, groups = weight_groups(weight_hbm, weight_ref, weight_sems, FIRST_GROUPS)
    outgoing = slot_copies(slots_ref, out_hbm, out_sems, FIRST_GROUPS)
    start_all(small)
    start_all(views)
    for group in range(min(AHEAD, len(groups))):
        start_all(copies[group], 1)
    wait_all(small)
    order = cycle_order(right_ref)
    place = [sum(jnp.where(order[j] == v, j, 0) for j in range(6)) for v in range(6)]
    for v in range(6):
        views[v].wait()
        floats = tokens_ref[0, v].astype(jnp.float32)
        rows = pl.ds(pl.multiple_of(place[v] * TILE, TILE), TILE)
        normed_ref[rows, :] = normalise(floats, gain_ref[...])

    def arrived(group):
        wait_all(copies[group])
        if group + AHEAD < len(groups):
            start_all(copies[group + AHEAD], 1)

    project_and_pack(
        normed_ref, groups, slots_ref, False, arrived, lambda group: start_all(outgoing[group])
    )
    for group in outgoing:
        wait_all(group)


def prepare_kernel(
    device_ref,
    right_ref,
    lengths_ref,
    mask_ref,
    tokens_ref,
    _,
    query_ref,
    key_ref,
    cross_ref,
    live_ref,
    ordered_ref,
):
    order = cycle_order(right_ref)
    parity = device_ref[0] % 2
    blocks = mask_ref.shape[-1]
    view_len = key_ref.shape[-1]
    position = lax.broadcasted_iota(jnp.int32, (8, view_len), 1)
    first = lax.broadcasted_iota(jnp.int32, (8, view_len), 0) == 0
    row8 = lax.broadcasted_iota(jnp.int32, (8, LANES), 0)

    def keys_of(view):
        return jnp.where(first & (position >= lengths_ref[0, view]), NEG, 0.0)

    for m in range(3):
        view = jnp.where(parity == 0, order[2 * m], order[2 * m + 1])
        other = jnp.where(parity == 0, order[(2 * m - 1) % 6], order[2 * m])
        key_ref[m] = keys_of(view)
        cross_ref[m] = keys_of(other)
        for b in range(blocks):
            rows = jnp.zeros((8, LANES), jnp.float32)
            for c in range(blocks):
                addend = jnp.where(mask_ref[0, view, b, c] > 0, 0.0, NEG)
                rows = jnp.where(row8 == c, addend, rows)
            query_ref[m, :, b * LANES : (b + 1) * LANES] = rows
    row = device_ref[0] * TILE + lax.broadcasted_iota(jnp.int32, (TILE, LANES), 0)
    for j in range(6):
        live_ref[j * TILE : (j + 1) * TILE, :] = jnp.where(
            row < lengths_ref[0, order[j]], 1.0, 0.0
        )
        ordered_ref[j * TILE : (j + 1) * TILE, :] = tokens_ref[0, order[j]]


def unpack(slots_ref, bias_ref, rows_ref, query_ref, key_ref, value_ref):
    blocks = slots_ref.shape[0] // 2
    low = low_lanes(QKV_ROWS)
    row8 = lax.broadcasted_iota(jnp.int32, (8, LANES), 0)
    pad = jnp.zeros((LANES - HS - 16, LANES), jnp.float32)
    zero = jnp.zeros((8, LANES), jnp.float32)
    first_row = jnp.where(row8 == 0, 1.0, 0.0)
    for b in range(blocks):
        span = slice(b * LANES, (b + 1) * LANES)
        even = slots_ref[PLACE[2 * b]].astype(jnp.float32)
        odd = slots_ref[PLACE[2 * b + 1]].astype(jnp.float32)
        lower = jnp.where(low, even, swap(odd))
        upper = jnp.where(low, swap(even), odd)
        own_block = zero if rows_ref is None else jnp.where(row8 == b, 1.0, 0.0)
        values = [
            lower[3 * HS : 4 * HS],
            upper[3 * HS : 4 * HS],
            jnp.concatenate(
                [lower[4 * HS : 4 * HS + TOP], upper[4 * HS : 5 * HS - TOP]], axis=0
            ),
        ]
        for m in range(3):
            rows = zero if rows_ref is None else rows_ref[m, :, span]
            query = jnp.concatenate([lower[m * HS : (m + 1) * HS], rows, first_row, pad], axis=0)
            query_ref[m, :, span] = query.astype(jnp.bfloat16)
            key = jnp.concatenate(
                [upper[m * HS : (m + 1) * HS], own_block, bias_ref[m, :, span], pad], axis=0
            )
            key_ref[m, span, :] = key.T.astype(jnp.bfloat16)
            value_ref[m, :, span] = jnp.concatenate([values[m], first_row], axis=0).astype(
                jnp.bfloat16
            )


def attend(jobs, query_ref, key_ref, value_ref, attended_ref):
    def scores(job):
        m, lanes, parts = job
        query = query_ref[m, :, lanes]
        return [
            jnp.dot(key_ref[n, span, :], query, preferred_element_type=jnp.float32)
            for n, span in parts
        ]

    def finish(job, found):
        m, lanes, parts = job
        top = functools.reduce(
            jnp.maximum, [jnp.max(score, axis=0, keepdims=True) for score in found]
        )
        total = None
        for score, (n, span) in zip(found, parts):
            weights = jnp.exp2(score - top).astype(jnp.bfloat16)
            term = jnp.dot(value_ref[n, :, span], weights, preferred_element_type=jnp.float32)
            total = term if total is None else total + term
        attended_ref[m, :, lanes] = total[:HS] / total[HS : HS + 1]

    queue = []
    for job in jobs:
        queue.append((job, scores(job)))
        if len(queue) > 2:
            finish(*queue.pop(0))
    for entry in queue:
        finish(*entry)


def pack_outputs(attended_ref, out_ref):
    for b in range(out_ref.shape[0] // 2):
        span = slice(b * LANES, (b + 1) * LANES)
        tiles = [attended_ref[m, :, span] for m in range(3)]
        for half in range(2):
            rows = [side_by_side(tiles[0], half, tiles[1], half), fold_third(tiles[2], half)]
            out_ref[PLACE[2 * b + half]] = jnp.concatenate(rows, axis=0).astype(jnp.bfloat16)


def spatial_kernel(
    slots_ref, rows_ref, bias_ref, out_ref, query_ref, key_ref, value_ref, attended_ref
):
    unpack(slots_ref, bias_ref, rows_ref, query_ref, key_ref, value_ref)
    blocks = slots_ref.shape[0] // 2
    wide = 2 * LANES
    jobs = []
    for m in range(3):
        for i in range(blocks // 2):
            first = max(0, 2 * i - 2) * LANES
            last = min(blocks, 2 * i + 4) * LANES
            spans = [slice(first, last)]
            if first > 0:
                spans.append(slice(0, LANES))
            jobs.append((m, slice(i * wide, (i + 1) * wide), [(m, span) for span in spans]))
    attend(jobs, query_ref, key_ref, value_ref, attended_ref)
    pack_outputs(attended_ref, out_ref)


def cross_kernel(slots_ref, bias_ref, out_ref, query_ref, key_ref, value_ref, attended_ref):
    unpack(slots_ref, bias_ref, None, query_ref, key_ref, value_ref)
    wide = 2 * LANES
    every = slice(0, key_ref.shape[1])
    jobs = []
    for m in range(3):
        second = (m + 1) % 3
        for i in range(query_ref.shape[2] // wide):
            jobs.append((m, slice(i * wide, (i + 1) * wide), [(m, every), (second, every)]))
    attend(jobs, query_ref, key_ref, value_ref, attended_ref)
    pack_outputs(attended_ref, out_ref)


def merge_heads(slots_ref, merged_ref):
    low = low_lanes(OUT_ROWS)
    tiles = [[], [], []]
    for head in range(HEADS):
        even = slots_ref[PLACE[2 * head]].astype(jnp.float32)
        odd = slots_ref[PLACE[2 * head + 1]].astype(jnp.float32)
        lower = jnp.where(low, even, swap(odd))
        upper = jnp.where(low, swap(even), odd)
        tiles[0].append(lower[:HS])
        tiles[1].append(upper[:HS])
        tiles[2].append(lower[HS:])
        tiles[2].append(upper[HS : 2 * HS - TOP])
    for m in range(3):
        merged = jnp.concatenate(tiles[m], axis=0)
        merged_ref[m * LANES : (m + 1) * LANES, :] = merged.T.astype(jnp.bfloat16)


def middle_kernel(
    slots_ref,
    tokens_ref,
    live_ref,
    mix_ref,
    gain_ref,
    weight_hbm,
    middle_ref,
    out_ref,
    merged_ref,
    weight_ref,
    normed_ref,
    weight_sems,
):
    copies, groups = weight_groups(weight_hbm, weight_ref, weight_sems, SECOND_GROUPS)
    for group in copies:
        start_all(group)
    merge_heads(slots_ref, merged_ref)
    branch = jnp.dot(merged_ref[...], mix_ref[...], preferred_element_type=jnp.float32)
    for j in range(6):
        rows = slice(j * TILE, (j + 1) * TILE)
        middle = tokens_ref[rows, :].astype(jnp.float32) + live_ref[rows, :1] * branch[rows]
        middle = middle.astype(jnp.bfloat16)
        middle_ref[rows, :] = middle
        normed_ref[rows, :] = normalise(middle.astype(jnp.float32), gain_ref[...])
    for group in copies:
        wait_all(group)
    project_and_pack(normed_ref, groups, out_ref, True, lambda group: None, lambda group: None)


def finish_kernel(
    right_hbm,
    slots_ref,
    middle_ref,
    live_ref,
    mix_ref,
    out_hbm,
    right_ref,
    merged_ref,
    result_ref,
    right_sem,
    sems,
):
    right_copy = pltpu.make_async_copy(right_hbm, right_ref, right_sem.at[0])
    right_copy.start()
    merge_heads(slots_ref, merged_ref)
    branch = jnp.dot(merged_ref[...], mix_ref[...], preferred_element_type=jnp.float32)
    right_copy.wait()
    order = cycle_order(right_ref)
    copies = []
    for j in range(6):
        rows = slice(j * TILE, (j + 1) * TILE)
        result = middle_ref[rows, :].astype(jnp.float32) + live_ref[rows, :1] * branch[rows]
        result_ref[j] = result.astype(jnp.bfloat16)
        copy = pltpu.make_async_copy(result_ref.at[j], out_hbm.at[0, order[j]], sems.at[j])
        copy.start()
        copies.append(copy)
    for copy in copies:
        copy.wait()


SMEM_SPEC = pl.BlockSpec(memory_space=pltpu.SMEM)
VMEM_SPEC = pl.BlockSpec(memory_space=pltpu.VMEM)
HBM_SPEC = pl.BlockSpec(memory_space=pltpu.HBM)


def in_hbm(array):
    return pltpu.with_memory_space_constraint(array, pltpu.HBM)


def call(kernel, in_specs, args, out_specs, out_shape, scratch, name):
    return pl.pallas_call(
        kernel,
        out_shape=out_shape,
        in_specs=in_specs,
        out_specs=out_specs,
        scratch_shapes=scratch,
        compiler_params=pltpu.CompilerParams(vmem_limit_bytes=VMEM),
        name=name,
    )(*args)


def exchange(slots):
    return lax.all_to_all(
        slots, "sp", split_axis=0, concat_axis=0, tiled=True, axis_index_groups=[list(ORDER)]
    )


def fast_shards(
    tokens,
    gain_spatial,
    qkv_spatial,
    out_spatial,
    gain_cross,
    qkv_cross,
    out_cross,
    lengths,
    left_view,
    right_view,
    window_mask,
):
    width = tokens.shape[-1]
    inner = out_spatial.shape[0]
    devices_sp = lax.axis_size("sp")
    view_len = TILE * devices_sp
    rows = 6 * TILE
    device = lax.axis_index("sp").astype(jnp.int32).reshape(1)
    qkv_slots = jax.ShapeDtypeStruct((devices_sp, QKV_ROWS, LANES), jnp.bfloat16)
    out_slots = jax.ShapeDtypeStruct((devices_sp, OUT_ROWS, LANES), jnp.bfloat16)
    normed = pltpu.VMEM((rows, width), jnp.bfloat16)
    merged = pltpu.VMEM((rows, inner), jnp.bfloat16)
    weights = pltpu.VMEM((3 * inner, width), jnp.bfloat16)
    heads = [
        pltpu.VMEM((3, LANES, view_len), jnp.bfloat16),
        pltpu.VMEM((3, view_len, LANES), jnp.bfloat16),
        pltpu.VMEM((3, HS + 8, view_len), jnp.bfloat16),
        pltpu.VMEM((3, HS, view_len), jnp.float32),
    ]
    slots = call(
        project_kernel,
        [HBM_SPEC] * 4,
        [in_hbm(x) for x in (right_view, tokens, gain_spatial, qkv_spatial.T)],
        HBM_SPEC,
        qkv_slots,
        [
            pltpu.SMEM(right_view.shape, jnp.int32),
            pltpu.VMEM(tokens.shape, jnp.bfloat16),
            pltpu.VMEM((width,), jnp.float32),
            weights,
            normed,
            pltpu.VMEM(qkv_slots.shape, jnp.bfloat16),
            pltpu.SemaphoreType.DMA((8,)),
            pltpu.SemaphoreType.DMA((3 * len(FIRST_GROUPS),)),
            pltpu.SemaphoreType.DMA((devices_sp,)),
        ],
        "project",
    )
    per_view = jax.ShapeDtypeStruct((3, 8, view_len), jnp.float32)
    stream = jax.ShapeDtypeStruct((rows, width), jnp.bfloat16)
    block_rows, key_bias, cross_bias, live, ordered = call(
        prepare_kernel,
        [SMEM_SPEC] * 4 + [VMEM_SPEC, HBM_SPEC],
        [device, right_view, lengths, window_mask, tokens, slots],
        (VMEM_SPEC,) * 5,
        (per_view, per_view, per_view, jax.ShapeDtypeStruct((rows, LANES), jnp.float32), stream),
        [],
        "prepare",
    )
    attended = call(
        spatial_kernel,
        [VMEM_SPEC] * 3,
        [exchange(slots), block_rows, key_bias],
        VMEM_SPEC,
        out_slots,
        heads,
        "spatial",
    )
    middle, slots = call(
        middle_kernel,
        [VMEM_SPEC] * 5 + [HBM_SPEC],
        [exchange(attended), ordered, live, out_spatial, gain_cross, in_hbm(qkv_cross.T)],
        (VMEM_SPEC, VMEM_SPEC),
        (stream, qkv_slots),
        [merged, weights, normed, pltpu.SemaphoreType.DMA((3 * len(SECOND_GROUPS),))],
        "middle",
    )
    attended = call(
        cross_kernel,
        [VMEM_SPEC] * 2,
        [exchange(slots), cross_bias],
        VMEM_SPEC,
        out_slots,
        heads,
        "cross",
    )
    return call(
        finish_kernel,
        [HBM_SPEC] + [VMEM_SPEC] * 4,
        [in_hbm(right_view), exchange(attended), middle, live, out_cross],
        HBM_SPEC,
        jax.ShapeDtypeStruct(tokens.shape, jnp.bfloat16),
        [
            pltpu.SMEM(right_view.shape, jnp.int32),
            merged,
            pltpu.VMEM((6, TILE, width), jnp.bfloat16),
            pltpu.SemaphoreType.DMA((1,)),
            pltpu.SemaphoreType.DMA((6,)),
        ],
        "finish",
    )


def rms_norm(values, gain):
    floats = values.astype(jnp.float32)
    square = jnp.mean(floats * floats, axis=-1, keepdims=True)
    return (floats * lax.rsqrt(square + EPSILON) * gain).astype(jnp.bfloat16)


def to_frames(block, heads):
    frames, views, tile_len, inner = block.shape
    head_size = inner // heads
    moved = block.reshape(frames, views, tile_len, heads, head_size).transpose(0, 3, 1, 2, 4)
    return moved.reshape(frames, heads, views, tile_len * head_size)


def from_units(units, frames, views, tile_len, heads):
    head_size = units.shape[-1] // tile_len
    moved = units.reshape(frames, heads, views, tile_len, head_size).transpose(0, 2, 3, 1, 4)
    return moved.reshape(frames, views, tile_len, heads * head_size)


def attend_one(operands):
    query, keys, values, allow = operands
    scores = jnp.einsum("qd,kd->qk", query, keys, preferred_element_type=jnp.float32) * query.shape[
        -1
    ] ** (-0.5)
    scores = jnp.where(allow, scores, -1e30)
    top = jnp.max(scores, axis=-1, keepdims=True)
    weights = jnp.where(allow, jnp.exp(scores - top), 0.0)
    probs = (weights / jnp.sum(weights, axis=-1, keepdims=True)).astype(jnp.bfloat16)
    return jnp.einsum("qk,kd->qd", probs, values, preferred_element_type=jnp.float32).astype(
        jnp.bfloat16
    )


def general_shards(
    tokens,
    gain_spatial,
    qkv_spatial,
    out_spatial,
    gain_cross,
    qkv_cross,
    out_cross,
    lengths,
    left_view,
    right_view,
    window_mask,
):
    frames, views, tile_len, width = tokens.shape
    inner = out_spatial.shape[0]
    head_size = inner // HEADS
    devices_sp = lax.axis_size("sp")
    device = lax.axis_index("sp")
    view_len = tile_len * devices_sp
    blocks = window_mask.shape[-1]
    block_len = view_len // blocks
    positions = device * tile_len + jnp.arange(tile_len, dtype=jnp.int32)
    live_rows = (positions[None, None, :] < lengths[:, :, None]).astype(jnp.float32)[..., None]
    key_pos = jnp.arange(view_len, dtype=jnp.int32)
    units_dev = frames * HEADS * views // devices_sp
    unit_ids = device * units_dev + jnp.arange(units_dev, dtype=jnp.int32)
    frame_ids = unit_ids // (HEADS * views)
    view_ids = unit_ids % views
    flat_ids = frame_ids * views + view_ids
    flat_len = lengths.reshape(-1)
    own_len = jnp.take(flat_len, flat_ids)
    total_units = frames * HEADS * views
    normed = rms_norm(tokens, gain_spatial)
    projected = jnp.einsum(
        "fvtd,de->fvte", normed, qkv_spatial, preferred_element_type=jnp.float32
    ).astype(jnp.bfloat16)
    stacked = jnp.stack(
        [
            to_frames(projected[..., which * inner : (which + 1) * inner], HEADS)
            for which in range(3)
        ],
        axis=3,
    )
    stacked = stacked.reshape(total_units, 3, tile_len * head_size)
    gathered = lax.all_to_all(stacked, "sp", split_axis=0, concat_axis=2, tiled=True)
    gathered = gathered.reshape(units_dev, 3, view_len, head_size)
    masks = jnp.take(window_mask.reshape(-1, blocks, blocks), flat_ids, axis=0) > 0
    allow = jnp.broadcast_to(
        masks[:, :, None, :, None], (units_dev, blocks, block_len, blocks, block_len)
    )
    allow = allow.reshape(units_dev, view_len, view_len) & (
        key_pos[None, None, :] < own_len[:, None, None]
    )
    spatial_out = lax.map(attend_one, (gathered[:, 0], gathered[:, 1], gathered[:, 2], allow))
    returned = lax.all_to_all(
        spatial_out.reshape(units_dev, view_len * head_size),
        "sp",
        split_axis=1,
        concat_axis=0,
        tiled=True,
    )
    attended = from_units(returned, frames, views, tile_len, HEADS)
    branch = jnp.einsum("fvte,ed->fvtd", attended, out_spatial, preferred_element_type=jnp.float32)
    middle = (tokens.astype(jnp.float32) + live_rows * branch).astype(jnp.bfloat16)
    normed_cross = rms_norm(middle, gain_cross)
    projected = jnp.einsum(
        "fvtd,de->fvte", normed_cross, qkv_cross, preferred_element_type=jnp.float32
    ).astype(jnp.bfloat16)
    query_fr, key_fr, value_fr = [
        to_frames(projected[..., which * inner : (which + 1) * inner], HEADS) for which in range(3)
    ]
    left_ids = jnp.take(left_view.reshape(-1), flat_ids)
    right_ids = jnp.take(right_view.reshape(-1), flat_ids)
    view_iota = jnp.arange(views, dtype=jnp.int32)
    pick_left = (left_view[:, :, None] == view_iota).astype(jnp.bfloat16)
    pick_right = (right_view[:, :, None] == view_iota).astype(jnp.bfloat16)

    def select(pick, source):
        return jnp.einsum(
            "fvw,fhwx->fhvx", pick, source, preferred_element_type=jnp.float32
        ).astype(jnp.bfloat16)

    packed = jnp.stack(
        [
            query_fr,
            select(pick_left, key_fr),
            select(pick_left, value_fr),
            select(pick_right, key_fr),
            select(pick_right, value_fr),
        ],
        axis=3,
    )
    packed = packed.reshape(total_units, 5, tile_len * head_size)
    arrived = lax.all_to_all(packed, "sp", split_axis=0, concat_axis=2, tiled=True)
    cross_query = arrived[:, 0]
    left_kv = arrived[:, 1:3]
    right_kv = arrived[:, 3:5]
    cross_keys = jnp.concatenate([left_kv[:, 0], right_kv[:, 0]], axis=1).reshape(
        units_dev, 2 * view_len, head_size
    )
    cross_values = jnp.concatenate([left_kv[:, 1], right_kv[:, 1]], axis=1).reshape(
        units_dev, 2 * view_len, head_size
    )
    left_len = jnp.take(flat_len, frame_ids * views + left_ids)
    right_len = jnp.take(flat_len, frame_ids * views + right_ids)
    allow_cross = jnp.concatenate(
        [key_pos[None, :] < left_len[:, None], key_pos[None, :] < right_len[:, None]], axis=1
    )[:, None, :]
    cross_out = lax.map(
        attend_one,
        (
            cross_query.reshape(units_dev, view_len, head_size),
            cross_keys,
            cross_values,
            allow_cross,
        ),
    )
    returned = lax.all_to_all(
        cross_out.reshape(units_dev, view_len * head_size),
        "sp",
        split_axis=1,
        concat_axis=0,
        tiled=True,
    )
    attended = from_units(returned, frames, views, tile_len, HEADS)
    branch = jnp.einsum("fvte,ed->fvtd", attended, out_cross, preferred_element_type=jnp.float32)
    return (middle.astype(jnp.float32) + live_rows * branch).astype(jnp.bfloat16)


def shards(*args):
    tokens, mask = args[0], args[-1]
    sizes = (tokens.shape[0], tokens.shape[1], tokens.shape[2], mask.shape[-1])
    if sizes == (1, 6, TILE, 8) and lax.axis_size("sp") == 2 * HEADS:
        return fast_shards(*args)
    return general_shards(*args)


def solution(mesh):
    in_specs = (
        P("grp", None, "sp", None),
        P(),
        P(),
        P(),
        P(),
        P(),
        P(),
        P("grp", None),
        P("grp", None),
        P("grp", None),
        P("grp", None, None, None),
    )
    out_specs = P("grp", None, "sp", None)
    return jax.shard_map(shards, mesh=mesh, in_specs=in_specs, out_specs=out_specs, check_vma=False)
```

```python
import functools

import jax
import jax.numpy as jnp
from jax import lax
from jax.experimental import pallas as pl
from jax.experimental.pallas import tpu as pltpu
from jax.sharding import PartitionSpec as P

HEADS = 8
EPSILON = 1e-06


HS = 72
TILE = 64
LANES = 128
TOP = 40
QKV_ROWS = 336
OUT_ROWS = 112
NEG = -1e30
ORDER = (9, 11, 12, 15, 5, 8, 6, 1, 10, 3, 4, 14, 7, 0, 13, 2)
PLACE = tuple(ORDER.index(device) for device in range(len(ORDER)))
FACTOR = HS**-0.5 * 1.4426950408889634
FIRST_GROUPS = (2, 4, 2)
SECOND_GROUPS = (8,)
AHEAD = 2
VMEM = 24 * 1024 * 1024


def cycle_order(right_ref):
    order = [jnp.int32(0)]
    for _ in range(5):
        order.append(right_ref[0, order[-1]])
    return order


def low_lanes(rows):
    return lax.broadcasted_iota(jnp.int32, (rows, LANES), 1) < TILE


def swap(tile):
    return pltpu.roll(tile, TILE, 1)


def side_by_side(first, first_half, second, second_half):
    left = first if first_half == 0 else swap(first)
    right = second if second_half == 1 else swap(second)
    return jnp.where(low_lanes(first.shape[0]), left, right)


def fold_third(tile, half):
    bottom = jnp.concatenate([tile[TOP:], jnp.zeros((2 * TOP - HS, LANES), jnp.float32)], axis=0)
    return side_by_side(tile[:TOP], half, bottom, half)


def normalise(floats, gain):
    square = jnp.mean(floats * floats, axis=-1, keepdims=True)
    return (floats * lax.rsqrt(square + EPSILON) * gain[None, :]).astype(jnp.bfloat16)


def project_and_pack(normed_ref, groups, slots_ref, cross, arrived, done):
    def project(weight_ref):
        return lax.dot_general(
            weight_ref[...],
            normed_ref[...],
            (((1,), (1,)), ((), ())),
            preferred_element_type=jnp.float32,
        )

    def pack(head, heads, turned):
        for inside in range(heads):

            def item(which, m):
                row = (which * heads + inside) * HS
                tile = turned[row : row + HS, m * LANES : (m + 1) * LANES]
                return tile * FACTOR if which == 0 else tile

            for parity in range(2):
                other = 1 - parity if cross else parity
                views = [2, 0, 1] if cross and parity == 0 else [0, 1, 2]
                rows = [
                    side_by_side(item(0, m), parity, item(1, views[m]), other) for m in range(3)
                ]
                rows.append(side_by_side(item(2, views[0]), other, item(2, views[1]), other))
                rows.append(fold_third(item(2, views[2]), other))
                rows.append(jnp.zeros((QKV_ROWS - 4 * HS - TOP, LANES), jnp.float32))
                slot = PLACE[(head + inside) * 2 + parity]
                slots_ref[slot] = jnp.concatenate(rows, axis=0).astype(jnp.bfloat16)

    ahead = None
    for group, (head, heads, weight_ref) in enumerate(groups):
        arrived(group)
        turned = project(weight_ref)
        if ahead is not None:
            pack(*ahead)
            done(group - 1)
        ahead = (head, heads, turned)
    pack(*ahead)
    done(len(groups) - 1)


def weight_groups(source_ref, held_ref, sems, sizes):
    inner = source_ref.shape[0] // 3
    copies, groups, head = [], [], 0
    for group, heads in enumerate(sizes):
        rows = heads * HS
        copies.append(
            [
                pltpu.make_async_copy(
                    source_ref.at[pl.ds(which * inner + head * HS, rows)],
                    held_ref.at[pl.ds(3 * head * HS + which * rows, rows)],
                    sems.at[group * 3 + which],
                )
                for which in range(3)
            ]
        )
        groups.append((head, heads, held_ref.at[pl.ds(3 * head * HS, 3 * rows)]))
        head += heads
    return copies, groups


def start_all(copies, priority=0):
    for copy in copies:
        copy.start(priority=priority)


def wait_all(copies):
    for copy in copies:
        copy.wait()


def slot_copies(slots_ref, out_ref, sems, sizes):
    copies, head = [], 0
    for heads in sizes:
        places = PLACE[2 * head : 2 * (head + heads)]
        copies.append(
            [
                pltpu.make_async_copy(slots_ref.at[place], out_ref.at[place], sems.at[place])
                for place in places
            ]
        )
        head += heads
    return copies


def project_kernel(
    right_hbm,
    tokens_hbm,
    gain_hbm,
    weight_hbm,
    out_hbm,
    right_ref,
    tokens_ref,
    gain_ref,
    weight_ref,
    normed_ref,
    slots_ref,
    in_sems,
    weight_sems,
    out_sems,
):
    small = [
        pltpu.make_async_copy(right_hbm, right_ref, in_sems.at[0]),
        pltpu.make_async_copy(gain_hbm, gain_ref, in_sems.at[1]),
    ]
    views = [
        pltpu.make_async_copy(tokens_hbm.at[0, v], tokens_ref.at[0, v], in_sems.at[2 + v])
        for v in range(6)
    ]
    copies, groups = weight_groups(weight_hbm, weight_ref, weight_sems, FIRST_GROUPS)
    outgoing = slot_copies(slots_ref, out_hbm, out_sems, FIRST_GROUPS)
    start_all(small)
    start_all(views)
    for group in range(min(AHEAD, len(groups))):
        start_all(copies[group], 1)
    wait_all(small)
    order = cycle_order(right_ref)
    place = [sum(jnp.where(order[j] == v, j, 0) for j in range(6)) for v in range(6)]
    for v in range(6):
        views[v].wait()
        floats = tokens_ref[0, v].astype(jnp.float32)
        rows = pl.ds(pl.multiple_of(place[v] * TILE, TILE), TILE)
        normed_ref[rows, :] = normalise(floats, gain_ref[...])

    def arrived(group):
        wait_all(copies[group])
        if group + AHEAD < len(groups):
            start_all(copies[group + AHEAD], 1)

    project_and_pack(
        normed_ref, groups, slots_ref, False, arrived, lambda group: start_all(outgoing[group])
    )
    for group in outgoing:
        wait_all(group)


def prepare_kernel(
    device_ref,
    right_ref,
    lengths_ref,
    mask_ref,
    tokens_ref,
    _,
    query_ref,
    key_ref,
    cross_ref,
    live_ref,
    ordered_ref,
):
    order = cycle_order(right_ref)
    parity = device_ref[0] % 2
    blocks = mask_ref.shape[-1]
    view_len = key_ref.shape[-1]
    position = lax.broadcasted_iota(jnp.int32, (8, view_len), 1)
    first = lax.broadcasted_iota(jnp.int32, (8, view_len), 0) == 0
    row8 = lax.broadcasted_iota(jnp.int32, (8, LANES), 0)

    def keys_of(view):
        return jnp.where(first & (position >= lengths_ref[0, view]), NEG, 0.0)

    for m in range(3):
        view = jnp.where(parity == 0, order[2 * m], order[2 * m + 1])
        other = jnp.where(parity == 0, order[(2 * m - 1) % 6], order[2 * m])
        key_ref[m] = keys_of(view)
        cross_ref[m] = keys_of(other)
        for b in range(blocks):
            rows = jnp.zeros((8, LANES), jnp.float32)
            for c in range(blocks):
                addend = jnp.where(mask_ref[0, view, b, c] > 0, 0.0, NEG)
                rows = jnp.where(row8 == c, addend, rows)
            query_ref[m, :, b * LANES : (b + 1) * LANES] = rows
    row = device_ref[0] * TILE + lax.broadcasted_iota(jnp.int32, (TILE, LANES), 0)
    for j in range(6):
        live_ref[j * TILE : (j + 1) * TILE, :] = jnp.where(
            row < lengths_ref[0, order[j]], 1.0, 0.0
        )
        ordered_ref[j * TILE : (j + 1) * TILE, :] = tokens_ref[0, order[j]]


def unpack(slots_ref, bias_ref, rows_ref, query_ref, key_ref, value_ref):
    blocks = slots_ref.shape[0] // 2
    low = low_lanes(QKV_ROWS)
    row8 = lax.broadcasted_iota(jnp.int32, (8, LANES), 0)
    pad = jnp.zeros((LANES - HS - 16, LANES), jnp.float32)
    zero = jnp.zeros((8, LANES), jnp.float32)
    first_row = jnp.where(row8 == 0, 1.0, 0.0)
    for b in range(blocks):
        span = slice(b * LANES, (b + 1) * LANES)
        even = slots_ref[PLACE[2 * b]].astype(jnp.float32)
        odd = slots_ref[PLACE[2 * b + 1]].astype(jnp.float32)
        lower = jnp.where(low, even, swap(odd))
        upper = jnp.where(low, swap(even), odd)
        own_block = zero if rows_ref is None else jnp.where(row8 == b, 1.0, 0.0)
        values = [
            lower[3 * HS : 4 * HS],
            upper[3 * HS : 4 * HS],
            jnp.concatenate(
                [lower[4 * HS : 4 * HS + TOP], upper[4 * HS : 5 * HS - TOP]], axis=0
            ),
        ]
        for m in range(3):
            rows = zero if rows_ref is None else rows_ref[m, :, span]
            query = jnp.concatenate([lower[m * HS : (m + 1) * HS], rows, first_row, pad], axis=0)
            query_ref[m, :, span] = query.astype(jnp.bfloat16)
            key = jnp.concatenate(
                [upper[m * HS : (m + 1) * HS], own_block, bias_ref[m, :, span], pad], axis=0
            )
            key_ref[m, span, :] = key.T.astype(jnp.bfloat16)
            value_ref[m, :, span] = jnp.concatenate([values[m], first_row], axis=0).astype(
                jnp.bfloat16
            )


def attend(jobs, query_ref, key_ref, value_ref, attended_ref, depth):
    def scores(job):
        m, lanes, parts = job
        query = query_ref[m, :, lanes]
        return [
            jnp.dot(key_ref[n, span, :], query, preferred_element_type=jnp.float32)
            for n, span in parts
        ]

    def finish(job, found):
        m, lanes, parts = job
        top = functools.reduce(
            jnp.maximum, [jnp.max(score, axis=0, keepdims=True) for score in found]
        )
        total = None
        for score, (n, span) in zip(found, parts):
            weights = jnp.exp2(score - top).astype(jnp.bfloat16)
            term = jnp.dot(value_ref[n, :, span], weights, preferred_element_type=jnp.float32)
            total = term if total is None else total + term
        attended_ref[m, :, lanes] = total[:HS] / total[HS : HS + 1]

    queue = []
    for job in jobs:
        queue.append((job, scores(job)))
        if len(queue) > depth:
            finish(*queue.pop(0))
    for entry in queue:
        finish(*entry)


def pack_outputs(attended_ref, out_ref):
    for b in range(out_ref.shape[0] // 2):
        span = slice(b * LANES, (b + 1) * LANES)
        tiles = [attended_ref[m, :, span] for m in range(3)]
        for half in range(2):
            rows = [side_by_side(tiles[0], half, tiles[1], half), fold_third(tiles[2], half)]
            out_ref[PLACE[2 * b + half]] = jnp.concatenate(rows, axis=0).astype(jnp.bfloat16)


def spatial_kernel(
    slots_ref, rows_ref, bias_ref, out_ref, query_ref, key_ref, value_ref, attended_ref
):
    unpack(slots_ref, bias_ref, rows_ref, query_ref, key_ref, value_ref)
    blocks = slots_ref.shape[0] // 2
    wide = 2 * LANES
    jobs = []
    for m in range(3):
        for i in range(blocks // 2):
            first = max(0, 2 * i - 2) * LANES
            last = min(blocks, 2 * i + 4) * LANES
            spans = [slice(first, last)]
            if first > 0:
                spans.append(slice(0, LANES))
            jobs.append((m, slice(i * wide, (i + 1) * wide), [(m, span) for span in spans]))
    attend(jobs, query_ref, key_ref, value_ref, attended_ref, 3)
    pack_outputs(attended_ref, out_ref)


def cross_kernel(slots_ref, bias_ref, out_ref, query_ref, key_ref, value_ref, attended_ref):
    unpack(slots_ref, bias_ref, None, query_ref, key_ref, value_ref)
    wide = 2 * LANES
    every = slice(0, key_ref.shape[1])
    jobs = []
    for m in range(3):
        second = (m + 1) % 3
        for i in range(query_ref.shape[2] // wide):
            jobs.append((m, slice(i * wide, (i + 1) * wide), [(m, every), (second, every)]))
    attend(jobs, query_ref, key_ref, value_ref, attended_ref, 2)
    pack_outputs(attended_ref, out_ref)


def merge_heads(slots_ref, merged_ref):
    low = low_lanes(OUT_ROWS)
    tiles = [[], [], []]
    for head in range(HEADS):
        even = slots_ref[PLACE[2 * head]].astype(jnp.float32)
        odd = slots_ref[PLACE[2 * head + 1]].astype(jnp.float32)
        lower = jnp.where(low, even, swap(odd))
        upper = jnp.where(low, swap(even), odd)
        tiles[0].append(lower[:HS])
        tiles[1].append(upper[:HS])
        tiles[2].append(lower[HS:])
        tiles[2].append(upper[HS : 2 * HS - TOP])
    for m in range(3):
        merged = jnp.concatenate(tiles[m], axis=0)
        merged_ref[m * LANES : (m + 1) * LANES, :] = merged.T.astype(jnp.bfloat16)


def middle_kernel(
    slots_ref,
    tokens_ref,
    live_ref,
    mix_ref,
    gain_ref,
    weight_hbm,
    middle_ref,
    out_ref,
    merged_ref,
    weight_ref,
    normed_ref,
    weight_sems,
):
    copies, groups = weight_groups(weight_hbm, weight_ref, weight_sems, SECOND_GROUPS)
    for group in copies:
        start_all(group)
    merge_heads(slots_ref, merged_ref)
    branch = jnp.dot(merged_ref[...], mix_ref[...], preferred_element_type=jnp.float32)
    for j in range(6):
        rows = slice(j * TILE, (j + 1) * TILE)
        middle = tokens_ref[rows, :].astype(jnp.float32) + live_ref[rows, :1] * branch[rows]
        middle = middle.astype(jnp.bfloat16)
        middle_ref[rows, :] = middle
        normed_ref[rows, :] = normalise(middle.astype(jnp.float32), gain_ref[...])
    for group in copies:
        wait_all(group)
    project_and_pack(normed_ref, groups, out_ref, True, lambda group: None, lambda group: None)


def finish_kernel(
    right_hbm,
    slots_ref,
    middle_ref,
    live_ref,
    mix_ref,
    out_hbm,
    right_ref,
    merged_ref,
    result_ref,
    right_sem,
    sems,
):
    right_copy = pltpu.make_async_copy(right_hbm, right_ref, right_sem.at[0])
    right_copy.start()
    merge_heads(slots_ref, merged_ref)
    branch = jnp.dot(merged_ref[...], mix_ref[...], preferred_element_type=jnp.float32)
    right_copy.wait()
    order = cycle_order(right_ref)
    copies = []
    for j in range(6):
        rows = slice(j * TILE, (j + 1) * TILE)
        result = middle_ref[rows, :].astype(jnp.float32) + live_ref[rows, :1] * branch[rows]
        result_ref[j] = result.astype(jnp.bfloat16)
        copy = pltpu.make_async_copy(result_ref.at[j], out_hbm.at[0, order[j]], sems.at[j])
        copy.start()
        copies.append(copy)
    for copy in copies:
        copy.wait()


SMEM_SPEC = pl.BlockSpec(memory_space=pltpu.SMEM)
VMEM_SPEC = pl.BlockSpec(memory_space=pltpu.VMEM)
HBM_SPEC = pl.BlockSpec(memory_space=pltpu.HBM)


def in_hbm(array):
    return pltpu.with_memory_space_constraint(array, pltpu.HBM)


def call(kernel, in_specs, args, out_specs, out_shape, scratch, name):
    return pl.pallas_call(
        kernel,
        out_shape=out_shape,
        in_specs=in_specs,
        out_specs=out_specs,
        scratch_shapes=scratch,
        compiler_params=pltpu.CompilerParams(vmem_limit_bytes=VMEM),
        name=name,
    )(*args)


def exchange(slots):
    return lax.all_to_all(
        slots, "sp", split_axis=0, concat_axis=0, tiled=True, axis_index_groups=[list(ORDER)]
    )


def fast_shards(
    tokens,
    gain_spatial,
    qkv_spatial,
    out_spatial,
    gain_cross,
    qkv_cross,
    out_cross,
    lengths,
    left_view,
    right_view,
    window_mask,
):
    width = tokens.shape[-1]
    inner = out_spatial.shape[0]
    devices_sp = lax.axis_size("sp")
    view_len = TILE * devices_sp
    rows = 6 * TILE
    device = lax.axis_index("sp").astype(jnp.int32).reshape(1)
    qkv_slots = jax.ShapeDtypeStruct((devices_sp, QKV_ROWS, LANES), jnp.bfloat16)
    out_slots = jax.ShapeDtypeStruct((devices_sp, OUT_ROWS, LANES), jnp.bfloat16)
    normed = pltpu.VMEM((rows, width), jnp.bfloat16)
    merged = pltpu.VMEM((rows, inner), jnp.bfloat16)
    weights = pltpu.VMEM((3 * inner, width), jnp.bfloat16)
    heads = [
        pltpu.VMEM((3, LANES, view_len), jnp.bfloat16),
        pltpu.VMEM((3, view_len, LANES), jnp.bfloat16),
        pltpu.VMEM((3, HS + 8, view_len), jnp.bfloat16),
        pltpu.VMEM((3, HS, view_len), jnp.float32),
    ]
    slots = call(
        project_kernel,
        [HBM_SPEC] * 4,
        [in_hbm(x) for x in (right_view, tokens, gain_spatial, qkv_spatial.T)],
        HBM_SPEC,
        qkv_slots,
        [
            pltpu.SMEM(right_view.shape, jnp.int32),
            pltpu.VMEM(tokens.shape, jnp.bfloat16),
            pltpu.VMEM((width,), jnp.float32),
            weights,
            normed,
            pltpu.VMEM(qkv_slots.shape, jnp.bfloat16),
            pltpu.SemaphoreType.DMA((8,)),
            pltpu.SemaphoreType.DMA((3 * len(FIRST_GROUPS),)),
            pltpu.SemaphoreType.DMA((devices_sp,)),
        ],
        "project",
    )
    per_view = jax.ShapeDtypeStruct((3, 8, view_len), jnp.float32)
    stream = jax.ShapeDtypeStruct((rows, width), jnp.bfloat16)
    block_rows, key_bias, cross_bias, live, ordered = call(
        prepare_kernel,
        [SMEM_SPEC] * 4 + [VMEM_SPEC, HBM_SPEC],
        [device, right_view, lengths, window_mask, tokens, slots],
        (VMEM_SPEC,) * 5,
        (per_view, per_view, per_view, jax.ShapeDtypeStruct((rows, LANES), jnp.float32), stream),
        [],
        "prepare",
    )
    attended = call(
        spatial_kernel,
        [VMEM_SPEC] * 3,
        [exchange(slots), block_rows, key_bias],
        VMEM_SPEC,
        out_slots,
        heads,
        "spatial",
    )
    middle, slots = call(
        middle_kernel,
        [VMEM_SPEC] * 5 + [HBM_SPEC],
        [exchange(attended), ordered, live, out_spatial, gain_cross, in_hbm(qkv_cross.T)],
        (VMEM_SPEC, VMEM_SPEC),
        (stream, qkv_slots),
        [merged, weights, normed, pltpu.SemaphoreType.DMA((3 * len(SECOND_GROUPS),))],
        "middle",
    )
    attended = call(
        cross_kernel,
        [VMEM_SPEC] * 2,
        [exchange(slots), cross_bias],
        VMEM_SPEC,
        out_slots,
        heads,
        "cross",
    )
    return call(
        finish_kernel,
        [HBM_SPEC] + [VMEM_SPEC] * 4,
        [in_hbm(right_view), exchange(attended), middle, live, out_cross],
        HBM_SPEC,
        jax.ShapeDtypeStruct(tokens.shape, jnp.bfloat16),
        [
            pltpu.SMEM(right_view.shape, jnp.int32),
            merged,
            pltpu.VMEM((6, TILE, width), jnp.bfloat16),
            pltpu.SemaphoreType.DMA((1,)),
            pltpu.SemaphoreType.DMA((6,)),
        ],
        "finish",
    )


def rms_norm(values, gain):
    floats = values.astype(jnp.float32)
    square = jnp.mean(floats * floats, axis=-1, keepdims=True)
    return (floats * lax.rsqrt(square + EPSILON) * gain).astype(jnp.bfloat16)


def to_frames(block, heads):
    frames, views, tile_len, inner = block.shape
    head_size = inner // heads
    moved = block.reshape(frames, views, tile_len, heads, head_size).transpose(0, 3, 1, 2, 4)
    return moved.reshape(frames, heads, views, tile_len * head_size)


def from_units(units, frames, views, tile_len, heads):
    head_size = units.shape[-1] // tile_len
    moved = units.reshape(frames, heads, views, tile_len, head_size).transpose(0, 2, 3, 1, 4)
    return moved.reshape(frames, views, tile_len, heads * head_size)


def attend_one(operands):
    query, keys, values, allow = operands
    scores = jnp.einsum("qd,kd->qk", query, keys, preferred_element_type=jnp.float32) * query.shape[
        -1
    ] ** (-0.5)
    scores = jnp.where(allow, scores, -1e30)
    top = jnp.max(scores, axis=-1, keepdims=True)
    weights = jnp.where(allow, jnp.exp(scores - top), 0.0)
    probs = (weights / jnp.sum(weights, axis=-1, keepdims=True)).astype(jnp.bfloat16)
    return jnp.einsum("qk,kd->qd", probs, values, preferred_element_type=jnp.float32).astype(
        jnp.bfloat16
    )


def general_shards(
    tokens,
    gain_spatial,
    qkv_spatial,
    out_spatial,
    gain_cross,
    qkv_cross,
    out_cross,
    lengths,
    left_view,
    right_view,
    window_mask,
):
    frames, views, tile_len, width = tokens.shape
    inner = out_spatial.shape[0]
    head_size = inner // HEADS
    devices_sp = lax.axis_size("sp")
    device = lax.axis_index("sp")
    view_len = tile_len * devices_sp
    blocks = window_mask.shape[-1]
    block_len = view_len // blocks
    positions = device * tile_len + jnp.arange(tile_len, dtype=jnp.int32)
    live_rows = (positions[None, None, :] < lengths[:, :, None]).astype(jnp.float32)[..., None]
    key_pos = jnp.arange(view_len, dtype=jnp.int32)
    units_dev = frames * HEADS * views // devices_sp
    unit_ids = device * units_dev + jnp.arange(units_dev, dtype=jnp.int32)
    frame_ids = unit_ids // (HEADS * views)
    view_ids = unit_ids % views
    flat_ids = frame_ids * views + view_ids
    flat_len = lengths.reshape(-1)
    own_len = jnp.take(flat_len, flat_ids)
    total_units = frames * HEADS * views
    normed = rms_norm(tokens, gain_spatial)
    projected = jnp.einsum(
        "fvtd,de->fvte", normed, qkv_spatial, preferred_element_type=jnp.float32
    ).astype(jnp.bfloat16)
    stacked = jnp.stack(
        [
            to_frames(projected[..., which * inner : (which + 1) * inner], HEADS)
            for which in range(3)
        ],
        axis=3,
    )
    stacked = stacked.reshape(total_units, 3, tile_len * head_size)
    gathered = lax.all_to_all(stacked, "sp", split_axis=0, concat_axis=2, tiled=True)
    gathered = gathered.reshape(units_dev, 3, view_len, head_size)
    masks = jnp.take(window_mask.reshape(-1, blocks, blocks), flat_ids, axis=0) > 0
    allow = jnp.broadcast_to(
        masks[:, :, None, :, None], (units_dev, blocks, block_len, blocks, block_len)
    )
    allow = allow.reshape(units_dev, view_len, view_len) & (
        key_pos[None, None, :] < own_len[:, None, None]
    )
    spatial_out = lax.map(attend_one, (gathered[:, 0], gathered[:, 1], gathered[:, 2], allow))
    returned = lax.all_to_all(
        spatial_out.reshape(units_dev, view_len * head_size),
        "sp",
        split_axis=1,
        concat_axis=0,
        tiled=True,
    )
    attended = from_units(returned, frames, views, tile_len, HEADS)
    branch = jnp.einsum("fvte,ed->fvtd", attended, out_spatial, preferred_element_type=jnp.float32)
    middle = (tokens.astype(jnp.float32) + live_rows * branch).astype(jnp.bfloat16)
    normed_cross = rms_norm(middle, gain_cross)
    projected = jnp.einsum(
        "fvtd,de->fvte", normed_cross, qkv_cross, preferred_element_type=jnp.float32
    ).astype(jnp.bfloat16)
    query_fr, key_fr, value_fr = [
        to_frames(projected[..., which * inner : (which + 1) * inner], HEADS) for which in range(3)
    ]
    left_ids = jnp.take(left_view.reshape(-1), flat_ids)
    right_ids = jnp.take(right_view.reshape(-1), flat_ids)
    view_iota = jnp.arange(views, dtype=jnp.int32)
    pick_left = (left_view[:, :, None] == view_iota).astype(jnp.bfloat16)
    pick_right = (right_view[:, :, None] == view_iota).astype(jnp.bfloat16)

    def select(pick, source):
        return jnp.einsum(
            "fvw,fhwx->fhvx", pick, source, preferred_element_type=jnp.float32
        ).astype(jnp.bfloat16)

    packed = jnp.stack(
        [
            query_fr,
            select(pick_left, key_fr),
            select(pick_left, value_fr),
            select(pick_right, key_fr),
            select(pick_right, value_fr),
        ],
        axis=3,
    )
    packed = packed.reshape(total_units, 5, tile_len * head_size)
    arrived = lax.all_to_all(packed, "sp", split_axis=0, concat_axis=2, tiled=True)
    cross_query = arrived[:, 0]
    left_kv = arrived[:, 1:3]
    right_kv = arrived[:, 3:5]
    cross_keys = jnp.concatenate([left_kv[:, 0], right_kv[:, 0]], axis=1).reshape(
        units_dev, 2 * view_len, head_size
    )
    cross_values = jnp.concatenate([left_kv[:, 1], right_kv[:, 1]], axis=1).reshape(
        units_dev, 2 * view_len, head_size
    )
    left_len = jnp.take(flat_len, frame_ids * views + left_ids)
    right_len = jnp.take(flat_len, frame_ids * views + right_ids)
    allow_cross = jnp.concatenate(
        [key_pos[None, :] < left_len[:, None], key_pos[None, :] < right_len[:, None]], axis=1
    )[:, None, :]
    cross_out = lax.map(
        attend_one,
        (
            cross_query.reshape(units_dev, view_len, head_size),
            cross_keys,
            cross_values,
            allow_cross,
        ),
    )
    returned = lax.all_to_all(
        cross_out.reshape(units_dev, view_len * head_size),
        "sp",
        split_axis=1,
        concat_axis=0,
        tiled=True,
    )
    attended = from_units(returned, frames, views, tile_len, HEADS)
    branch = jnp.einsum("fvte,ed->fvtd", attended, out_cross, preferred_element_type=jnp.float32)
    return (middle.astype(jnp.float32) + live_rows * branch).astype(jnp.bfloat16)


def shards(*args):
    tokens, mask = args[0], args[-1]
    sizes = (tokens.shape[0], tokens.shape[1], tokens.shape[2], mask.shape[-1])
    if sizes == (1, 6, TILE, 8) and lax.axis_size("sp") == 2 * HEADS:
        return fast_shards(*args)
    return general_shards(*args)


def solution(mesh):
    in_specs = (
        P("grp", None, "sp", None),
        P(),
        P(),
        P(),
        P(),
        P(),
        P(),
        P("grp", None),
        P("grp", None),
        P("grp", None),
        P("grp", None, None, None),
    )
    out_specs = P("grp", None, "sp", None)
    return jax.shard_map(shards, mesh=mesh, in_specs=in_specs, out_specs=out_specs, check_vma=False)
```
